256 devices in a mesh: layer: 8 (over x, z_hi), latent: 8 (over z_lo, core), token: 4 (over y).
Axes of the slice: x: 4, y: 4, z: 8 (z_hi: 2, z_lo: 4; z = z_hi * 4 + z_lo), core: 2. Of those that a mesh axis runs over, the one named last changes fastest.
Arguments:
- streams: bfloat16 [8, 4096, 8192], P('layer', 'token', 'latent'), may hold values from -6 to 6
- active_latents: int32 [4096, 64], P('token'), may hold values from 0 to 383, all different within a row
- enc_weight: float32 [8, 384, 8192], P('layer', 'latent', 'token'), may hold values from -6 to 6
- enc_moment: float32 [8, 384, 8192], P('layer', 'latent', 'token'), may hold values from -0.0029296875 to 0.0029296875
- enc_second: float32 [8, 384, 8192], P('layer', 'latent', 'token'), may hold values from 1e-09 to 1e-07
- dec_weight: float32 [8, 384, 8192], P('layer', 'latent', 'token'), may hold values from -6 to 6
- dec_moment: float32 [8, 384, 8192], P('layer', 'latent', 'token'), may hold values from -0.0029296875 to 0.0029296875
- dec_second: float32 [8, 384, 8192], P('layer', 'latent', 'token'), may hold values from 1e-09 to 1e-07
Outputs:
- enc_weight_new: float32 [8, 384, 8192], P('layer', 'latent', 'token')
- enc_moment_new: float32 [8, 384, 8192], P('layer', 'latent', 'token')
- enc_second_new: float32 [8, 384, 8192], P('layer', 'latent', 'token')
- dec_weight_new: float32 [8, 384, 8192], P('layer', 'latent', 'token')
- dec_moment_new: float32 [8, 384, 8192], P('layer', 'latent', 'token')
- dec_second_new: float32 [8, 384, 8192], P('layer', 'latent', 'token')
The draws below stay inside these ranges and needn't reach their ends.
Inputs may be any that keep to these rules, and one draw needn't show every extreme that they name: `active_latents`: each row names 64 different latents; every latent is named by some row.
All inputs are finite; a program needn't handle non-finite values.
Results may differ from the reference program's by a relative error of at most 0.0056.
Values may be sent and summed in bfloat16 or wider, within the bound.
No kernel may reach another device: no remote copies, remote signals or barrier semaphores. Data moves between devices by JAX's collectives and lax.ppermute only.
A program may use at most 64 MiB of HBM per device.

```python
import math
import jax
import jax.numpy as jnp
from jax import lax

D = 8192
K = 64
ADAM_STEP = 100
LAYERS = 8
M = 384
TOKENS = 4096


def block_levels(own_key, shape, pieces, low, top_value):
    gain = 1.0
    for position, shards_of in pieces:
        heights = jax.random.uniform(jax.random.fold_in(jax.random.fold_in(own_key, 6), position), (shards_of,), jnp.float32, low / len(pieces), top_value / len(pieces))
        gain = gain * jnp.repeat(jnp.exp(heights), shape[position] // shards_of).reshape((-1,) + (1,) * (len(shape) - 1 - position))
    return gain


def choose_distinct(rng, rows, number_of, top, lift):
    order = jax.random.permutation(jax.random.fold_in(rng, 1), number_of)
    pull = order
    for power in range(3):
        pull = pull * pull // number_of
    pull = pull * lift // number_of
    chance = jax.random.randint(jax.random.fold_in(rng, 2), (rows, number_of), 0, 4096) + pull
    sure = jax.random.permutation(jax.random.fold_in(rng, 3), rows)[jnp.arange(number_of) % rows]
    chance = jnp.where(jnp.arange(rows)[:, None] == sure[None, :], 1 << 14, chance)
    merit = chance * number_of + jnp.arange(number_of)
    return lax.top_k(merit.astype(jnp.int32), top)[1].astype(jnp.int32)


def scatter_about(rng, extent, scale, reach, cuts=(), kind=jnp.bfloat16):
    values = jax.random.normal(rng, extent, jnp.float32) * scale
    if len(cuts) > 0:
        values = block_levels(rng, extent, cuts, -0.22, 0.18) * values
    return jnp.clip(values, min=-reach, max=reach).astype(kind)


def setup_inputs(seed: int = 0) -> dict:
    arg_keys = jax.random.split(jax.random.key(seed), 9)
    return {
        "streams": scatter_about(arg_keys[0], (LAYERS, TOKENS, D), 1.0, 6.0, ((0, 8), (1, 4), (2, 8))),
        "active_latents": choose_distinct(arg_keys[1], TOKENS, M, K, 1365),
        "enc_weight": scatter_about(arg_keys[2], (LAYERS, M, D), 1.0, 6.0, ((0, 8), (1, 8), (2, 4)), jnp.float32),
        "enc_moment": scatter_about(arg_keys[3], (LAYERS, M, D), 0.0002, 0.0029296875, ((0, 8), (1, 8), (2, 4)), jnp.float32),
        "enc_second": jnp.clip(jnp.exp(math.log(1.0000000116860974e-07) - 4.6051702 * jax.random.uniform(arg_keys[4], (LAYERS, M, D), jnp.float32) ** block_levels(arg_keys[4], (LAYERS, M, D), ((0, 8), (1, 8), (2, 4)), -0.2, 0.2)), 9.999999717180685e-10, 1.0000000116860974e-07),
        "dec_weight": scatter_about(arg_keys[5], (LAYERS, M, D), 1.0, 6.0, ((0, 8), (1, 8), (2, 4)), jnp.float32),
        "dec_moment": scatter_about(arg_keys[6], (LAYERS, M, D), 0.0002, 0.0029296875, ((0, 8), (1, 8), (2, 4)), jnp.float32),
        "dec_second": jnp.clip(jnp.exp(math.log(1.0000000116860974e-07) - 4.6051702 * jax.random.uniform(arg_keys[7], (LAYERS, M, D), jnp.float32) ** block_levels(arg_keys[7], (LAYERS, M, D), ((0, 8), (1, 8), (2, 4)), -0.2, 0.2)), 9.999999717180685e-10, 1.0000000116860974e-07),
    }


def adam_step(weight, moment, second, gradient):
    moment_new = 0.9 * moment + 0.1 * gradient
    second_new = 0.999 * second + 0.001 * gradient * gradient
    first_fix = 1.0 - 0.9 ** ADAM_STEP
    second_fix = 1.0 - 0.999 ** ADAM_STEP
    weight_new = weight - 0.2 * (moment_new / first_fix) / (jnp.sqrt(second_new / second_fix) + 1e-08)
    return (weight_new, moment_new, second_new)

def reference(streams, active_latents, enc_weight, enc_moment, enc_second, dec_weight, dec_moment, dec_second):
    enc_scale = 1.0 / math.sqrt(LAYERS * D)
    dec_scale = 1.0 / math.sqrt(K)
    enc_bf = enc_weight.astype(jnp.bfloat16)
    dec_bf = dec_weight.astype(jnp.bfloat16)
    pre = jnp.zeros((TOKENS, M), jnp.float32)
    for layer in range(LAYERS):
        pre = pre + jnp.dot(streams[layer], enc_bf[layer].T, preferred_element_type=jnp.float32)
    row_ids = jnp.arange(TOKENS, dtype=jnp.int32)[:, None]
    selected = jnp.zeros((TOKENS, M), jnp.float32).at[row_ids, active_latents].set(1.0)
    codes = (pre * enc_scale * selected).astype(jnp.bfloat16)
    backsum = jnp.zeros((TOKENS, M), jnp.float32)
    dec_grads = []
    for layer in range(LAYERS):
        rebuilt = jnp.dot(codes, dec_bf[layer], preferred_element_type=jnp.float32) * dec_scale
        errors = (rebuilt - streams[layer].astype(jnp.float32)).astype(jnp.bfloat16)
        backsum = backsum + jnp.dot(errors, dec_bf[layer].T, preferred_element_type=jnp.float32)
        dec_grads.append(jnp.dot(codes.T, errors, preferred_element_type=jnp.float32) * (dec_scale / TOKENS))
    backward = (backsum * dec_scale * selected).astype(jnp.bfloat16)
    enc_grads = []
    for layer in range(LAYERS):
        enc_grads.append(jnp.dot(backward.T, streams[layer], preferred_element_type=jnp.float32) * (enc_scale / TOKENS))
    enc_grad = jnp.stack(enc_grads)
    dec_grad = jnp.stack(dec_grads)
    enc_out = adam_step(enc_weight, enc_moment, enc_second, enc_grad)
    dec_out = adam_step(dec_weight, dec_moment, dec_second, dec_grad)
    return (enc_out[0], enc_out[1], enc_out[2], dec_out[0], dec_out[1], dec_out[2])
```

```python
import math

import jax
import jax.numpy as jnp
from jax import lax
from jax.experimental import pallas as pl
from jax.experimental.pallas import tpu as pltpu
from jax.sharding import PartitionSpec as P

K = 64
ADAM_STEP = 100
LATENTS = 384
OWN = 48
PAIR = 96
LANES = 128
PARTS = LATENTS // LANES
ROWS = 1024
FEATS = 1024
GROUP = ("layer", "latent")
GROUP_SIZE = 64
PLANE = ("latent", "token")
CHUNK = 256
CHUNKS = ROWS // CHUNK
HALF = CHUNK // 2
F32 = jnp.float32
BF16 = jnp.bfloat16
VMEM_BYTES = 40 * 1024 * 1024


def place(z, core, y):
    return (z * 2 + core) * 4 + y


def plane_pairs(target):
    return [
        (place(z, core, y), place(*target(z, core, y)))
        for z in range(4)
        for core in range(2)
        for y in range(4)
    ]


TRANSPOSED = plane_pairs(lambda z, core, y: (y, core, z))


def homeward(step):
    return plane_pairs(lambda z, core, y: (y ^ step, core, z))


def swapped(count, step):
    return [(i, i ^ step) for i in range(count)]


def params():
    return pltpu.CompilerParams(vmem_limit_bytes=VMEM_BYTES)


def cost(flops, moved):
    return pl.CostEstimate(flops=flops, bytes_accessed=moved, transcendentals=0)


def lane_take(table, column):
    return jnp.take_along_axis(table, column, axis=1, mode="promise_in_bounds")


def compact(dense, index):
    pairs = dense.reshape(dense.shape[0] // 16, 2, 8, LATENTS)
    first = pairs[:, 0].reshape(dense.shape[0] // 2, LATENTS)
    second = pairs[:, 1].reshape(dense.shape[0] // 2, LATENTS)
    column = jnp.bitwise_and(index, LANES - 1)
    part = jnp.right_shift(index, 7)
    low = lax.broadcasted_iota(jnp.int32, index.shape, 1) < K
    out = None
    for q in range(PARTS):
        cut = slice(q * LANES, (q + 1) * LANES)
        found = jnp.where(low, lane_take(first[:, cut], column), lane_take(second[:, cut], column))
        out = found if out is None else jnp.where(part == q, found, out)
    return out


def spread(packed, slot):
    rows = slot.shape[0]
    pairs = slot.reshape(rows // 16, 2, 8, LATENTS)
    sides = []
    for side in range(2):
        at = pairs[:, side].reshape(rows // 2, LATENTS)
        cols = []
        for q in range(PARTS):
            here = at[:, q * LANES : (q + 1) * LANES]
            cols.append(jnp.where(here >= 0, lane_take(packed, jnp.bitwise_and(here, LANES - 1)), 0.0))
        sides.append(jnp.concatenate(cols, axis=1).reshape(rows // 16, 1, 8, LATENTS))
    return jnp.concatenate(sides, axis=1).reshape(rows, LATENTS).astype(BF16)


def slot_kernel(active_ref, slot_ref):
    width = active_ref.shape[1]
    for block in range(LATENTS // 32):
        ids = lax.broadcasted_iota(jnp.int32, (32, width), 0) + block * 32

        def look(k, held):
            row = active_ref[pl.ds(k, 1), :]
            return jnp.where(ids == row, k, held)

        held = lax.fori_loop(0, K, look, jnp.full((32, width), -1, jnp.int32), unroll=8)
        token = lax.broadcasted_iota(jnp.int32, (32, width), 1)
        lift = jnp.where(jnp.bitwise_and(token, 8) > 0, K, 0)
        slot_ref[block * 32 : (block + 1) * 32, :] = jnp.where(held >= 0, held + lift, -1)


def find_slots(active_t):
    return pl.pallas_call(
        slot_kernel,
        grid=(ROWS // LANES,),
        in_specs=[pl.BlockSpec((K, LANES), lambda i: (0, i))],
        out_specs=pl.BlockSpec((LATENTS, LANES), lambda i: (0, i)),
        out_shape=jax.ShapeDtypeStruct((LATENTS, ROWS), jnp.int32),
        cost_estimate=cost(LATENTS * ROWS * K * 16, 2 * 1024 * 1024),
        name="find_slots",
    )(active_t)


def assemble(parts, whole):
    for step, part in enumerate(parts):
        whole[step * PAIR : (step + 1) * PAIR, :] = part[...]


def pre_kernel(streams_ref, e0, e1, e2, e3, index_ref, out_ref, weight):
    @pl.when(pl.program_id(0) == 0)
    def _():
        assemble((e0, e1, e2, e3), weight)

    pre = lax.dot_general(
        streams_ref[...], weight[...], (((1,), (1,)), ((), ())), preferred_element_type=F32
    )
    out_ref[...] = compact(pre, index_ref[...])


def whole_spec(shape):
    return pl.BlockSpec(shape, lambda i: (0,) * len(shape))


def row_spec(rows, width):
    return pl.BlockSpec((rows, width), lambda i: (i, 0))


def pre_sums(streams, enc_parts, index):
    return pl.pallas_call(
        pre_kernel,
        grid=(CHUNKS,),
        in_specs=[row_spec(CHUNK, FEATS)]
        + [whole_spec((PAIR, FEATS))] * 4
        + [row_spec(HALF, LANES)],
        out_specs=row_spec(HALF, LANES),
        out_shape=jax.ShapeDtypeStruct((ROWS // 2, LANES), F32),
        scratch_shapes=[pltpu.VMEM((LATENTS, FEATS), BF16)],
        compiler_params=params(),
        cost_estimate=cost(2 * ROWS * FEATS * LATENTS, 4 * 1024 * 1024),
        name="pre_sums",
    )(streams, *enc_parts, index)


def total_kernel(scale, parts_ref, out_ref):
    total = jnp.sum(parts_ref[...], axis=0) * scale
    out_ref[...] = jnp.broadcast_to(total[None], (GROUP_SIZE, 8, LANES)).reshape(GROUP_SIZE * 8, LANES).astype(BF16)


def group_total(partial, scale):
    parts = lax.all_to_all(partial.reshape(GROUP_SIZE, 8, LANES), GROUP, 0, 0, tiled=True)
    copies = pl.pallas_call(
        lambda parts_ref, out_ref: total_kernel(scale, parts_ref, out_ref),
        out_shape=jax.ShapeDtypeStruct((ROWS // 2, LANES), BF16),
        cost_estimate=cost(GROUP_SIZE * 8 * LANES, 512 * 1024),
        name="group_total",
    )(parts)
    back = lax.all_to_all(copies.reshape(GROUP_SIZE, 8, LANES), GROUP, 0, 0, tiled=True)
    return back.reshape(ROWS // 2, LANES)


def errors_body(scale, packed_ref, slot_ref, streams_ref, d0, d1, d2, d3, index_ref, back_ref, codes_ref, errors_ref, weight):
    @pl.when(pl.program_id(0) == 0)
    def _():
        assemble((d0, d1, d2, d3), weight)

    codes = spread(packed_ref[...].astype(F32), slot_ref[...])
    codes_ref[...] = codes
    rebuilt = jnp.dot(codes, weight[...], preferred_element_type=F32) * scale
    errors = (rebuilt - streams_ref[...].astype(F32)).astype(BF16)
    errors_ref[...] = errors
    back = lax.dot_general(errors, weight[...], (((1,), (1,)), ((), ())), preferred_element_type=F32)
    back_ref[...] = compact(back, index_ref[...])


def errors_and_back(packed, slots, streams, dec_parts, index, scale):
    return pl.pallas_call(
        lambda *refs: errors_body(scale, *refs),
        grid=(CHUNKS,),
        in_specs=[row_spec(HALF, LANES), row_spec(CHUNK, LATENTS), row_spec(CHUNK, FEATS)]
        + [whole_spec((PAIR, FEATS))] * 4
        + [row_spec(HALF, LANES)],
        out_specs=[row_spec(HALF, LANES), row_spec(CHUNK, LATENTS), row_spec(CHUNK, FEATS)],
        out_shape=[
            jax.ShapeDtypeStruct((ROWS // 2, LANES), F32),
            jax.ShapeDtypeStruct((ROWS, LATENTS), BF16),
            jax.ShapeDtypeStruct((ROWS, FEATS), BF16),
        ],
        scratch_shapes=[pltpu.VMEM((LATENTS, FEATS), BF16)],
        compiler_params=params(),
        cost_estimate=cost(4 * ROWS * FEATS * LATENTS, 8 * 1024 * 1024),
        name="errors_and_back",
    )(packed, slots, streams, *dec_parts, index)


def split_out(total, scale, keep_ref, send_ref):
    scaled = (total * scale).astype(BF16)
    for step in range(4):
        base = step * PAIR
        keep_ref[step] = scaled[base : base + OWN]
        send_ref[step] = scaled[base + OWN : base + PAIR]


def gradient_body(scale, codes_ref, errors_ref, keep_ref, send_ref, total):
    part = lax.dot_general(codes_ref[...], errors_ref[...], (((0,), (0,)), ((), ())), preferred_element_type=F32)
    add_and_split(part, scale, keep_ref, send_ref, total)


def add_and_split(part, scale, keep_ref, send_ref, total):
    step = pl.program_id(0)

    @pl.when(step == 0)
    def _():
        total[...] = part

    @pl.when(step > 0)
    def _():
        total[...] += part

    @pl.when(step == CHUNKS - 1)
    def _():
        split_out(total[...], scale, keep_ref, send_ref)


def spread_gradient_body(scale, packed_ref, slot_ref, streams_ref, keep_ref, send_ref, total):
    codes = spread(packed_ref[...].astype(F32), slot_ref[...])
    part = lax.dot_general(codes, streams_ref[...], (((0,), (0,)), ((), ())), preferred_element_type=F32)
    add_and_split(part, scale, keep_ref, send_ref, total)


def gradient_call(body, in_specs, scale, name):
    return pl.pallas_call(
        lambda *refs: body(scale, *refs),
        grid=(CHUNKS,),
        in_specs=in_specs,
        out_specs=[whole_spec((4, OWN, FEATS))] * 2,
        out_shape=[jax.ShapeDtypeStruct((4, OWN, FEATS), BF16)] * 2,
        scratch_shapes=[pltpu.VMEM((LATENTS, FEATS), F32)],
        compiler_params=params(),
        cost_estimate=cost(2 * ROWS * FEATS * LATENTS, 4 * 1024 * 1024),
        name=name,
    )


def send_home(keep, send):
    got = lax.ppermute(send, "latent", swapped(8, 1))
    return [
        lax.ppermute(jnp.concatenate([keep[step], got[step]], axis=0), PLANE, homeward(step))
        for step in range(4)
    ]


def adam_kernel(core_ref, g0, g1, g2, g3, weight_ref, moment_ref, second_ref, weight_out, moment_out, second_out):
    gradient = g0[...].astype(F32) + g1[...].astype(F32) + g2[...].astype(F32) + g3[...].astype(F32)
    moment_new = 0.9 * moment_ref[0] + 0.1 * gradient
    second_new = 0.999 * second_ref[0] + 0.001 * gradient * gradient
    first_fix = 1.0 - 0.9**ADAM_STEP
    second_fix = 1.0 - 0.999**ADAM_STEP
    weight_out[0] = weight_ref[0] - 0.2 * (moment_new / first_fix) / (jnp.sqrt(second_new / second_fix) + 1e-08)
    moment_out[0] = moment_new
    second_out[0] = second_new


def adam(core, grads, weight, moment, second):
    near = pl.BlockSpec((OWN, FEATS), lambda i, core_ref: (i, 0))
    far = pl.BlockSpec((1, OWN, FEATS), lambda i, core_ref: (0, 0, jnp.bitwise_xor(i, core_ref[0])))
    shape = jax.ShapeDtypeStruct(weight.shape, F32)
    return pl.pallas_call(
        adam_kernel,
        grid_spec=pltpu.PrefetchScalarGridSpec(
            num_scalar_prefetch=1, grid=(2,), in_specs=[near] * 4 + [far] * 3, out_specs=[far] * 3
        ),
        out_shape=[shape] * 3,
        cost_estimate=cost(OWN * 2048 * 16, 3 * 1024 * 1024),
        name="adam",
    )(core, *grads, weight, moment, second)


def gather_weight(weight, core):
    low, high = weight[0, :, :FEATS], weight[0, :, FEATS:]
    keep = jnp.where(core == 0, low, high).astype(BF16)
    send = jnp.where(core == 0, high, low).astype(BF16)
    got = lax.ppermute(send, "latent", swapped(8, 1))
    turned = lax.ppermute(jnp.concatenate([keep, got], axis=0), PLANE, TRANSPOSED)
    return [turned] + [lax.ppermute(turned, "token", swapped(4, step)) for step in range(1, 4)]


def body(
    streams, active_latents, enc_weight, enc_moment, enc_second, dec_weight, dec_moment, dec_second
):
    tokens_all = ROWS * 4
    enc_scale = 1.0 / math.sqrt(8 * 8192)
    dec_scale = 1.0 / math.sqrt(K)
    core = jnp.bitwise_and(lax.axis_index("latent"), 1)
    row = lax.axis_index("token")
    own_rows = streams[0]
    enc_parts = gather_weight(enc_weight, core)
    owner = active_latents // OWN
    turned = jnp.bitwise_xor(owner, row * 2 + core)
    local = active_latents + (turned - owner) * OWN
    index = local.reshape(GROUP_SIZE, 2, 8, K).transpose(0, 2, 1, 3).reshape(ROWS // 2, 2 * K)
    slots = find_slots(local.T).T
    pre_partial = pre_sums(own_rows, enc_parts, index)
    dec_held, pre_partial = lax.optimization_barrier((dec_weight, pre_partial))
    dec_parts = gather_weight(dec_held, core)
    codes = group_total(pre_partial, enc_scale)
    back_partial, codes_wide, errors = errors_and_back(codes, slots, own_rows, dec_parts, index, dec_scale)
    rows_in = [row_spec(CHUNK, LATENTS), row_spec(CHUNK, FEATS)]
    dec_keep, dec_send = gradient_call(gradient_body, rows_in, dec_scale / tokens_all, "dec_gradient")(codes_wide, errors)
    backward = group_total(back_partial, dec_scale)
    dec_grads = send_home(dec_keep, dec_send)
    core_list = core.reshape(1)
    dec_out = adam(core_list, dec_grads, dec_weight, dec_moment, dec_second)
    enc_keep, enc_send = gradient_call(
        spread_gradient_body, [row_spec(HALF, LANES)] + rows_in, enc_scale / tokens_all, "enc_gradient"
    )(backward, slots, own_rows)
    enc_grads = send_home(enc_keep, enc_send)
    enc_out = adam(core_list, enc_grads, enc_weight, enc_moment, enc_second)
    return (*enc_out, *dec_out)


def solution(mesh):
    arrays = P("layer", "latent", "token")
    in_specs = (P("layer", "token", "latent"), P("token", None)) + (arrays,) * 6
    return jax.shard_map(body, mesh=mesh, in_specs=in_specs, out_specs=(arrays,) * 6, check_vma=False)
```

```python
import math

import jax
import jax.numpy as jnp
from jax import lax
from jax.experimental import pallas as pl
from jax.experimental.pallas import tpu as pltpu
from jax.sharding import PartitionSpec as P

K = 64
ADAM_STEP = 100
LATENTS = 384
OWN = 48
PAIR = 96
LANES = 128
PARTS = LATENTS // LANES
ROWS = 1024
FEATS = 1024
GROUP = ("layer", "latent")
GROUP_SIZE = 64
PLANE = ("latent", "token")
CHUNK = 256
CHUNKS = ROWS // CHUNK
HALF = CHUNK // 2
F32 = jnp.float32
BF16 = jnp.bfloat16
VMEM_BYTES = 20 * 1024 * 1024
SIDE = LATENTS // 2


def place(z, core, y):
    return (z * 2 + core) * 4 + y


def plane_pairs(target):
    return [
        (place(z, core, y), place(*target(z, core, y)))
        for z in range(4)
        for core in range(2)
        for y in range(4)
    ]


TRANSPOSED = plane_pairs(lambda z, core, y: (y, core, z))


def homeward(step):
    return plane_pairs(lambda z, core, y: (y ^ step, core, z))


def swapped(count, step):
    return [(i, i ^ step) for i in range(count)]


def params():
    return pltpu.CompilerParams(vmem_limit_bytes=VMEM_BYTES)


def cost(flops, moved):
    return pl.CostEstimate(flops=flops, bytes_accessed=moved, transcendentals=0)


def lane_take(table, column):
    return jnp.take_along_axis(table, column, axis=1, mode="promise_in_bounds")


def compact(dense, index):
    pairs = dense.reshape(dense.shape[0] // 16, 2, 8, LATENTS)
    first = pairs[:, 0].reshape(dense.shape[0] // 2, LATENTS)
    second = pairs[:, 1].reshape(dense.shape[0] // 2, LATENTS)
    column = jnp.bitwise_and(index, LANES - 1)
    part = jnp.right_shift(index, 7)
    low = lax.broadcasted_iota(jnp.int32, index.shape, 1) < K
    out = None
    for q in range(PARTS):
        cut = slice(q * LANES, (q + 1) * LANES)
        found = jnp.where(low, lane_take(first[:, cut], column), lane_take(second[:, cut], column))
        out = found if out is None else jnp.where(part == q, found, out)
    return out


def spread(packed, slot):
    rows = slot.shape[0]
    pairs = slot.reshape(rows // 16, 2, 8, LATENTS)
    sides = []
    for side in range(2):
        at = pairs[:, side].reshape(rows // 2, LATENTS)
        cols = []
        for q in range(PARTS):
            here = at[:, q * LANES : (q + 1) * LANES]
            cols.append(jnp.where(here >= 0, lane_take(packed, jnp.bitwise_and(here, LANES - 1)), 0.0))
        sides.append(jnp.concatenate(cols, axis=1).reshape(rows // 16, 1, 8, LATENTS))
    return jnp.concatenate(sides, axis=1).reshape(rows, LATENTS).astype(BF16)


def slot_kernel(place_ref, active_ref, index_ref, slot_ref, local, table):
    width = active_ref.shape[1]
    active = active_ref[...]
    owner = jnp.right_shift(active * 1366, 16)
    side = jnp.bitwise_xor(jnp.bitwise_and(owner, 1), place_ref[1])
    step = jnp.bitwise_xor(jnp.right_shift(owner, 1), place_ref[0])
    local[...] = side * SIDE + step * OWN + (active - owner * OWN)
    turned = local[...].T.reshape(width // 16, 2, 8, K)
    index_ref[...] = jnp.concatenate(
        [turned[:, 0].reshape(width // 2, K), turned[:, 1].reshape(width // 2, K)], axis=1
    )
    token = lax.broadcasted_iota(jnp.int32, (64, width), 1)
    lift = jnp.where(jnp.bitwise_and(token, 8) > 0, K, 0)
    for block in range(LATENTS // 64):
        ids = lax.broadcasted_iota(jnp.int32, (64, width), 0) + block * 64

        def look(k, held):
            return jnp.where(ids == local[pl.ds(k, 1), :], k, held)

        held = lax.fori_loop(0, K, look, jnp.full((64, width), -1, jnp.int32), unroll=16)
        table[block * 64 : (block + 1) * 64, :] = jnp.where(held >= 0, held + lift, -1)
    slot_ref[...] = table[...].T


def find_slots(position, active_t):
    return pl.pallas_call(
        slot_kernel,
        grid_spec=pltpu.PrefetchScalarGridSpec(
            num_scalar_prefetch=1,
            grid=(ROWS // LANES,),
            in_specs=[pl.BlockSpec((K, LANES), lambda i, at: (0, i))],
            out_specs=[
                pl.BlockSpec((LANES // 2, LANES), lambda i, at: (i, 0)),
                pl.BlockSpec((LANES, LATENTS), lambda i, at: (i, 0)),
            ],
            scratch_shapes=[pltpu.VMEM((K, LANES), jnp.int32), pltpu.VMEM((LATENTS, LANES), jnp.int32)],
        ),
        out_shape=[
            jax.ShapeDtypeStruct((ROWS // 2, LANES), jnp.int32),
            jax.ShapeDtypeStruct((ROWS, LATENTS), jnp.int32),
        ],
        compiler_params=params(),
        cost_estimate=cost(LATENTS * ROWS * K * 16, 2 * 1024 * 1024),
        name="find_slots",
    )(position, active_t)


def assemble(parts, whole):
    for step, part in enumerate(parts):
        for side in range(2):
            start = side * SIDE + step * OWN
            whole[start : start + OWN, :] = part[side * OWN : (side + 1) * OWN, :]


def pre_kernel(streams_ref, e0, e1, e2, e3, index_ref, out_ref, weight):
    @pl.when(pl.program_id(0) == 0)
    def _():
        assemble((e0, e1, e2, e3), weight)

    pre = lax.dot_general(
        streams_ref[...], weight[...], (((1,), (1,)), ((), ())), preferred_element_type=F32
    )
    out_ref[...] = compact(pre, index_ref[...])


def whole_spec(shape):
    return pl.BlockSpec(shape, lambda i: (0,) * len(shape))


def row_spec(rows, width):
    return pl.BlockSpec((rows, width), lambda i: (i, 0))


def pre_sums(streams, enc_parts, index):
    return pl.pallas_call(
        pre_kernel,
        grid=(CHUNKS,),
        in_specs=[row_spec(CHUNK, FEATS)]
        + [whole_spec((PAIR, FEATS))] * 4
        + [row_spec(HALF, LANES)],
        out_specs=row_spec(HALF, LANES),
        out_shape=jax.ShapeDtypeStruct((ROWS // 2, LANES), F32),
        scratch_shapes=[pltpu.VMEM((LATENTS, FEATS), BF16)],
        compiler_params=params(),
        cost_estimate=cost(2 * ROWS * FEATS * LATENTS, 4 * 1024 * 1024),
        name="pre_sums",
    )(streams, *enc_parts, index)


def total_kernel(scale, parts_ref, out_ref):
    total = jnp.sum(parts_ref[...], axis=0) * scale
    out_ref[...] = jnp.broadcast_to(total[None], (GROUP_SIZE, 8, LANES)).reshape(GROUP_SIZE * 8, LANES).astype(BF16)


def exchange(partial):
    return lax.all_to_all(partial.reshape(GROUP_SIZE, 8, LANES), GROUP, 0, 0, tiled=True)


def share(parts, scale):
    copies = pl.pallas_call(
        lambda parts_ref, out_ref: total_kernel(scale, parts_ref, out_ref),
        out_shape=jax.ShapeDtypeStruct((ROWS // 2, LANES), BF16),
        compiler_params=params(),
        cost_estimate=cost(GROUP_SIZE * 8 * LANES, 512 * 1024),
        name="group_total",
    )(parts)
    return exchange(copies).reshape(ROWS // 2, LANES)


def errors_body(scale, packed_ref, slot_ref, streams_ref, d0, d1, d2, d3, index_ref, back_ref, codes_ref, errors_ref, weight):
    @pl.when(pl.program_id(0) == 0)
    def _():
        assemble((d0, d1, d2, d3), weight)

    codes = spread(packed_ref[...].astype(F32), slot_ref[...])
    codes_ref[...] = codes
    rebuilt = jnp.dot(codes, weight[...], preferred_element_type=F32) * scale
    errors = (rebuilt - streams_ref[...].astype(F32)).astype(BF16)
    errors_ref[...] = errors
    back = lax.dot_general(errors, weight[...], (((1,), (1,)), ((), ())), preferred_element_type=F32)
    back_ref[...] = compact(back, index_ref[...])


def errors_and_back(packed, slots, streams, dec_parts, index, scale):
    return pl.pallas_call(
        lambda *refs: errors_body(scale, *refs),
        grid=(CHUNKS,),
        in_specs=[row_spec(HALF, LANES), row_spec(CHUNK, LATENTS), row_spec(CHUNK, FEATS)]
        + [whole_spec((PAIR, FEATS))] * 4
        + [row_spec(HALF, LANES)],
        out_specs=[row_spec(HALF, LANES), row_spec(CHUNK, LATENTS), row_spec(CHUNK, FEATS)],
        out_shape=[
            jax.ShapeDtypeStruct((ROWS // 2, LANES), F32),
            jax.ShapeDtypeStruct((ROWS, LATENTS), BF16),
            jax.ShapeDtypeStruct((ROWS, FEATS), BF16),
        ],
        scratch_shapes=[pltpu.VMEM((LATENTS, FEATS), BF16)],
        compiler_params=params(),
        cost_estimate=cost(4 * ROWS * FEATS * LATENTS, 8 * 1024 * 1024),
        name="errors_and_back",
    )(packed, slots, streams, *dec_parts, index)


def accumulate(part, total):
    step = pl.program_id(0)

    @pl.when(step == 0)
    def _():
        total[...] = part

    @pl.when(step > 0)
    def _():
        total[...] += part


def dec_gradient_body(scale, codes_ref, errors_ref, keep_ref, send_ref, total):
    part = lax.dot_general(codes_ref[...], errors_ref[...], (((0,), (0,)), ((), ())), preferred_element_type=F32)
    accumulate(part, total)

    @pl.when(pl.program_id(0) == CHUNKS - 1)
    def _():
        for step in range(4):
            for side, out_ref in enumerate((keep_ref, send_ref)):
                start = side * SIDE + step * OWN
                out_ref[step] = (total[start : start + OWN, :] * scale).astype(BF16)


def dec_gradient(codes, errors, scale):
    return pl.pallas_call(
        lambda *refs: dec_gradient_body(scale, *refs),
        grid=(CHUNKS,),
        in_specs=[row_spec(CHUNK, LATENTS), row_spec(CHUNK, FEATS)],
        out_specs=[whole_spec((4, OWN, FEATS))] * 2,
        out_shape=[jax.ShapeDtypeStruct((4, OWN, FEATS), BF16)] * 2,
        scratch_shapes=[pltpu.VMEM((LATENTS, FEATS), F32)],
        compiler_params=params(),
        cost_estimate=cost(2 * ROWS * FEATS * LATENTS, 4 * 1024 * 1024),
        name="dec_gradient",
    )(codes, errors)


def enc_gradient_body(scale, packed_ref, slot_ref, near_ref, far_ref, g0, g1, g2, g3, total):
    codes = spread(packed_ref[...].astype(F32), slot_ref[...])[:, :SIDE]
    parts = [
        lax.dot_general(codes, ref[...], (((0,), (0,)), ((), ())), preferred_element_type=F32)
        for ref in (near_ref, far_ref)
    ]
    accumulate(jnp.concatenate(parts, axis=1), total)

    @pl.when(pl.program_id(0) == CHUNKS - 1)
    def _():
        for step, out_ref in enumerate((g0, g1, g2, g3)):
            out_ref[...] = (total[step * OWN : (step + 1) * OWN, :] * scale).astype(BF16)


def enc_gradient(packed, slots, near, far, scale):
    return pl.pallas_call(
        lambda *refs: enc_gradient_body(scale, *refs),
        grid=(CHUNKS,),
        in_specs=[row_spec(HALF, LANES), row_spec(CHUNK, LATENTS)] + [row_spec(CHUNK, FEATS)] * 2,
        out_specs=[whole_spec((OWN, 2 * FEATS))] * 4,
        out_shape=[jax.ShapeDtypeStruct((OWN, 2 * FEATS), BF16)] * 4,
        scratch_shapes=[pltpu.VMEM((SIDE, 2 * FEATS), F32)],
        compiler_params=params(),
        cost_estimate=cost(2 * ROWS * FEATS * LATENTS, 6 * 1024 * 1024),
        name="enc_gradient",
    )(packed, slots, near, far)


def send_home(parts):
    return [lax.ppermute(part, PLANE, homeward(step)) for step, part in enumerate(parts)]


def adam_kernel(core_ref, g0, g1, g2, g3, weight_ref, moment_ref, second_ref, weight_out, moment_out, second_out):
    gradient = g0[...].astype(F32) + g1[...].astype(F32) + g2[...].astype(F32) + g3[...].astype(F32)
    moment_new = 0.9 * moment_ref[0] + 0.1 * gradient
    second_new = 0.999 * second_ref[0] + 0.001 * gradient * gradient
    first_fix = 1.0 - 0.9**ADAM_STEP
    second_fix = 1.0 - 0.999**ADAM_STEP
    weight_out[0] = weight_ref[0] - 0.2 * (moment_new / first_fix) / (jnp.sqrt(second_new / second_fix) + 1e-08)
    moment_out[0] = moment_new
    second_out[0] = second_new


def adam(core, grads, weight, moment, second):
    near = pl.BlockSpec((OWN, FEATS), lambda i, core_ref: (0, i))
    far = pl.BlockSpec((1, OWN, FEATS), lambda i, core_ref: (0, 0, jnp.bitwise_xor(i, core_ref[0])))
    shape = jax.ShapeDtypeStruct(weight.shape, F32)
    return pl.pallas_call(
        adam_kernel,
        grid_spec=pltpu.PrefetchScalarGridSpec(
            num_scalar_prefetch=1, grid=(2,), in_specs=[near] * 4 + [far] * 3, out_specs=[far] * 3
        ),
        out_shape=[shape] * 3,
        compiler_params=params(),
        cost_estimate=cost(OWN * 2048 * 16, 3 * 1024 * 1024),
        name="adam",
    )(core, *grads, weight, moment, second)


def over_token(turned):
    return [turned] + [lax.ppermute(turned, "token", swapped(4, step)) for step in range(1, 4)]


def body(
    streams, active_latents, enc_weight, enc_moment, enc_second, dec_weight, dec_moment, dec_second
):
    tokens_all = ROWS * 4
    enc_scale = 1.0 / math.sqrt(8 * 8192)
    dec_scale = 1.0 / math.sqrt(K)
    core = jnp.bitwise_and(lax.axis_index("latent"), 1)
    position = jnp.stack([lax.axis_index("token"), core]).astype(jnp.int32)
    own_rows = streams[0]

    both = jnp.concatenate([enc_weight, dec_weight], axis=0).astype(BF16)
    low, high = both[:, :, :FEATS], both[:, :, FEATS:]
    keep = jnp.where(core == 0, low, high)
    got = lax.ppermute(jnp.where(core == 0, high, low), "latent", swapped(8, 1))
    enc_pair = jnp.concatenate([keep[0], got[0]], axis=0)
    dec_pair = jnp.concatenate([keep[1], got[1]], axis=0)
    enc_pair, active_t = lax.optimization_barrier((enc_pair, active_latents.T))
    enc_turned = lax.ppermute(enc_pair, PLANE, TRANSPOSED)
    index, slots = find_slots(position, active_t)
    enc_turned, index, slots, dec_pair = lax.optimization_barrier((enc_turned, index, slots, dec_pair))
    dec_turned = lax.ppermute(dec_pair, PLANE, TRANSPOSED)
    enc_parts = over_token(enc_turned)
    pre_partial = pre_sums(own_rows, enc_parts, index)
    dec_turned, pre_partial, other_rows = lax.optimization_barrier((dec_turned, pre_partial, own_rows))

    codes_sums = exchange(pre_partial)
    dec_parts = over_token(dec_turned)
    far_rows = lax.ppermute(other_rows, "latent", swapped(8, 1))
    codes_sums, dec_parts = lax.optimization_barrier((codes_sums, dec_parts))
    codes = share(codes_sums, enc_scale)
    back_partial, codes_wide, errors = errors_and_back(codes, slots, own_rows, dec_parts, index, dec_scale)

    back_sums = exchange(back_partial)
    dec_keep, dec_send = dec_gradient(codes_wide, errors, dec_scale / tokens_all)
    dec_got = lax.ppermute(dec_send, "latent", swapped(8, 1))
    dec_grads = send_home([jnp.concatenate([dec_keep[step], dec_got[step]], axis=1) for step in range(4)])
    backward = share(back_sums, dec_scale)
    backward, dec_grads, far_rows = lax.optimization_barrier((backward, dec_grads, far_rows))
    enc_parts_out = enc_gradient(backward, slots, own_rows, far_rows, enc_scale / tokens_all)
    enc_grads = send_home(enc_parts_out)
    core_list = core.reshape(1)
    dec_out = adam(core_list, dec_grads, dec_weight, dec_moment, dec_second)
    enc_out = adam(core_list, enc_grads, enc_weight, enc_moment, enc_second)
    return (*enc_out, *dec_out)


def solution(mesh):
    arrays = P("layer", "latent", "token")
    in_specs = (P("layer", "token", "latent"), P("token", None)) + (arrays,) * 6
    return jax.shard_map(body, mesh=mesh, in_specs=in_specs, out_specs=(arrays,) * 6, check_vma=False)
```

```python
import math

import jax
import jax.numpy as jnp
from jax import lax
from jax.experimental import pallas as pl
from jax.experimental.pallas import tpu as pltpu
from jax.sharding import PartitionSpec as P

K = 64
ADAM_STEP = 100
LATENTS = 384
OWN = 48
PAIR = 96
LANES = 128
PARTS = LATENTS // LANES
ROWS = 1024
FEATS = 1024
GROUP = ("layer", "latent")
GROUP_SIZE = 64
PLANE = ("latent", "token")
CHUNK = 256
CHUNKS = ROWS // CHUNK
HALF = CHUNK // 2
F32 = jnp.float32
BF16 = jnp.bfloat16
VMEM_BYTES = 20 * 1024 * 1024
SIDE = LATENTS // 2
QUARTER = 256


def place(z, core, y):
    return (z * 2 + core) * 4 + y


def plane_pairs(target):
    return [
        (place(z, core, y), place(*target(z, core, y)))
        for z in range(4)
        for core in range(2)
        for y in range(4)
    ]


TRANSPOSED = plane_pairs(lambda z, core, y: (y, core, z))
ALONG_Y = plane_pairs(lambda z, core, y: (z, core, z ^ y))
ALONG_Z = plane_pairs(lambda z, core, y: (z ^ y, core, y))


def homeward(step):
    return plane_pairs(lambda z, core, y: (y ^ step, core, z))


def swapped(count, step):
    return [(i, i ^ step) for i in range(count)]


def params():
    return pltpu.CompilerParams(vmem_limit_bytes=VMEM_BYTES)


LITTLE = pl.CostEstimate(flops=1024, bytes_accessed=1024, transcendentals=0)


def in_hbm(*arrays):
    return [pltpu.with_memory_space_constraint(array, pltpu.HBM) for array in arrays]


def lane_take(table, column):
    return jnp.take_along_axis(table, column, axis=1, mode="promise_in_bounds")


def compact(dense, index):
    pairs = dense.reshape(dense.shape[0] // 16, 2, 8, LATENTS)
    first = pairs[:, 0].reshape(dense.shape[0] // 2, LATENTS)
    second = pairs[:, 1].reshape(dense.shape[0] // 2, LATENTS)
    column = jnp.bitwise_and(index, LANES - 1)
    part = jnp.right_shift(index, 7)
    low = lax.broadcasted_iota(jnp.int32, index.shape, 1) < K
    out = None
    for q in range(PARTS):
        cut = slice(q * LANES, (q + 1) * LANES)
        found = jnp.where(low, lane_take(first[:, cut], column), lane_take(second[:, cut], column))
        out = found if out is None else jnp.where(part == q, found, out)
    return out


def spread(packed, slot):
    slot = slot.astype(F32).astype(jnp.int32)
    rows = slot.shape[0]
    pairs = slot.reshape(rows // 16, 2, 8, LATENTS)
    sides = []
    for side in range(2):
        at = pairs[:, side].reshape(rows // 2, LATENTS)
        cols = []
        for q in range(PARTS):
            here = at[:, q * LANES : (q + 1) * LANES]
            cols.append(jnp.where(here >= 0, lane_take(packed, jnp.bitwise_and(here, LANES - 1)), 0.0))
        sides.append(jnp.concatenate(cols, axis=1).reshape(rows // 16, 1, 8, LATENTS))
    return jnp.concatenate(sides, axis=1).reshape(rows, LATENTS).astype(BF16)


def index_kernel(place_ref, active_ref, index_ref, local_ref):
    width = active_ref.shape[1]
    active = active_ref[...]
    owner = jnp.right_shift(active * 1366, 16)
    side = jnp.bitwise_xor(jnp.bitwise_and(owner, 1), place_ref[1])
    step = jnp.bitwise_xor(jnp.right_shift(owner, 1), place_ref[0])
    local = side * SIDE + step * OWN + (active - owner * OWN)
    local_ref[...] = local
    turned = local.T.reshape(width // 16, 2, 8, K)
    index_ref[...] = jnp.concatenate(
        [turned[:, 0].reshape(width // 2, K), turned[:, 1].reshape(width // 2, K)], axis=1
    )


def find_index(position, active_t):
    return pl.pallas_call(
        index_kernel,
        grid_spec=pltpu.PrefetchScalarGridSpec(
            num_scalar_prefetch=1,
            grid=(2,),
            in_specs=[pl.BlockSpec((K, ROWS // 2), lambda i, at: (0, i))],
            out_specs=[
                pl.BlockSpec((ROWS // 4, LANES), lambda i, at: (i, 0)),
                pl.BlockSpec((K, ROWS // 2), lambda i, at: (0, i)),
            ],
        ),
        out_shape=[
            pltpu.HBM((ROWS // 2, LANES), jnp.int32),
            pltpu.HBM((K, ROWS), jnp.int32),
        ],
        compiler_params=params(),
        cost_estimate=LITTLE,
        name="find_index",
    )(position, active_t)


def slot_kernel(local_ref, *refs):
    slot_ref, table = refs[-2:]
    width = local_ref.shape[1]
    token = lax.broadcasted_iota(jnp.int32, (64, width), 1)
    lift = jnp.where(jnp.bitwise_and(token, 8) > 0, K, 0)
    for block in range(LATENTS // 64):
        ids = lax.broadcasted_iota(jnp.int32, (64, width), 0) + block * 64

        def look(k, held):
            return jnp.where(ids == local_ref[pl.ds(k, 1), :], k, held)

        held = lax.fori_loop(0, K, look, jnp.full((64, width), -1, jnp.int32), unroll=16)
        table[block * 64 : (block + 1) * 64, :] = jnp.where(held >= 0, held + lift, -1).astype(F32)
    slot_ref[...] = table[...].T.astype(BF16)


def find_slots(local, piece, before=None):
    steps = CHUNK // LANES
    held = [] if before is None else [before]
    return pl.pallas_call(
        slot_kernel,
        grid=(steps,),
        in_specs=[pl.BlockSpec((K, LANES), lambda i: (0, piece * steps + i))]
        + [pl.BlockSpec(memory_space=pl.ANY)] * len(held),
        out_specs=pl.BlockSpec((LANES, LATENTS), lambda i: (piece * steps + i, 0)),
        out_shape=pltpu.HBM((ROWS, LATENTS), BF16),
        input_output_aliases={1: 0} if held else {},
        scratch_shapes=[pltpu.VMEM((LATENTS, LANES), F32)],
        compiler_params=params(),
        cost_estimate=LITTLE,
        name="find_slots",
    )(*in_hbm(local, *held))


def prefetched(grid, in_specs, out_specs, scratch=()):
    return pltpu.PrefetchScalarGridSpec(
        num_scalar_prefetch=1, grid=grid, in_specs=in_specs, out_specs=out_specs, scratch_shapes=scratch
    )


def quarter_lanes(position, step):
    start = jnp.bitwise_xor(position[0], step) * QUARTER
    return pl.ds(pl.multiple_of(start, QUARTER), QUARTER)


def cast_kernel(position, enc_ref, dec_ref, keep_ref, send_ref):
    for array, ref in enumerate((enc_ref, dec_ref)):
        for turned, out_ref in enumerate((keep_ref, send_ref)):
            start = jnp.bitwise_xor(position[1], turned) * FEATS
            half = ref[0, :, pl.ds(pl.multiple_of(start, FEATS), FEATS)]
            out_ref[array] = half.astype(BF16)


def cast_weights(position, enc, dec):
    return pl.pallas_call(
        cast_kernel,
        grid_spec=prefetched((1,), [whole_spec(enc.shape)] * 2, [whole_spec((2, OWN, FEATS))] * 2),
        out_shape=[jax.ShapeDtypeStruct((2, OWN, FEATS), BF16)] * 2,
        compiler_params=params(),
        cost_estimate=LITTLE,
        name="cast_weights",
    )(position, *in_hbm(enc, dec))


def pair_kernel(keep_ref, got_ref, enc_ref, dec_ref):
    for array, out_ref in enumerate((enc_ref, dec_ref)):
        out_ref[:OWN, :] = keep_ref[array]
        out_ref[OWN:, :] = got_ref[array]


def pair(keep, got):
    return pl.pallas_call(
        pair_kernel,
        out_shape=[jax.ShapeDtypeStruct((PAIR, FEATS), BF16)] * 2,
        compiler_params=params(),
        cost_estimate=LITTLE,
        name="pair",
    )(keep, got)


def over(axis, size, array, step):
    return lax.ppermute(array, axis, swapped(size, step))


def token_gather(near):
    one, three = over("token", 4, near, 1), over("token", 4, near, 3)
    return [near, one, three, over("token", 4, three[:OWN], 1), over("token", 4, one[OWN:], 3)]


def assemble(parts, whole, turn=0):
    near, one, three, two_low, two_high = parts
    for step, part, side in (
        (0, near, 0), (0, near, 1), (1, one, 0), (1, one, 1), (3, three, 0), (3, three, 1), (2, two_low, 0), (2, two_high, 1)
    ):
        start = side * SIDE + jnp.bitwise_xor(step, turn) * OWN
        first = side * OWN if part.shape[0] == PAIR else 0
        whole[pl.ds(pl.multiple_of(start, 16), OWN), :] = part[first : first + OWN, :]


PART_SHAPES = ((PAIR, FEATS),) * 3 + ((OWN, FEATS),) * 2


def pre_kernel(streams_ref, q0, q1, q3, q2a, q2b, index_ref, out_ref, weight):
    @pl.when(pl.program_id(0) == 0)
    def _():
        assemble((q0, q1, q3, q2a, q2b), weight)

    pre = lax.dot_general(
        streams_ref[...], weight[...], (((1,), (1,)), ((), ())), preferred_element_type=F32
    )
    out_ref[...] = compact(pre, index_ref[...])


def whole_spec(shape):
    return pl.BlockSpec(shape, lambda i, *at: (0,) * len(shape))


def row_spec(rows, width):
    return pl.BlockSpec((rows, width), lambda i, *at: (i, 0))


def pre_sums(streams, enc_parts, index):
    return pl.pallas_call(
        pre_kernel,
        grid=(CHUNKS,),
        in_specs=[row_spec(CHUNK, FEATS)]
        + [whole_spec(shape) for shape in PART_SHAPES]
        + [row_spec(HALF, LANES)],
        out_specs=row_spec(HALF, LANES),
        out_shape=jax.ShapeDtypeStruct((ROWS // 2, LANES), F32),
        scratch_shapes=[pltpu.VMEM((LATENTS, FEATS), BF16)],
        compiler_params=params(),
        cost_estimate=LITTLE,
        name="pre_sums",
    )(streams, *enc_parts, *in_hbm(index))


def total_kernel(scale, parts_ref, out_ref):
    total = jnp.sum(parts_ref[...], axis=0) * scale
    out_ref[...] = jnp.broadcast_to(total[None], (GROUP_SIZE, 8, LANES)).reshape(GROUP_SIZE * 8, LANES).astype(BF16)


def exchange(partial):
    return lax.all_to_all(partial.reshape(GROUP_SIZE, 8, LANES), GROUP, 0, 0, tiled=True)


def share(parts, scale):
    copies = pl.pallas_call(
        lambda parts_ref, out_ref: total_kernel(scale, parts_ref, out_ref),
        out_shape=jax.ShapeDtypeStruct((ROWS // 2, LANES), BF16),
        compiler_params=params(),
        cost_estimate=LITTLE,
        name="group_total",
    )(parts)
    return exchange(copies).reshape(ROWS // 2, LANES)


def accumulate(part, total):
    step = pl.program_id(0)

    @pl.when(step == 0)
    def _():
        total[...] = part

    @pl.when(step > 0)
    def _():
        total[...] += part


def errors_body(
    scale, grad_scale, position, packed_ref, slot_ref, streams_ref, q0, q1, q3, q2a, q2b, index_ref, back_ref, *rest
):
    weight, total = rest[4:]

    @pl.when(pl.program_id(0) == 0)
    def _():
        assemble((q0, q1, q3, q2a, q2b), weight, position[2])

    codes = spread(packed_ref[...].astype(F32), slot_ref[...])
    rebuilt = jnp.dot(codes, weight[...], preferred_element_type=F32) * scale
    errors = (rebuilt - streams_ref[...].astype(F32)).astype(BF16)
    back = lax.dot_general(errors, weight[...], (((1,), (1,)), ((), ())), preferred_element_type=F32)
    back_ref[...] = compact(back, index_ref[...])
    accumulate(
        lax.dot_general(codes, errors, (((0,), (0,)), ((), ())), preferred_element_type=F32), total
    )

    @pl.when(pl.program_id(0) == CHUNKS - 1)
    def _():
        for step in range(4):
            rest[step][...] = (total[:, quarter_lanes(position, step)] * grad_scale).astype(BF16)


def errors_and_back(position, packed, slots, streams, dec_parts, index, scale, grad_scale):
    return pl.pallas_call(
        lambda *refs: errors_body(scale, grad_scale, *refs),
        grid_spec=prefetched(
            (CHUNKS,),
            [row_spec(HALF, LANES), row_spec(CHUNK, LATENTS), row_spec(CHUNK, FEATS)]
            + [whole_spec(shape) for shape in PART_SHAPES]
            + [row_spec(HALF, LANES)],
            [row_spec(HALF, LANES)] + [whole_spec((LATENTS, QUARTER))] * 4,
            [pltpu.VMEM((LATENTS, FEATS), BF16), pltpu.VMEM((LATENTS, FEATS), F32)],
        ),
        out_shape=[jax.ShapeDtypeStruct((ROWS // 2, LANES), F32)] + [pltpu.HBM((LATENTS, QUARTER), BF16)] * 4,
        compiler_params=params(),
        cost_estimate=LITTLE,
        name="errors_and_back",
    )(position, packed, *in_hbm(slots, streams, *dec_parts, index))


def dec_total_kernel(p0, p1, p2, p3, keep_ref, send_ref):
    for side, out_ref in enumerate((keep_ref, send_ref)):
        for block in range(4):
            sums = None
            for step, part in enumerate((p0, p1, p2, p3)):
                start = side * SIDE + (block ^ step) * OWN
                term = part[start : start + OWN, :].astype(F32)
                sums = term if sums is None else sums + term
            out_ref[block * OWN : (block + 1) * OWN, :] = sums.astype(BF16)


def dec_total(parts):
    return pl.pallas_call(
        dec_total_kernel,
        out_shape=[pltpu.HBM((SIDE, QUARTER), BF16), jax.ShapeDtypeStruct((SIDE, QUARTER), BF16)],
        compiler_params=params(),
        cost_estimate=LITTLE,
        name="dec_total",
    )(*in_hbm(*parts))


def enc_gradient_body(scale, packed_ref, slot_ref, near_ref, far_ref, keep_ref, got_ref, g0, g1, g2, g3, total):
    codes = spread(packed_ref[...].astype(F32), slot_ref[...])[:, :SIDE]
    parts = [
        lax.dot_general(codes, ref[...], (((0,), (0,)), ((), ())), preferred_element_type=F32)
        for ref in (near_ref, far_ref)
    ]
    accumulate(jnp.concatenate(parts, axis=1), total)

    @pl.when(pl.program_id(0) == CHUNKS - 1)
    def _():
        for step, out_ref in enumerate((g0, g1, g2, g3)):
            rows = slice(step * OWN, (step + 1) * OWN)
            out_ref[:, : 2 * FEATS] = (total[rows, :] * scale).astype(BF16)
            out_ref[:, 2 * FEATS : 2 * FEATS + QUARTER] = keep_ref[rows, :]
            out_ref[:, 2 * FEATS + QUARTER :] = got_ref[rows, :]


RIDE = 2 * FEATS + 2 * QUARTER


def enc_gradient(packed, slots, near, far, keep, got, scale):
    return pl.pallas_call(
        lambda *refs: enc_gradient_body(scale, *refs),
        grid=(CHUNKS,),
        in_specs=[row_spec(HALF, LANES), row_spec(CHUNK, LATENTS)]
        + [row_spec(CHUNK, FEATS)] * 2
        + [whole_spec((SIDE, QUARTER))] * 2,
        out_specs=[whole_spec((OWN, RIDE))] * 4,
        out_shape=[jax.ShapeDtypeStruct((OWN, RIDE), BF16)] * 4,
        scratch_shapes=[pltpu.VMEM((SIDE, 2 * FEATS), F32)],
        compiler_params=params(),
        cost_estimate=LITTLE,
        name="enc_gradient",
    )(packed, *in_hbm(slots, near, far, keep, got))


def adam_update(gradient, weight, moment, second):
    moment_new = 0.9 * moment + 0.1 * gradient
    second_new = 0.999 * second + 0.001 * gradient * gradient
    first_fix = 1.0 - 0.9**ADAM_STEP
    second_fix = 1.0 - 0.999**ADAM_STEP
    weight_new = weight - 0.2 * (moment_new / first_fix) / (jnp.sqrt(second_new / second_fix) + 1e-08)
    return weight_new, moment_new, second_new


def adam_kernel(position, *refs):
    enc_grads, dec_grads, enc_in, dec_in, enc_out, dec_out = (
        refs[:4], refs[4:8], refs[8:11], refs[11:14], refs[14:17], refs[17:20]
    )
    gradient = sum(ref[...].astype(F32) for ref in enc_grads)
    for out_ref, value in zip(enc_out, adam_update(gradient, *[ref[0] for ref in enc_in])):
        out_ref[0] = value
    for step, ref in enumerate(dec_grads):
        start = jnp.bitwise_xor(position[2], step) * QUARTER
        lanes = pl.ds(pl.multiple_of(start, QUARTER), QUARTER)
        held = [source[0, :, lanes] for source in dec_in]
        for out_ref, value in zip(dec_out, adam_update(ref[...].astype(F32), *held)):
            out_ref[0, :, lanes] = value


def adam(position, grads, enc, dec):
    enc_part = pl.BlockSpec((OWN, FEATS), lambda i, at: (0, i))
    dec_part = pl.BlockSpec((OWN, QUARTER), lambda i, at: (0, 2 * FEATS // QUARTER + i))
    state = pl.BlockSpec((1, OWN, FEATS), lambda i, at: (0, 0, jnp.bitwise_xor(i, at[1])))
    return pl.pallas_call(
        adam_kernel,
        grid_spec=prefetched((2,), [enc_part] * 4 + [dec_part] * 4 + [state] * 6, [state] * 6),
        out_shape=[jax.ShapeDtypeStruct(array.shape, F32) for array in enc + dec],
        compiler_params=params(),
        cost_estimate=LITTLE,
        name="adam",
    )(position, *grads, *grads, *enc, *dec)


def body(
    streams, active_latents, enc_weight, enc_moment, enc_second, dec_weight, dec_moment, dec_second
):
    tokens_all = ROWS * 4
    enc_scale = 1.0 / math.sqrt(8 * 8192)
    dec_scale = 1.0 / math.sqrt(K)
    latent = lax.axis_index("latent")
    row = lax.axis_index("token")
    core = jnp.bitwise_and(latent, 1)
    column = jnp.right_shift(latent, 1)
    position = jnp.stack([row, core, column]).astype(jnp.int32)
    own_rows = streams[0]

    keep, send = cast_weights(position, enc_weight, dec_weight)
    got = over("latent", 8, send, 1)
    index, local = find_index(position, active_latents.T)
    got, local = lax.optimization_barrier((got, local))
    enc_pair, dec_pair = pair(keep, got)
    turned = lax.ppermute(enc_pair, PLANE, TRANSPOSED)
    dec_moved = lax.ppermute(dec_pair, PLANE, ALONG_Y)
    slots = None
    for piece in range(3):
        slots = find_slots(local, piece, slots)
    turned, dec_moved, slots = lax.optimization_barrier((turned, dec_moved, slots))
    enc_parts = token_gather(turned)
    dec_near = lax.ppermute(dec_moved, PLANE, ALONG_Z)
    slots = find_slots(local, 3, slots)
    enc_parts, dec_near, slots = lax.optimization_barrier((enc_parts, dec_near, slots))
    pre_partial = pre_sums(own_rows, enc_parts, index)

    pre_partial, dec_near = lax.optimization_barrier((pre_partial, dec_near))
    code_sums = exchange(pre_partial)
    dec_one, dec_three = over("token", 4, dec_near, 1), over("token", 4, dec_near, 3)
    code_sums, dec_one, dec_three, other_rows = lax.optimization_barrier(
        (code_sums, dec_one, dec_three, own_rows)
    )
    codes = share(code_sums, enc_scale)
    dec_parts = [
        dec_near, dec_one, dec_three, over("token", 4, dec_three[:OWN], 1), over("token", 4, dec_one[OWN:], 3)
    ]
    far_rows = over("latent", 8, other_rows, 1)
    back_partial, *pieces = errors_and_back(
        position, codes, slots, own_rows, dec_parts, index, dec_scale, dec_scale / tokens_all
    )

    back_sums = exchange(back_partial)
    pieces = [pieces[0]] + [over("token", 4, pieces[step], step) for step in range(1, 4)]
    back_sums, pieces[1], pieces[3] = lax.optimization_barrier((back_sums, pieces[1], pieces[3]))
    backward = share(back_sums, dec_scale)
    dec_keep, dec_send = dec_total(pieces)
    dec_got = over("latent", 8, dec_send, 1)
    backward, dec_keep, dec_got, far_rows = lax.optimization_barrier((backward, dec_keep, dec_got, far_rows))
    riders = enc_gradient(backward, slots, own_rows, far_rows, dec_keep, dec_got, enc_scale / tokens_all)
    grads = [lax.ppermute(part, PLANE, homeward(step)) for step, part in enumerate(riders)]
    return tuple(
        adam(position, grads, [enc_weight, enc_moment, enc_second], [dec_weight, dec_moment, dec_second])
    )


def solution(mesh):
    arrays = P("layer", "latent", "token")
    in_specs = (P("layer", "token", "latent"), P("token", None)) + (arrays,) * 6
    return jax.shard_map(body, mesh=mesh, in_specs=in_specs, out_specs=(arrays,) * 6, check_vma=False)
```

```python
import math

import jax
import jax.numpy as jnp
from jax import lax
from jax.experimental import pallas as pl
from jax.experimental.pallas import tpu as pltpu
from jax.sharding import PartitionSpec as P

K = 64
ADAM_STEP = 100
LATENTS = 384
OWN = 48
PAIR = 96
LANES = 128
PARTS = LATENTS // LANES
ROWS = 1024
FEATS = 1024
GROUP = ("layer", "latent")
GROUP_SIZE = 64
PLANE = ("latent", "token")
PIECE = 256
CHUNK = 512
CHUNKS = ROWS // CHUNK
HALF = CHUNK // 2
SHARE = ROWS // 4
BLOCK = SHARE // 4
HALF_STEPS = CHUNKS // 2
F32 = jnp.float32
BF16 = jnp.bfloat16
VMEM_BYTES = 20 * 1024 * 1024
SIDE = LATENTS // 2
QUARTER = 256


def place(z, core, y):
    return (z * 2 + core) * 4 + y


def plane_pairs(target):
    return [
        (place(z, core, y), place(*target(z, core, y)))
        for z in range(4)
        for core in range(2)
        for y in range(4)
    ]


TRANSPOSED = plane_pairs(lambda z, core, y: (y, core, z))
ALONG_Y = plane_pairs(lambda z, core, y: (z, core, z ^ y))
ALONG_Z = plane_pairs(lambda z, core, y: (z ^ y, core, y))


def homeward(step):
    return plane_pairs(lambda z, core, y: (y ^ step, core, z))


def swapped(count, step):
    return [(i, i ^ step) for i in range(count)]


def params():
    return pltpu.CompilerParams(vmem_limit_bytes=VMEM_BYTES)


LITTLE = pl.CostEstimate(flops=1024, bytes_accessed=1024, transcendentals=0)


def in_hbm(*arrays):
    return [pltpu.with_memory_space_constraint(array, pltpu.HBM) for array in arrays]


def lane_take(table, column):
    return jnp.take_along_axis(table, column, axis=1, mode="promise_in_bounds")


def compact(dense, index):
    pairs = dense.reshape(dense.shape[0] // 16, 2, 8, LATENTS)
    first = pairs[:, 0].reshape(dense.shape[0] // 2, LATENTS)
    second = pairs[:, 1].reshape(dense.shape[0] // 2, LATENTS)
    column = jnp.bitwise_and(index, LANES - 1)
    part = jnp.right_shift(index, 7)
    low = lax.broadcasted_iota(jnp.int32, index.shape, 1) < K
    out = None
    for q in range(PARTS):
        cut = slice(q * LANES, (q + 1) * LANES)
        found = jnp.where(low, lane_take(first[:, cut], column), lane_take(second[:, cut], column))
        out = found if out is None else jnp.where(part == q, found, out)
    return out


def spread(packed, slot):
    slot = slot.astype(F32).astype(jnp.int32)
    rows = slot.shape[0]
    pairs = slot.reshape(rows // 16, 2, 8, LATENTS)
    sides = []
    for side in range(2):
        at = pairs[:, side].reshape(rows // 2, LATENTS)
        cols = []
        for q in range(PARTS):
            here = at[:, q * LANES : (q + 1) * LANES]
            cols.append(jnp.where(here >= 0, lane_take(packed, jnp.bitwise_and(here, LANES - 1)), 0.0))
        sides.append(jnp.concatenate(cols, axis=1).reshape(rows // 16, 1, 8, LATENTS))
    return jnp.concatenate(sides, axis=1).reshape(rows, LATENTS).astype(BF16)


def index_kernel(place_ref, active_ref, index_ref, local_ref):
    width = active_ref.shape[1]
    active = active_ref[...]
    owner = jnp.right_shift(active * 1366, 16)
    side = jnp.bitwise_xor(jnp.bitwise_and(owner, 1), place_ref[1])
    step = jnp.bitwise_xor(jnp.right_shift(owner, 1), place_ref[0])
    local = side * SIDE + step * OWN + (active - owner * OWN)
    local_ref[...] = local
    turned = local.T.reshape(width // 16, 2, 8, K)
    index_ref[...] = jnp.concatenate(
        [turned[:, 0].reshape(width // 2, K), turned[:, 1].reshape(width // 2, K)], axis=1
    )


def find_index(position, active_t):
    return pl.pallas_call(
        index_kernel,
        grid_spec=pltpu.PrefetchScalarGridSpec(
            num_scalar_prefetch=1,
            grid=(2,),
            in_specs=[pl.BlockSpec((K, ROWS // 2), lambda i, at: (0, i))],
            out_specs=[
                pl.BlockSpec((ROWS // 4, LANES), lambda i, at: (i, 0)),
                pl.BlockSpec((K, ROWS // 2), lambda i, at: (0, i)),
            ],
        ),
        out_shape=[
            jax.ShapeDtypeStruct((ROWS // 2, LANES), jnp.int32),
            jax.ShapeDtypeStruct((K, ROWS), jnp.int32),
        ],
        compiler_params=params(),
        cost_estimate=LITTLE,
        name="find_index",
    )(position, active_t)


def slot_kernel(local_ref, *refs):
    slot_ref, table = refs[-2:]
    width = local_ref.shape[1]
    token = lax.broadcasted_iota(jnp.int32, (64, width), 1)
    lift = jnp.where(jnp.bitwise_and(token, 8) > 0, K, 0)
    for block in range(LATENTS // 64):
        ids = lax.broadcasted_iota(jnp.int32, (64, width), 0) + block * 64

        def look(k, held):
            return jnp.where(ids == local_ref[pl.ds(k, 1), :], k, held)

        held = lax.fori_loop(0, K, look, jnp.full((64, width), -1, jnp.int32), unroll=16)
        table[block * 64 : (block + 1) * 64, :] = jnp.where(held >= 0, held + lift, -1).astype(F32)
    slot_ref[...] = table[...].T.astype(BF16)


def find_slots(local, piece, before=None):
    steps = PIECE // LANES
    held = [] if before is None else [before]
    return pl.pallas_call(
        slot_kernel,
        grid=(steps,),
        in_specs=[pl.BlockSpec((K, LANES), lambda i: (0, piece * steps + i))]
        + [pl.BlockSpec(memory_space=pl.ANY)] * len(held),
        out_specs=pl.BlockSpec((LANES, LATENTS), lambda i: (piece * steps + i, 0)),
        out_shape=pltpu.HBM((ROWS, LATENTS), BF16),
        input_output_aliases={1: 0} if held else {},
        scratch_shapes=[pltpu.VMEM((LATENTS, LANES), F32)],
        compiler_params=params(),
        cost_estimate=LITTLE,
        name="find_slots",
    )(local, *in_hbm(*held))


def prefetched(grid, in_specs, out_specs, scratch=()):
    return pltpu.PrefetchScalarGridSpec(
        num_scalar_prefetch=1, grid=grid, in_specs=in_specs, out_specs=out_specs, scratch_shapes=scratch
    )


def quarter_lanes(position, step):
    start = jnp.bitwise_xor(position[0], step) * QUARTER
    return pl.ds(pl.multiple_of(start, QUARTER), QUARTER)


def cast_kernel(position, enc_ref, dec_ref, keep_ref, send_ref):
    for array, ref in enumerate((enc_ref, dec_ref)):
        for turned, out_ref in enumerate((keep_ref, send_ref)):
            start = jnp.bitwise_xor(position[1], turned) * FEATS
            half = ref[0, :, pl.ds(pl.multiple_of(start, FEATS), FEATS)]
            out_ref[array] = half.astype(BF16)


def cast_weights(position, enc, dec):
    return pl.pallas_call(
        cast_kernel,
        grid_spec=prefetched((1,), [whole_spec(enc.shape)] * 2, [whole_spec((2, OWN, FEATS))] * 2),
        out_shape=[jax.ShapeDtypeStruct((2, OWN, FEATS), BF16)] * 2,
        compiler_params=params(),
        cost_estimate=LITTLE,
        name="cast_weights",
    )(position, *in_hbm(enc, dec))


def pair_kernel(keep_ref, got_ref, enc_ref, dec_ref):
    for array, out_ref in enumerate((enc_ref, dec_ref)):
        out_ref[:OWN, :] = keep_ref[array]
        out_ref[OWN:, :] = got_ref[array]


def pair(keep, got):
    return pl.pallas_call(
        pair_kernel,
        out_shape=[jax.ShapeDtypeStruct((PAIR, FEATS), BF16)] * 2,
        compiler_params=params(),
        cost_estimate=LITTLE,
        name="pair",
    )(keep, got)


def over(axis, size, array, step):
    return lax.ppermute(array, axis, swapped(size, step))


def token_gather(near):
    one, three = over("token", 4, near, 1), over("token", 4, near, 3)
    return [near, one, three, over("token", 4, three[:OWN], 1), over("token", 4, one[OWN:], 3)]


def assemble(parts, whole, turn=0):
    near, one, three, two_low, two_high = parts
    for step, part, side in (
        (0, near, 0), (0, near, 1), (1, one, 0), (1, one, 1), (3, three, 0), (3, three, 1), (2, two_low, 0), (2, two_high, 1)
    ):
        start = side * SIDE + jnp.bitwise_xor(step, turn) * OWN
        first = side * OWN if part.shape[0] == PAIR else 0
        whole[pl.ds(pl.multiple_of(start, 16), OWN), :] = part[first : first + OWN, :]


PART_SHAPES = ((PAIR, FEATS),) * 3 + ((OWN, FEATS),) * 2


def put_half(position, value, keep_ref, send_ref):
    step = pl.program_id(0)
    start = (step % HALF_STEPS) * HALF
    rows = pl.ds(pl.multiple_of(start, HALF), HALF)
    mine = step // HALF_STEPS == position[1]

    @pl.when(mine)
    def _():
        keep_ref[rows, :] = value

    @pl.when(jnp.logical_not(mine))
    def _():
        send_ref[rows, :] = value


def get_half(position, own_ref, other_ref):
    step = pl.program_id(0)
    mine = step // HALF_STEPS == position[1]
    return jnp.where(mine, own_ref[...].astype(F32), other_ref[...].astype(F32))


def pre_kernel(position, streams_ref, q0, q1, q3, q2a, q2b, index_ref, keep_ref, send_ref, weight):
    @pl.when(pl.program_id(0) == 0)
    def _():
        assemble((q0, q1, q3, q2a, q2b), weight)

    pre = lax.dot_general(
        streams_ref[...], weight[...], (((1,), (1,)), ((), ())), preferred_element_type=F32
    )
    put_half(position, compact(pre, index_ref[...]), keep_ref, send_ref)


def whole_spec(shape):
    return pl.BlockSpec(shape, lambda i, *at: (0,) * len(shape))


def row_spec(rows, width):
    return pl.BlockSpec((rows, width), lambda i, *at: (i, 0))


def half_spec():
    return pl.BlockSpec((HALF, LANES), lambda i, *at: (i % HALF_STEPS, 0))


def pre_sums(position, streams, enc_parts, index):
    return pl.pallas_call(
        pre_kernel,
        grid_spec=prefetched(
            (CHUNKS,),
            [row_spec(CHUNK, FEATS)] + [whole_spec(shape) for shape in PART_SHAPES] + [row_spec(HALF, LANES)],
            [whole_spec((SHARE, LANES))] * 2,
            [pltpu.VMEM((LATENTS, FEATS), BF16)],
        ),
        out_shape=[jax.ShapeDtypeStruct((SHARE, LANES), F32)] * 2,
        compiler_params=params(),
        cost_estimate=LITTLE,
        name="pre_sums",
    )(position, streams, *enc_parts, index)


def fold_kernel(position, keep_ref, got_ref, *out_refs):
    for step, out_ref in enumerate(out_refs):
        start = jnp.bitwise_xor(position[2], step) * BLOCK
        rows = pl.ds(pl.multiple_of(start, BLOCK), BLOCK)
        out_ref[...] = keep_ref[rows, :] + got_ref[rows, :]


def fold(position, keep, got):
    return pl.pallas_call(
        fold_kernel,
        grid_spec=prefetched((1,), [whole_spec((SHARE, LANES))] * 2, [whole_spec((BLOCK, LANES))] * 4),
        out_shape=[jax.ShapeDtypeStruct((BLOCK, LANES), F32)] * 4,
        compiler_params=params(),
        cost_estimate=LITTLE,
        name="fold",
    )(position, keep, got)


def unfold_kernel(position, *refs):
    out_ref = refs[-1]
    for step, ref in enumerate(refs[:-1]):
        start = jnp.bitwise_xor(position[2], step) * BLOCK
        out_ref[pl.ds(pl.multiple_of(start, BLOCK), BLOCK), :] = ref[...]


def unfold(position, parts):
    return pl.pallas_call(
        unfold_kernel,
        grid_spec=prefetched((1,), [whole_spec((BLOCK, LANES))] * 4, whole_spec((SHARE, LANES))),
        out_shape=jax.ShapeDtypeStruct((SHARE, LANES), BF16),
        compiler_params=params(),
        cost_estimate=LITTLE,
        name="unfold",
    )(position, *parts)


def sum_of_four(parts):
    return (parts[0] + parts[1]) + (parts[2] + parts[3])


def with_partners(axis, parts):
    return [parts[0]] + [over(axis, 8, parts[step], 2 * step) for step in range(1, 4)]


def group_sum(position, keep, send, scale):
    parts = fold(position, keep, over("latent", 8, send, 1))
    block = sum_of_four(with_partners("latent", parts))
    block = sum_of_four(with_partners("layer", [block] * 4))
    total = ((block + over("layer", 8, block, 1)) * scale).astype(BF16)
    own = unfold(position, with_partners("latent", [total] * 4))
    return own, over("latent", 8, own, 1)


def accumulate(part, total):
    step = pl.program_id(0)

    @pl.when(step == 0)
    def _():
        total[...] = part

    @pl.when(step > 0)
    def _():
        total[...] += part


def errors_body(
    scale, grad_scale, position, own_ref, other_ref, slot_ref, streams_ref, q0, q1, q3, q2a, q2b, index_ref, *rest
):
    weight, total = rest[6:]

    @pl.when(pl.program_id(0) == 0)
    def _():
        assemble((q0, q1, q3, q2a, q2b), weight, position[2])

    codes = spread(get_half(position, own_ref, other_ref), slot_ref[...])
    rebuilt = jnp.dot(codes, weight[...], preferred_element_type=F32) * scale
    errors = (rebuilt - streams_ref[...].astype(F32)).astype(BF16)
    back = lax.dot_general(errors, weight[...], (((1,), (1,)), ((), ())), preferred_element_type=F32)
    put_half(position, compact(back, index_ref[...]), rest[0], rest[1])
    accumulate(
        lax.dot_general(codes, errors, (((0,), (0,)), ((), ())), preferred_element_type=F32), total
    )

    @pl.when(pl.program_id(0) == CHUNKS - 1)
    def _():
        for step in range(4):
            rest[2 + step][...] = (total[:, quarter_lanes(position, step)] * grad_scale).astype(BF16)


def errors_and_back(position, packed, slots, streams, dec_parts, index, scale, grad_scale):
    return pl.pallas_call(
        lambda *refs: errors_body(scale, grad_scale, *refs),
        grid_spec=prefetched(
            (CHUNKS,),
            [half_spec()] * 2
            + [row_spec(CHUNK, LATENTS), row_spec(CHUNK, FEATS)]
            + [whole_spec(shape) for shape in PART_SHAPES]
            + [row_spec(HALF, LANES)],
            [whole_spec((SHARE, LANES))] * 2 + [whole_spec((LATENTS, QUARTER))] * 4,
            [pltpu.VMEM((LATENTS, FEATS), BF16), pltpu.VMEM((LATENTS, FEATS), F32)],
        ),
        out_shape=[jax.ShapeDtypeStruct((SHARE, LANES), F32)] * 2
        + [jax.ShapeDtypeStruct((LATENTS, QUARTER), BF16)] * 4,
        compiler_params=params(),
        cost_estimate=LITTLE,
        name="errors_and_back",
    )(position, *packed, *in_hbm(slots), streams, *dec_parts, index)


def dec_total_kernel(p0, p1, p2, p3, keep_ref, send_ref):
    for side, out_ref in enumerate((keep_ref, send_ref)):
        for block in range(4):
            sums = None
            for step, part in enumerate((p0, p1, p2, p3)):
                start = side * SIDE + (block ^ step) * OWN
                term = part[start : start + OWN, :].astype(F32)
                sums = term if sums is None else sums + term
            out_ref[block * OWN : (block + 1) * OWN, :] = sums.astype(BF16)


def dec_total(parts):
    return pl.pallas_call(
        dec_total_kernel,
        out_shape=[jax.ShapeDtypeStruct((SIDE, QUARTER), BF16)] * 2,
        compiler_params=params(),
        cost_estimate=LITTLE,
        name="dec_total",
    )(*parts)


def enc_gradient_body(scale, position, own_ref, other_ref, slot_ref, near_ref, far_ref, keep_ref, got_ref, g0, g1, g2, g3, total):
    codes = spread(get_half(position, own_ref, other_ref), slot_ref[...])[:, :SIDE]
    parts = [
        lax.dot_general(codes, ref[...], (((0,), (0,)), ((), ())), preferred_element_type=F32)
        for ref in (near_ref, far_ref)
    ]
    accumulate(jnp.concatenate(parts, axis=1), total)

    @pl.when(pl.program_id(0) == CHUNKS - 1)
    def _():
        for step, out_ref in enumerate((g0, g1, g2, g3)):
            rows = slice(step * OWN, (step + 1) * OWN)
            out_ref[:, : 2 * FEATS] = (total[rows, :] * scale).astype(BF16)
            out_ref[:, 2 * FEATS : 2 * FEATS + QUARTER] = keep_ref[rows, :]
            out_ref[:, 2 * FEATS + QUARTER :] = got_ref[rows, :]


RIDE = 2 * FEATS + 2 * QUARTER


def enc_gradient(position, packed, slots, near, far, keep, got, scale):
    return pl.pallas_call(
        lambda *refs: enc_gradient_body(scale, *refs),
        grid_spec=prefetched(
            (CHUNKS,),
            [half_spec()] * 2
            + [row_spec(CHUNK, LATENTS)]
            + [row_spec(CHUNK, FEATS)] * 2
            + [whole_spec((SIDE, QUARTER))] * 2,
            [whole_spec((OWN, RIDE))] * 4,
            [pltpu.VMEM((SIDE, 2 * FEATS), F32)],
        ),
        out_shape=[jax.ShapeDtypeStruct((OWN, RIDE), BF16)] * 4,
        compiler_params=params(),
        cost_estimate=LITTLE,
        name="enc_gradient",
    )(position, *packed, *in_hbm(slots), near, far, keep, got)


def adam_update(gradient, weight, moment, second):
    moment_new = 0.9 * moment + 0.1 * gradient
    second_new = 0.999 * second + 0.001 * gradient * gradient
    first_fix = 1.0 - 0.9**ADAM_STEP
    second_fix = 1.0 - 0.999**ADAM_STEP
    weight_new = weight - 0.2 * (moment_new / first_fix) / (jnp.sqrt(second_new / second_fix) + 1e-08)
    return weight_new, moment_new, second_new


def adam_kernel(position, *refs):
    enc_grads, dec_grads, enc_in, dec_in, enc_out, dec_out = (
        refs[:4], refs[4:8], refs[8:11], refs[11:14], refs[14:17], refs[17:20]
    )
    gradient = sum(ref[...].astype(F32) for ref in enc_grads)
    for out_ref, value in zip(enc_out, adam_update(gradient, *[ref[0] for ref in enc_in])):
        out_ref[0] = value
    for step, ref in enumerate(dec_grads):
        start = jnp.bitwise_xor(position[2], step) * QUARTER
        lanes = pl.ds(pl.multiple_of(start, QUARTER), QUARTER)
        held = [source[0, :, lanes] for source in dec_in]
        for out_ref, value in zip(dec_out, adam_update(ref[...].astype(F32), *held)):
            out_ref[0, :, lanes] = value


def adam(position, grads, enc, dec):
    enc_part = pl.BlockSpec((OWN, FEATS), lambda i, at: (0, i))
    dec_part = pl.BlockSpec((OWN, QUARTER), lambda i, at: (0, 2 * FEATS // QUARTER + i))
    state = pl.BlockSpec((1, OWN, FEATS), lambda i, at: (0, 0, jnp.bitwise_xor(i, at[1])))
    return pl.pallas_call(
        adam_kernel,
        grid_spec=prefetched((2,), [enc_part] * 4 + [dec_part] * 4 + [state] * 6, [state] * 6),
        out_shape=[jax.ShapeDtypeStruct(array.shape, F32) for array in enc + dec],
        compiler_params=params(),
        cost_estimate=LITTLE,
        name="adam",
    )(position, *grads, *grads, *enc, *dec)


def body(
    streams, active_latents, enc_weight, enc_moment, enc_second, dec_weight, dec_moment, dec_second
):
    tokens_all = ROWS * 4
    enc_scale = 1.0 / math.sqrt(8 * 8192)
    dec_scale = 1.0 / math.sqrt(K)
    latent = lax.axis_index("latent")
    row = lax.axis_index("token")
    core = jnp.bitwise_and(latent, 1)
    column = jnp.right_shift(latent, 1)
    position = jnp.stack([row, core, column]).astype(jnp.int32)
    own_rows = streams[0]

    keep, send = cast_weights(position, enc_weight, dec_weight)
    got = over("latent", 8, send, 1)
    index, local = find_index(position, active_latents.T)
    got, local = lax.optimization_barrier((got, local))
    enc_pair, dec_pair = pair(keep, got)
    turned = lax.ppermute(enc_pair, PLANE, TRANSPOSED)
    dec_moved = lax.ppermute(dec_pair, PLANE, ALONG_Y)
    slots = None
    for piece in range(3):
        slots = find_slots(local, piece, slots)
    turned, dec_moved, slots = lax.optimization_barrier((turned, dec_moved, slots))
    enc_parts = token_gather(turned)
    dec_near = lax.ppermute(dec_moved, PLANE, ALONG_Z)
    slots = find_slots(local, 3, slots)
    enc_parts, dec_near, slots = lax.optimization_barrier((enc_parts, dec_near, slots))
    keep, send = pre_sums(position, own_rows, enc_parts, index)
    codes = group_sum(position, keep, send, enc_scale)
    keep, send, dec_near, other_rows = lax.optimization_barrier((keep, send, dec_near, own_rows))
    dec_parts = token_gather(dec_near)
    far_rows = over("latent", 8, other_rows, 1)
    keep, send, *pieces = errors_and_back(
        position, codes, slots, own_rows, dec_parts, index, dec_scale, dec_scale / tokens_all
    )
    backward = group_sum(position, keep, send, dec_scale)
    pieces = [pieces[0]] + [over("token", 4, pieces[step], step) for step in range(1, 4)]
    dec_keep, dec_send = dec_total(pieces)
    dec_got = over("latent", 8, dec_send, 1)
    riders = enc_gradient(
        position, backward, slots, own_rows, far_rows, dec_keep, dec_got, enc_scale / tokens_all
    )
    grads = [lax.ppermute(part, PLANE, homeward(step)) for step, part in enumerate(riders)]
    return tuple(
        adam(position, grads, [enc_weight, enc_moment, enc_second], [dec_weight, dec_moment, dec_second])
    )


def solution(mesh):
    arrays = P("layer", "latent", "token")
    in_specs = (P("layer", "token", "latent"), P("token", None)) + (arrays,) * 6
    return jax.shard_map(body, mesh=mesh, in_specs=in_specs, out_specs=(arrays,) * 6, check_vma=False)
```

```python
import math

import jax
import jax.numpy as jnp
from jax import lax
from jax.experimental import pallas as pl
from jax.experimental.pallas import tpu as pltpu
from jax.sharding import PartitionSpec as P

K = 64
ADAM_STEP = 100
LATENTS = 384
OWN = 48
PAIR = 96
LANES = 128
PARTS = LATENTS // LANES
ROWS = 1024
FEATS = 1024
GROUP = ("layer", "latent")
GROUP_SIZE = 64
PLANE = ("latent", "token")
PIECE = 256
CHUNK = 512
CHUNKS = ROWS // CHUNK
HALF = CHUNK // 2
SHARE = ROWS // 4
BLOCK = SHARE // 4
HALF_STEPS = CHUNKS // 2
F32 = jnp.float32
BF16 = jnp.bfloat16
VMEM_BYTES = 20 * 1024 * 1024
SIDE = LATENTS // 2
QUARTER = 256


def place(z, core, y):
    return (z * 2 + core) * 4 + y


def plane_pairs(target):
    return [
        (place(z, core, y), place(*target(z, core, y)))
        for z in range(4)
        for core in range(2)
        for y in range(4)
    ]


TRANSPOSED = plane_pairs(lambda z, core, y: (y, core, z))
ALONG_Y = plane_pairs(lambda z, core, y: (z, core, z ^ y))
ALONG_Z = plane_pairs(lambda z, core, y: (z ^ y, core, y))


def homeward(step):
    return plane_pairs(lambda z, core, y: (y ^ step, core, z))


def swapped(count, step):
    return [(i, i ^ step) for i in range(count)]


def params():
    return pltpu.CompilerParams(vmem_limit_bytes=VMEM_BYTES)


LITTLE = pl.CostEstimate(flops=1024, bytes_accessed=1024, transcendentals=0)


def in_hbm(*arrays):
    return [pltpu.with_memory_space_constraint(array, pltpu.HBM) for array in arrays]


def lane_take(table, column):
    return jnp.take_along_axis(table, column, axis=1, mode="promise_in_bounds")


def compact(dense, index):
    pairs = dense.reshape(dense.shape[0] // 16, 2, 8, LATENTS)
    first = pairs[:, 0].reshape(dense.shape[0] // 2, LATENTS)
    second = pairs[:, 1].reshape(dense.shape[0] // 2, LATENTS)
    column = jnp.bitwise_and(index, LANES - 1)
    part = jnp.right_shift(index, 7)
    low = lax.broadcasted_iota(jnp.int32, index.shape, 1) < K
    out = None
    for q in range(PARTS):
        cut = slice(q * LANES, (q + 1) * LANES)
        found = jnp.where(low, lane_take(first[:, cut], column), lane_take(second[:, cut], column))
        out = found if out is None else jnp.where(part == q, found, out)
    return out


def spread(packed, slot):
    slot = slot.astype(F32).astype(jnp.int32)
    rows = slot.shape[0]
    pairs = slot.reshape(rows // 16, 2, 8, LATENTS)
    sides = []
    for side in range(2):
        at = pairs[:, side].reshape(rows // 2, LATENTS)
        cols = []
        for q in range(PARTS):
            here = at[:, q * LANES : (q + 1) * LANES]
            cols.append(jnp.where(here >= 0, lane_take(packed, jnp.bitwise_and(here, LANES - 1)), 0.0))
        sides.append(jnp.concatenate(cols, axis=1).reshape(rows // 16, 1, 8, LATENTS))
    return jnp.concatenate(sides, axis=1).reshape(rows, LATENTS).astype(BF16)


def index_kernel(place_ref, active_ref, index_ref, local_ref):
    width = active_ref.shape[1]
    active = active_ref[...]
    owner = jnp.right_shift(active * 1366, 16)
    side = jnp.bitwise_xor(jnp.bitwise_and(owner, 1), place_ref[1])
    step = jnp.bitwise_xor(jnp.right_shift(owner, 1), place_ref[0])
    local = side * SIDE + step * OWN + (active - owner * OWN)
    local_ref[...] = local
    turned = local.T.reshape(width // 16, 2, 8, K)
    index_ref[...] = jnp.concatenate(
        [turned[:, 0].reshape(width // 2, K), turned[:, 1].reshape(width // 2, K)], axis=1
    )


def find_index(position, active_t):
    return pl.pallas_call(
        index_kernel,
        grid_spec=pltpu.PrefetchScalarGridSpec(
            num_scalar_prefetch=1,
            grid=(2,),
            in_specs=[pl.BlockSpec((K, ROWS // 2), lambda i, at: (0, i))],
            out_specs=[
                pl.BlockSpec((ROWS // 4, LANES), lambda i, at: (i, 0)),
                pl.BlockSpec((K, ROWS // 2), lambda i, at: (0, i)),
            ],
        ),
        out_shape=[
            jax.ShapeDtypeStruct((ROWS // 2, LANES), jnp.int32),
            jax.ShapeDtypeStruct((K, ROWS), jnp.int32),
        ],
        compiler_params=params(),
        cost_estimate=LITTLE,
        name="find_index",
    )(position, active_t)


def slot_kernel(local_ref, *refs):
    slot_ref, table = refs[-2:]
    width = local_ref.shape[1]
    token = lax.broadcasted_iota(jnp.int32, (64, width), 1)
    lift = jnp.where(jnp.bitwise_and(token, 8) > 0, K, 0)
    for block in range(LATENTS // 64):
        ids = lax.broadcasted_iota(jnp.int32, (64, width), 0) + block * 64

        def look(k, held):
            return jnp.where(ids == local_ref[pl.ds(k, 1), :], k, held)

        held = lax.fori_loop(0, K, look, jnp.full((64, width), -1, jnp.int32), unroll=16)
        table[block * 64 : (block + 1) * 64, :] = jnp.where(held >= 0, held + lift, -1).astype(F32)
    slot_ref[...] = table[...].T.astype(BF16)


def find_slots(local, piece, before=None):
    steps = PIECE // LANES
    held = [] if before is None else [before]
    return pl.pallas_call(
        slot_kernel,
        grid=(steps,),
        in_specs=[pl.BlockSpec((K, LANES), lambda i: (0, piece * steps + i))]
        + [pl.BlockSpec(memory_space=pl.ANY)] * len(held),
        out_specs=pl.BlockSpec((LANES, LATENTS), lambda i: (piece * steps + i, 0)),
        out_shape=pltpu.HBM((ROWS, LATENTS), BF16),
        input_output_aliases={1: 0} if held else {},
        scratch_shapes=[pltpu.VMEM((LATENTS, LANES), F32)],
        compiler_params=params(),
        cost_estimate=LITTLE,
        name="find_slots",
    )(local, *in_hbm(*held))


def prefetched(grid, in_specs, out_specs, scratch=()):
    return pltpu.PrefetchScalarGridSpec(
        num_scalar_prefetch=1, grid=grid, in_specs=in_specs, out_specs=out_specs, scratch_shapes=scratch
    )


def quarter_lanes(position, step):
    start = jnp.bitwise_xor(position[0], step) * QUARTER
    return pl.ds(pl.multiple_of(start, QUARTER), QUARTER)


def cast_kernel(position, enc_ref, dec_ref, keep_ref, send_ref):
    for array, ref in enumerate((enc_ref, dec_ref)):
        for turned, out_ref in enumerate((keep_ref, send_ref)):
            start = jnp.bitwise_xor(position[1], turned) * FEATS
            half = ref[0, :, pl.ds(pl.multiple_of(start, FEATS), FEATS)]
            out_ref[array] = half.astype(BF16)


def cast_weights(position, enc, dec):
    return pl.pallas_call(
        cast_kernel,
        grid_spec=prefetched((1,), [whole_spec(enc.shape)] * 2, [whole_spec((2, OWN, FEATS))] * 2),
        out_shape=[jax.ShapeDtypeStruct((2, OWN, FEATS), BF16)] * 2,
        compiler_params=params(),
        cost_estimate=LITTLE,
        name="cast_weights",
    )(position, *in_hbm(enc, dec))


def pair_kernel(keep_ref, got_ref, enc_ref, dec_ref):
    for array, out_ref in enumerate((enc_ref, dec_ref)):
        out_ref[:OWN, :] = keep_ref[array]
        out_ref[OWN:, :] = got_ref[array]


def pair(keep, got):
    return pl.pallas_call(
        pair_kernel,
        out_shape=[jax.ShapeDtypeStruct((PAIR, FEATS), BF16)] * 2,
        compiler_params=params(),
        cost_estimate=LITTLE,
        name="pair",
    )(keep, got)


def over(axis, size, array, step):
    return lax.ppermute(array, axis, swapped(size, step))


def token_gather(near):
    one, three = over("token", 4, near, 1), over("token", 4, near, 3)
    return [near, one, three, over("token", 4, three[:OWN], 1), over("token", 4, one[OWN:], 3)]


def assemble(parts, whole, turn=0):
    for step, part in parts:
        for first in range(0, part.shape[0], OWN):
            side = first // OWN if part.shape[0] == PAIR else HALVES[step]
            start = side * SIDE + jnp.bitwise_xor(step & 3, turn) * OWN
            whole[pl.ds(pl.multiple_of(start, 16), OWN), :] = part[first : first + OWN, :]


HALVES = {2: 0, 6: 1}
ENC_SHAPES = ((PAIR, FEATS),) * 3 + ((OWN, FEATS),) * 2
ENC_STEPS = (0, 1, 3, 2, 6)
DEC_SHAPES = ((PAIR, FEATS),) * 4


def put_half(position, value, keep_ref, send_ref):
    step = pl.program_id(0)
    start = (step % HALF_STEPS) * HALF
    rows = pl.ds(pl.multiple_of(start, HALF), HALF)
    mine = step // HALF_STEPS == position[1]

    @pl.when(mine)
    def _():
        keep_ref[rows, :] = value

    @pl.when(jnp.logical_not(mine))
    def _():
        send_ref[rows, :] = value


def unpack(position, parts, packed):
    for step, part in enumerate(parts):
        block = jnp.bitwise_xor(position[2], step) * BLOCK
        for side in range(2):
            start = jnp.bitwise_xor(position[1], side) * SHARE + block
            rows = pl.ds(pl.multiple_of(start, BLOCK), BLOCK)
            packed[rows, :] = part[side * BLOCK : (side + 1) * BLOCK, :]


def packed_rows(packed):
    start = pl.program_id(0) * HALF
    return packed[pl.ds(pl.multiple_of(start, HALF), HALF), :].astype(F32)


def pre_kernel(position, streams_ref, q0, q1, q3, q2a, q2b, index_ref, keep_ref, send_ref, weight):
    @pl.when(pl.program_id(0) == 0)
    def _():
        assemble(list(zip(ENC_STEPS, (q0, q1, q3, q2a, q2b))), weight)

    pre = lax.dot_general(
        streams_ref[...], weight[...], (((1,), (1,)), ((), ())), preferred_element_type=F32
    )
    put_half(position, compact(pre, index_ref[...]), keep_ref, send_ref)


def whole_spec(shape):
    return pl.BlockSpec(shape, lambda i, *at: (0,) * len(shape))


def row_spec(rows, width):
    return pl.BlockSpec((rows, width), lambda i, *at: (i, 0))


def pre_sums(position, streams, enc_parts, index):
    return pl.pallas_call(
        pre_kernel,
        grid_spec=prefetched(
            (CHUNKS,),
            [row_spec(CHUNK, FEATS)] + [whole_spec(shape) for shape in ENC_SHAPES] + [row_spec(HALF, LANES)],
            [whole_spec((SHARE, LANES))] * 2,
            [pltpu.VMEM((LATENTS, FEATS), BF16)],
        ),
        out_shape=[jax.ShapeDtypeStruct((SHARE, LANES), F32)] * 2,
        compiler_params=params(),
        cost_estimate=LITTLE,
        name="pre_sums",
    )(position, streams, *enc_parts, index)


def fold_kernel(position, keep_ref, got_ref, *out_refs):
    for step, out_ref in enumerate(out_refs):
        start = jnp.bitwise_xor(position[2], step) * BLOCK
        rows = pl.ds(pl.multiple_of(start, BLOCK), BLOCK)
        out_ref[...] = keep_ref[rows, :] + got_ref[rows, :]


def fold(position, keep, got):
    return pl.pallas_call(
        fold_kernel,
        grid_spec=prefetched((1,), [whole_spec((SHARE, LANES))] * 2, [whole_spec((BLOCK, LANES))] * 4),
        out_shape=[jax.ShapeDtypeStruct((BLOCK, LANES), F32)] * 4,
        compiler_params=params(),
        cost_estimate=LITTLE,
        name="fold",
    )(position, keep, got)


def couple_kernel(own_ref, other_ref, out_ref):
    out_ref[:BLOCK, :] = own_ref[...]
    out_ref[BLOCK:, :] = other_ref[...]


def couple(own, other):
    return pl.pallas_call(
        couple_kernel,
        out_shape=jax.ShapeDtypeStruct((2 * BLOCK, LANES), BF16),
        compiler_params=params(),
        cost_estimate=LITTLE,
        name="couple",
    )(own, other)


def sum_of_four(parts):
    return (parts[0] + parts[1]) + (parts[2] + parts[3])


def with_partners(axis, parts):
    return [parts[0]] + [over(axis, 8, parts[step], 2 * step) for step in range(1, 4)]


def group_sum(position, keep, send, scale):
    parts = fold(position, keep, over("latent", 8, send, 1))
    block = sum_of_four(with_partners("latent", parts))
    block = sum_of_four(with_partners("layer", [block] * 4))
    total = ((block + over("layer", 8, block, 1)) * scale).astype(BF16)
    total = couple(total, over("latent", 8, total, 1))
    return with_partners("latent", [total] * 4)


def accumulate(part, total):
    step = pl.program_id(0)

    @pl.when(step == 0)
    def _():
        total[...] = part

    @pl.when(step > 0)
    def _():
        total[...] += part


def errors_body(
    scale, position, p0, p1, p2, p3, slot_ref, streams_ref, q0, q1, q2, q3, index_ref, keep_ref, send_ref, codes_ref, errors_ref, weight, packed
):
    @pl.when(pl.program_id(0) == 0)
    def _():
        assemble(list(enumerate((q0, q1, q2, q3))), weight, position[2])
        unpack(position, (p0, p1, p2, p3), packed)

    codes = spread(packed_rows(packed), slot_ref[...])
    codes_ref[...] = codes
    rebuilt = jnp.dot(codes, weight[...], preferred_element_type=F32) * scale
    errors = (rebuilt - streams_ref[...].astype(F32)).astype(BF16)
    errors_ref[...] = errors
    back = lax.dot_general(errors, weight[...], (((1,), (1,)), ((), ())), preferred_element_type=F32)
    put_half(position, compact(back, index_ref[...]), keep_ref, send_ref)


def errors_and_back(position, packed, slots, streams, dec_parts, index, scale):
    return pl.pallas_call(
        lambda *refs: errors_body(scale, *refs),
        grid_spec=prefetched(
            (CHUNKS,),
            [whole_spec((2 * BLOCK, LANES))] * 4
            + [row_spec(CHUNK, LATENTS), row_spec(CHUNK, FEATS)]
            + [whole_spec(shape) for shape in DEC_SHAPES]
            + [row_spec(HALF, LANES)],
            [whole_spec((SHARE, LANES))] * 2 + [row_spec(CHUNK, LATENTS), row_spec(CHUNK, FEATS)],
            [pltpu.VMEM((LATENTS, FEATS), BF16), pltpu.VMEM((ROWS // 2, LANES), BF16)],
        ),
        out_shape=[jax.ShapeDtypeStruct((SHARE, LANES), F32)] * 2
        + [jax.ShapeDtypeStruct((ROWS, LATENTS), BF16), jax.ShapeDtypeStruct((ROWS, FEATS), BF16)],
        compiler_params=params(),
        cost_estimate=LITTLE,
        name="errors_and_back",
    )(position, *packed, *in_hbm(slots), streams, *dec_parts, index)


def dec_gradient_body(scale, position, codes_ref, errors_ref, p0, p1, p2, p3, total):
    accumulate(
        lax.dot_general(codes_ref[...], errors_ref[...], (((0,), (0,)), ((), ())), preferred_element_type=F32),
        total,
    )

    @pl.when(pl.program_id(0) == CHUNKS - 1)
    def _():
        for step, out_ref in enumerate((p0, p1, p2, p3)):
            out_ref[...] = (total[:, quarter_lanes(position, step)] * scale).astype(BF16)


def dec_gradient(position, codes, errors, scale):
    return pl.pallas_call(
        lambda *refs: dec_gradient_body(scale, *refs),
        grid_spec=prefetched(
            (CHUNKS,),
            [row_spec(CHUNK, LATENTS), row_spec(CHUNK, FEATS)],
            [whole_spec((LATENTS, QUARTER))] * 4,
            [pltpu.VMEM((LATENTS, FEATS), F32)],
        ),
        out_shape=[jax.ShapeDtypeStruct((LATENTS, QUARTER), BF16)] * 4,
        compiler_params=params(),
        cost_estimate=LITTLE,
        name="dec_gradient",
    )(position, codes, errors)


def dec_total_kernel(p0, p1, p2, p3, keep_ref, send_ref):
    for side, out_ref in enumerate((keep_ref, send_ref)):
        for block in range(4):
            sums = None
            for step, part in enumerate((p0, p1, p2, p3)):
                start = side * SIDE + (block ^ step) * OWN
                term = part[start : start + OWN, :].astype(F32)
                sums = term if sums is None else sums + term
            out_ref[block * OWN : (block + 1) * OWN, :] = sums.astype(BF16)


def dec_total(parts):
    return pl.pallas_call(
        dec_total_kernel,
        out_shape=[jax.ShapeDtypeStruct((SIDE, QUARTER), BF16)] * 2,
        compiler_params=params(),
        cost_estimate=LITTLE,
        name="dec_total",
    )(*parts)


def enc_gradient_body(scale, position, p0, p1, p2, p3, slot_ref, near_ref, far_ref, keep_ref, got_ref, g0, g1, g2, g3, total, packed):
    @pl.when(pl.program_id(0) == 0)
    def _():
        unpack(position, (p0, p1, p2, p3), packed)

    codes = spread(packed_rows(packed), slot_ref[...])[:, :SIDE]
    parts = [
        lax.dot_general(codes, ref[...], (((0,), (0,)), ((), ())), preferred_element_type=F32)
        for ref in (near_ref, far_ref)
    ]
    accumulate(jnp.concatenate(parts, axis=1), total)

    @pl.when(pl.program_id(0) == CHUNKS - 1)
    def _():
        for step, out_ref in enumerate((g0, g1, g2, g3)):
            rows = slice(step * OWN, (step + 1) * OWN)
            out_ref[:, : 2 * FEATS] = (total[rows, :] * scale).astype(BF16)
            out_ref[:, 2 * FEATS : 2 * FEATS + QUARTER] = keep_ref[rows, :]
            out_ref[:, 2 * FEATS + QUARTER :] = got_ref[rows, :]


RIDE = 2 * FEATS + 2 * QUARTER


def enc_gradient(position, packed, slots, near, far, keep, got, scale):
    return pl.pallas_call(
        lambda *refs: enc_gradient_body(scale, *refs),
        grid_spec=prefetched(
            (CHUNKS,),
            [whole_spec((2 * BLOCK, LANES))] * 4
            + [row_spec(CHUNK, LATENTS)]
            + [row_spec(CHUNK, FEATS)] * 2
            + [whole_spec((SIDE, QUARTER))] * 2,
            [whole_spec((OWN, RIDE))] * 4,
            [pltpu.VMEM((SIDE, 2 * FEATS), F32), pltpu.VMEM((ROWS // 2, LANES), BF16)],
        ),
        out_shape=[jax.ShapeDtypeStruct((OWN, RIDE), BF16)] * 4,
        compiler_params=params(),
        cost_estimate=LITTLE,
        name="enc_gradient",
    )(position, *packed, *in_hbm(slots), near, far, keep, got)


def adam_update(gradient, weight, moment, second):
    moment_new = 0.9 * moment + 0.1 * gradient
    second_new = 0.999 * second + 0.001 * gradient * gradient
    first_fix = 1.0 - 0.9**ADAM_STEP
    second_fix = 1.0 - 0.999**ADAM_STEP
    weight_new = weight - 0.2 * (moment_new / first_fix) / (jnp.sqrt(second_new / second_fix) + 1e-08)
    return weight_new, moment_new, second_new


def adam_kernel(position, *refs):
    enc_grads, dec_grads, enc_in, dec_in, enc_out, dec_out = (
        refs[:4], refs[4:8], refs[8:11], refs[11:14], refs[14:17], refs[17:20]
    )
    gradient = sum(ref[...].astype(F32) for ref in enc_grads)
    for out_ref, value in zip(enc_out, adam_update(gradient, *[ref[0] for ref in enc_in])):
        out_ref[0] = value
    for step, ref in enumerate(dec_grads):
        start = jnp.bitwise_xor(position[2], step) * QUARTER
        lanes = pl.ds(pl.multiple_of(start, QUARTER), QUARTER)
        held = [source[0, :, lanes] for source in dec_in]
        for out_ref, value in zip(dec_out, adam_update(ref[...].astype(F32), *held)):
            out_ref[0, :, lanes] = value


def adam(position, grads, enc, dec):
    enc_part = pl.BlockSpec((OWN, FEATS), lambda i, at: (0, i))
    dec_part = pl.BlockSpec((OWN, QUARTER), lambda i, at: (0, 2 * FEATS // QUARTER + i))
    state = pl.BlockSpec((1, OWN, FEATS), lambda i, at: (0, 0, jnp.bitwise_xor(i, at[1])))
    return pl.pallas_call(
        adam_kernel,
        grid_spec=prefetched((2,), [enc_part] * 4 + [dec_part] * 4 + [state] * 6, [state] * 6),
        out_shape=[jax.ShapeDtypeStruct(array.shape, F32) for array in enc + dec],
        compiler_params=params(),
        cost_estimate=LITTLE,
        name="adam",
    )(position, *grads, *grads, *enc, *dec)


def body(
    streams, active_latents, enc_weight, enc_moment, enc_second, dec_weight, dec_moment, dec_second
):
    tokens_all = ROWS * 4
    enc_scale = 1.0 / math.sqrt(8 * 8192)
    dec_scale = 1.0 / math.sqrt(K)
    latent = lax.axis_index("latent")
    row = lax.axis_index("token")
    core = jnp.bitwise_and(latent, 1)
    column = jnp.right_shift(latent, 1)
    position = jnp.stack([row, core, column]).astype(jnp.int32)
    own_rows = streams[0]

    keep, send = cast_weights(position, enc_weight, dec_weight)
    got = over("latent", 8, send, 1)
    index, local = find_index(position, active_latents.T)
    got, local = lax.optimization_barrier((got, local))
    enc_pair, dec_pair = pair(keep, got)
    enc_pair, dec_pair, other_rows = lax.optimization_barrier((enc_pair, dec_pair, own_rows))
    turned = lax.ppermute(enc_pair, PLANE, TRANSPOSED)
    dec_moved = lax.ppermute(dec_pair, PLANE, ALONG_Y)
    far_rows = over("latent", 8, other_rows, 1)
    slots = None
    for piece in range(ROWS // PIECE):
        slots = find_slots(local, piece, slots)
    turned, dec_moved, slots, far_rows = lax.optimization_barrier((turned, dec_moved, slots, far_rows))
    enc_parts = token_gather(turned)
    dec_near = lax.ppermute(dec_moved, PLANE, ALONG_Z)
    enc_parts, dec_near = lax.optimization_barrier((enc_parts, dec_near))
    keep, send = pre_sums(position, own_rows, enc_parts, index)
    codes = group_sum(position, keep, send, enc_scale)
    keep, send, dec_near = lax.optimization_barrier((keep, send, dec_near))
    dec_parts = [dec_near] + [over("token", 4, dec_near, step) for step in range(1, 4)]
    keep, send, codes_wide, errors = errors_and_back(position, codes, slots, own_rows, dec_parts, index, dec_scale)
    backward = group_sum(position, keep, send, dec_scale)
    keep, send, codes_wide, errors = lax.optimization_barrier((keep, send, codes_wide, errors))
    pieces = dec_gradient(position, codes_wide, errors, dec_scale / tokens_all)
    pieces = [pieces[0]] + [over("token", 4, pieces[step], step) for step in range(1, 4)]
    dec_keep, dec_send = dec_total(pieces)
    dec_got = over("latent", 8, dec_send, 1)
    riders = enc_gradient(
        position, backward, slots, own_rows, far_rows, dec_keep, dec_got, enc_scale / tokens_all
    )
    grads = [lax.ppermute(part, PLANE, homeward(step)) for step, part in enumerate(riders)]
    return tuple(
        adam(position, grads, [enc_weight, enc_moment, enc_second], [dec_weight, dec_moment, dec_second])
    )


def solution(mesh):
    arrays = P("layer", "latent", "token")
    in_specs = (P("layer", "token", "latent"), P("token", None)) + (arrays,) * 6
    return jax.shard_map(body, mesh=mesh, in_specs=in_specs, out_specs=(arrays,) * 6, check_vma=False)
```

```python
import math

import jax
import jax.numpy as jnp
from jax import lax
from jax.experimental import pallas as pl
from jax.experimental.pallas import tpu as pltpu
from jax.sharding import PartitionSpec as P

K = 64
ADAM_STEP = 100
LATENTS = 384
OWN = 48
PAIR = 96
LANES = 128
PARTS = LATENTS // LANES
ROWS = 1024
FEATS = 1024
GROUP = ("layer", "latent")
GROUP_SIZE = 64
PLANE = ("latent", "token")
PIECE = 256
CHUNK = 512
CHUNKS = ROWS // CHUNK
HALF = CHUNK // 2
SHARE = ROWS // 4
BLOCK = SHARE // 4
HALF_STEPS = CHUNKS // 2
F32 = jnp.float32
BF16 = jnp.bfloat16
VMEM_BYTES = 20 * 1024 * 1024
SIDE = LATENTS // 2
QUARTER = 256


def place(z, core, y):
    return (z * 2 + core) * 4 + y


def plane_pairs(target):
    return [
        (place(z, core, y), place(*target(z, core, y)))
        for z in range(4)
        for core in range(2)
        for y in range(4)
    ]


TRANSPOSED = plane_pairs(lambda z, core, y: (y, core, z))
ALONG_Y = plane_pairs(lambda z, core, y: (z, core, z ^ y))
ALONG_Z = plane_pairs(lambda z, core, y: (z ^ y, core, y))


def homeward(step):
    return plane_pairs(lambda z, core, y: (y ^ step, core, z))


def swapped(count, step):
    return [(i, i ^ step) for i in range(count)]


def params():
    return pltpu.CompilerParams(vmem_limit_bytes=VMEM_BYTES)


LITTLE = pl.CostEstimate(flops=1024, bytes_accessed=1024, transcendentals=0)


def in_hbm(*arrays):
    return [pltpu.with_memory_space_constraint(array, pltpu.HBM) for array in arrays]


def lane_take(table, column):
    return jnp.take_along_axis(table, column, axis=1, mode="promise_in_bounds")


def compact(dense, index):
    pairs = dense.reshape(dense.shape[0] // 16, 2, 8, LATENTS)
    first = pairs[:, 0].reshape(dense.shape[0] // 2, LATENTS)
    second = pairs[:, 1].reshape(dense.shape[0] // 2, LATENTS)
    column = jnp.bitwise_and(index, LANES - 1)
    part = jnp.right_shift(index, 7)
    low = lax.broadcasted_iota(jnp.int32, index.shape, 1) < K
    out = None
    for q in range(PARTS):
        cut = slice(q * LANES, (q + 1) * LANES)
        found = jnp.where(low, lane_take(first[:, cut], column), lane_take(second[:, cut], column))
        out = found if out is None else jnp.where(part == q, found, out)
    return out


def spread(packed, slot):
    slot = slot.astype(F32).astype(jnp.int32)
    rows = slot.shape[0]
    pairs = slot.reshape(rows // 16, 2, 8, LATENTS)
    sides = []
    for side in range(2):
        at = pairs[:, side].reshape(rows // 2, LATENTS)
        cols = []
        for q in range(PARTS):
            here = at[:, q * LANES : (q + 1) * LANES]
            cols.append(jnp.where(here >= 0, lane_take(packed, jnp.bitwise_and(here, LANES - 1)), 0.0))
        sides.append(jnp.concatenate(cols, axis=1).reshape(rows // 16, 1, 8, LATENTS))
    return jnp.concatenate(sides, axis=1).reshape(rows, LATENTS).astype(BF16)


def index_kernel(place_ref, active_ref, index_ref, local_ref):
    width = active_ref.shape[1]
    active = active_ref[...]
    owner = jnp.right_shift(active * 1366, 16)
    side = jnp.bitwise_xor(jnp.bitwise_and(owner, 1), place_ref[1])
    step = jnp.bitwise_xor(jnp.right_shift(owner, 1), place_ref[0])
    local = side * SIDE + step * OWN + (active - owner * OWN)
    local_ref[...] = local
    turned = local.T.reshape(width // 16, 2, 8, K)
    index_ref[...] = jnp.concatenate(
        [turned[:, 0].reshape(width // 2, K), turned[:, 1].reshape(width // 2, K)], axis=1
    )


def find_index(position, active_t):
    return pl.pallas_call(
        index_kernel,
        grid_spec=pltpu.PrefetchScalarGridSpec(
            num_scalar_prefetch=1,
            grid=(2,),
            in_specs=[pl.BlockSpec((K, ROWS // 2), lambda i, at: (0, i))],
            out_specs=[
                pl.BlockSpec((ROWS // 4, LANES), lambda i, at: (i, 0)),
                pl.BlockSpec((K, ROWS // 2), lambda i, at: (0, i)),
            ],
        ),
        out_shape=[
            jax.ShapeDtypeStruct((ROWS // 2, LANES), jnp.int32),
            jax.ShapeDtypeStruct((K, ROWS), jnp.int32),
        ],
        compiler_params=params(),
        cost_estimate=LITTLE,
        name="find_index",
    )(position, *in_hbm(active_t))


def slot_kernel(local_ref, *refs):
    slot_ref, table = refs[-2:]
    width = local_ref.shape[1]
    token = lax.broadcasted_iota(jnp.int32, (64, width), 1)
    lift = jnp.where(jnp.bitwise_and(token, 8) > 0, K, 0)
    for block in range(LATENTS // 64):
        ids = lax.broadcasted_iota(jnp.int32, (64, width), 0) + block * 64

        def look(k, held):
            return jnp.where(ids == local_ref[pl.ds(k, 1), :], k, held)

        held = lax.fori_loop(0, K, look, jnp.full((64, width), -1, jnp.int32), unroll=16)
        table[block * 64 : (block + 1) * 64, :] = jnp.where(held >= 0, held + lift, -1).astype(F32)
    slot_ref[...] = table[...].T.astype(BF16)


def find_slots(local, piece, before=None):
    steps = PIECE // LANES
    held = [] if before is None else [before]
    return pl.pallas_call(
        slot_kernel,
        grid=(steps,),
        in_specs=[pl.BlockSpec((K, LANES), lambda i: (0, piece * steps + i))]
        + [pl.BlockSpec(memory_space=pl.ANY)] * len(held),
        out_specs=pl.BlockSpec((LANES, LATENTS), lambda i: (piece * steps + i, 0)),
        out_shape=pltpu.HBM((ROWS, LATENTS), BF16),
        input_output_aliases={1: 0} if held else {},
        scratch_shapes=[pltpu.VMEM((LATENTS, LANES), F32)],
        compiler_params=params(),
        cost_estimate=LITTLE,
        name="find_slots",
    )(local, *in_hbm(*held))


def prefetched(grid, in_specs, out_specs, scratch=()):
    return pltpu.PrefetchScalarGridSpec(
        num_scalar_prefetch=1, grid=grid, in_specs=in_specs, out_specs=out_specs, scratch_shapes=scratch
    )


def quarter_lanes(position, step):
    start = jnp.bitwise_xor(position[0], step) * QUARTER
    return pl.ds(pl.multiple_of(start, QUARTER), QUARTER)


def cast_kernel(position, enc_ref, dec_ref, keep_ref, send_ref):
    for array, ref in enumerate((enc_ref, dec_ref)):
        for turned, out_ref in enumerate((keep_ref, send_ref)):
            start = jnp.bitwise_xor(position[1], turned) * FEATS
            half = ref[0, :, pl.ds(pl.multiple_of(start, FEATS), FEATS)]
            out_ref[array] = half.astype(BF16)


def cast_weights(position, enc, dec):
    return pl.pallas_call(
        cast_kernel,
        grid_spec=prefetched((1,), [whole_spec(enc.shape)] * 2, [whole_spec((2, OWN, FEATS))] * 2),
        out_shape=[jax.ShapeDtypeStruct((2, OWN, FEATS), BF16)] * 2,
        compiler_params=params(),
        cost_estimate=LITTLE,
        name="cast_weights",
    )(position, *in_hbm(enc, dec))


def pair_kernel(keep_ref, got_ref, enc_ref, dec_ref):
    for array, out_ref in enumerate((enc_ref, dec_ref)):
        out_ref[:OWN, :] = keep_ref[array]
        out_ref[OWN:, :] = got_ref[array]


def pair(keep, got):
    return pl.pallas_call(
        pair_kernel,
        out_shape=[jax.ShapeDtypeStruct((PAIR, FEATS), BF16)] * 2,
        compiler_params=params(),
        cost_estimate=LITTLE,
        name="pair",
    )(keep, got)


def over(axis, size, array, step):
    return lax.ppermute(array, axis, swapped(size, step))


def token_gather(near):
    one, three = over("token", 4, near, 1), over("token", 4, near, 3)
    return [near, one, three, over("token", 4, three[:OWN], 1), over("token", 4, one[OWN:], 3)]


def assemble(parts, whole, turn=0):
    for step, part in parts:
        for first in range(0, part.shape[0], OWN):
            side = first // OWN if part.shape[0] == PAIR else HALVES[step]
            start = side * SIDE + jnp.bitwise_xor(step & 3, turn) * OWN
            whole[pl.ds(pl.multiple_of(start, 16), OWN), :] = part[first : first + OWN, :]


HALVES = {2: 0, 6: 1}
ENC_SHAPES = ((PAIR, FEATS),) * 3 + ((OWN, FEATS),) * 2
ENC_STEPS = (0, 1, 3, 2, 6)
DEC_SHAPES = ((PAIR, FEATS),) * 4


def put_half(position, value, keep_ref, send_ref):
    step = pl.program_id(0)
    start = (step % HALF_STEPS) * HALF
    rows = pl.ds(pl.multiple_of(start, HALF), HALF)
    mine = step // HALF_STEPS == position[1]

    @pl.when(mine)
    def _():
        keep_ref[rows, :] = value

    @pl.when(jnp.logical_not(mine))
    def _():
        send_ref[rows, :] = value


def unpack(position, parts, packed):
    for step, part in enumerate(parts):
        block = jnp.bitwise_xor(position[2], step) * BLOCK
        for side in range(2):
            start = jnp.bitwise_xor(position[1], side) * SHARE + block
            rows = pl.ds(pl.multiple_of(start, BLOCK), BLOCK)
            packed[rows, :] = part[side * BLOCK : (side + 1) * BLOCK, :]


def packed_rows(packed):
    start = pl.program_id(0) * HALF
    return packed[pl.ds(pl.multiple_of(start, HALF), HALF), :].astype(F32)


def pre_kernel(position, streams_ref, q0, q1, q3, q2a, q2b, index_ref, keep_ref, send_ref, weight):
    @pl.when(pl.program_id(0) == 0)
    def _():
        assemble(list(zip(ENC_STEPS, (q0, q1, q3, q2a, q2b))), weight)

    pre = lax.dot_general(
        streams_ref[...], weight[...], (((1,), (1,)), ((), ())), preferred_element_type=F32
    )
    put_half(position, compact(pre, index_ref[...]), keep_ref, send_ref)


def whole_spec(shape):
    return pl.BlockSpec(shape, lambda i, *at: (0,) * len(shape))


def row_spec(rows, width):
    return pl.BlockSpec((rows, width), lambda i, *at: (i, 0))


def pre_sums(position, streams, enc_parts, index):
    return pl.pallas_call(
        pre_kernel,
        grid_spec=prefetched(
            (CHUNKS,),
            [row_spec(CHUNK, FEATS)] + [whole_spec(shape) for shape in ENC_SHAPES] + [row_spec(HALF, LANES)],
            [whole_spec((SHARE, LANES))] * 2,
            [pltpu.VMEM((LATENTS, FEATS), BF16)],
        ),
        out_shape=[jax.ShapeDtypeStruct((SHARE, LANES), F32)] * 2,
        compiler_params=params(),
        cost_estimate=LITTLE,
        name="pre_sums",
    )(position, streams, *enc_parts, index)


def fold_kernel(position, keep_ref, got_ref, *out_refs):
    for step, out_ref in enumerate(out_refs):
        start = jnp.bitwise_xor(position[2], step) * BLOCK
        rows = pl.ds(pl.multiple_of(start, BLOCK), BLOCK)
        out_ref[...] = keep_ref[rows, :] + got_ref[rows, :]


def fold(position, keep, got):
    return pl.pallas_call(
        fold_kernel,
        grid_spec=prefetched((1,), [whole_spec((SHARE, LANES))] * 2, [whole_spec((BLOCK, LANES))] * 4),
        out_shape=[jax.ShapeDtypeStruct((BLOCK, LANES), F32)] * 4,
        compiler_params=params(),
        cost_estimate=LITTLE,
        name="fold",
    )(position, keep, got)


def couple_kernel(own_ref, other_ref, out_ref):
    out_ref[:BLOCK, :] = own_ref[...]
    out_ref[BLOCK:, :] = other_ref[...]


def couple(own, other):
    return pl.pallas_call(
        couple_kernel,
        out_shape=jax.ShapeDtypeStruct((2 * BLOCK, LANES), BF16),
        compiler_params=params(),
        cost_estimate=LITTLE,
        name="couple",
    )(own, other)


def sum_of_four(parts):
    return (parts[0] + parts[1]) + (parts[2] + parts[3])


def with_partners(axis, parts):
    return [parts[0]] + [over(axis, 8, parts[step], 2 * step) for step in range(1, 4)]


def group_sum(position, keep, send, scale):
    parts = fold(position, keep, over("latent", 8, send, 1))
    block = sum_of_four(with_partners("latent", parts))
    block = sum_of_four(with_partners("layer", [block] * 4))
    total = ((block + over("layer", 8, block, 1)) * scale).astype(BF16)
    return couple(total, over("latent", 8, total, 1))


def accumulate(part, total):
    step = pl.program_id(0)

    @pl.when(step == 0)
    def _():
        total[...] = part

    @pl.when(step > 0)
    def _():
        total[...] += part


def errors_body(
    scale, position, p0, p1, p2, p3, slot_ref, streams_ref, q0, q1, q2, q3, index_ref, keep_ref, send_ref, codes_ref, errors_ref, weight, packed
):
    @pl.when(pl.program_id(0) == 0)
    def _():
        assemble(list(enumerate((q0, q1, q2, q3))), weight, position[2])
        unpack(position, (p0, p1, p2, p3), packed)

    codes = spread(packed_rows(packed), slot_ref[...])
    codes_ref[...] = codes
    rebuilt = jnp.dot(codes, weight[...], preferred_element_type=F32) * scale
    errors = (rebuilt - streams_ref[...].astype(F32)).astype(BF16)
    errors_ref[...] = errors
    back = lax.dot_general(errors, weight[...], (((1,), (1,)), ((), ())), preferred_element_type=F32)
    put_half(position, compact(back, index_ref[...]), keep_ref, send_ref)


def errors_and_back(position, packed, slots, streams, dec_parts, index, scale):
    return pl.pallas_call(
        lambda *refs: errors_body(scale, *refs),
        grid_spec=prefetched(
            (CHUNKS,),
            [whole_spec((2 * BLOCK, LANES))] * 4
            + [row_spec(CHUNK, LATENTS), row_spec(CHUNK, FEATS)]
            + [whole_spec(shape) for shape in DEC_SHAPES]
            + [row_spec(HALF, LANES)],
            [whole_spec((SHARE, LANES))] * 2 + [row_spec(CHUNK, LATENTS), row_spec(CHUNK, FEATS)],
            [pltpu.VMEM((LATENTS, FEATS), BF16), pltpu.VMEM((ROWS // 2, LANES), BF16)],
        ),
        out_shape=[jax.ShapeDtypeStruct((SHARE, LANES), F32)] * 2
        + [jax.ShapeDtypeStruct((ROWS, LATENTS), BF16), jax.ShapeDtypeStruct((ROWS, FEATS), BF16)],
        compiler_params=params(),
        cost_estimate=LITTLE,
        name="errors_and_back",
    )(position, *packed, *in_hbm(slots), streams, *dec_parts, index)


def dec_gradient_body(scale, position, codes_ref, errors_ref, p0, p1, p2, p3, total):
    accumulate(
        lax.dot_general(codes_ref[...], errors_ref[...], (((0,), (0,)), ((), ())), preferred_element_type=F32),
        total,
    )

    @pl.when(pl.program_id(0) == CHUNKS - 1)
    def _():
        for step, out_ref in enumerate((p0, p1, p2, p3)):
            out_ref[...] = (total[:, quarter_lanes(position, step)] * scale).astype(BF16)


def dec_gradient(position, codes, errors, scale):
    return pl.pallas_call(
        lambda *refs: dec_gradient_body(scale, *refs),
        grid_spec=prefetched(
            (CHUNKS,),
            [row_spec(CHUNK, LATENTS), row_spec(CHUNK, FEATS)],
            [whole_spec((LATENTS, QUARTER))] * 4,
            [pltpu.VMEM((LATENTS, FEATS), F32)],
        ),
        out_shape=[jax.ShapeDtypeStruct((LATENTS, QUARTER), BF16)] * 4,
        compiler_params=params(),
        cost_estimate=LITTLE,
        name="dec_gradient",
    )(position, codes, errors)


def dec_total_kernel(p0, p1, p2, p3, keep_ref, send_ref):
    for side, out_ref in enumerate((keep_ref, send_ref)):
        for block in range(4):
            sums = None
            for step, part in enumerate((p0, p1, p2, p3)):
                start = side * SIDE + (block ^ step) * OWN
                term = part[start : start + OWN, :].astype(F32)
                sums = term if sums is None else sums + term
            out_ref[block * OWN : (block + 1) * OWN, :] = sums.astype(BF16)


def dec_total(parts):
    return pl.pallas_call(
        dec_total_kernel,
        out_shape=[jax.ShapeDtypeStruct((SIDE, QUARTER), BF16)] * 2,
        compiler_params=params(),
        cost_estimate=LITTLE,
        name="dec_total",
    )(*parts)


def enc_gradient_body(scale, position, p0, p1, p2, p3, slot_ref, near_ref, far_ref, keep_ref, got_ref, g0, g1, g2, g3, total, packed):
    @pl.when(pl.program_id(0) == 0)
    def _():
        unpack(position, (p0, p1, p2, p3), packed)

    codes = spread(packed_rows(packed), slot_ref[...])[:, :SIDE]
    parts = [
        lax.dot_general(codes, ref[...], (((0,), (0,)), ((), ())), preferred_element_type=F32)
        for ref in (near_ref, far_ref)
    ]
    accumulate(jnp.concatenate(parts, axis=1), total)

    @pl.when(pl.program_id(0) == CHUNKS - 1)
    def _():
        for step, out_ref in enumerate((g0, g1, g2, g3)):
            rows = slice(step * OWN, (step + 1) * OWN)
            out_ref[:, : 2 * FEATS] = (total[rows, :] * scale).astype(BF16)
            out_ref[:, 2 * FEATS : 2 * FEATS + QUARTER] = keep_ref[rows, :]
            out_ref[:, 2 * FEATS + QUARTER :] = got_ref[rows, :]


RIDE = 2 * FEATS + 2 * QUARTER


def enc_gradient(position, packed, slots, near, far, keep, got, scale):
    return pl.pallas_call(
        lambda *refs: enc_gradient_body(scale, *refs),
        grid_spec=prefetched(
            (CHUNKS,),
            [whole_spec((2 * BLOCK, LANES))] * 4
            + [row_spec(CHUNK, LATENTS)]
            + [row_spec(CHUNK, FEATS)] * 2
            + [whole_spec((SIDE, QUARTER))] * 2,
            [whole_spec((OWN, RIDE))] * 4,
            [pltpu.VMEM((SIDE, 2 * FEATS), F32), pltpu.VMEM((ROWS // 2, LANES), BF16)],
        ),
        out_shape=[jax.ShapeDtypeStruct((OWN, RIDE), BF16)] * 4,
        compiler_params=params(),
        cost_estimate=LITTLE,
        name="enc_gradient",
    )(position, *packed, *in_hbm(slots), near, far, keep, got)


def adam_update(gradient, weight, moment, second):
    moment_new = 0.9 * moment + 0.1 * gradient
    second_new = 0.999 * second + 0.001 * gradient * gradient
    first_fix = 1.0 - 0.9**ADAM_STEP
    second_fix = 1.0 - 0.999**ADAM_STEP
    weight_new = weight - 0.2 * (moment_new / first_fix) / (jnp.sqrt(second_new / second_fix) + 1e-08)
    return weight_new, moment_new, second_new


def adam_kernel(position, *refs):
    enc_grads, dec_grads, enc_in, dec_in, enc_out, dec_out = (
        refs[:4], refs[4:8], refs[8:11], refs[11:14], refs[14:17], refs[17:20]
    )
    gradient = sum(ref[...].astype(F32) for ref in enc_grads)
    for out_ref, value in zip(enc_out, adam_update(gradient, *[ref[0] for ref in enc_in])):
        out_ref[0] = value
    for step, ref in enumerate(dec_grads):
        start = jnp.bitwise_xor(position[2], step) * QUARTER
        lanes = pl.ds(pl.multiple_of(start, QUARTER), QUARTER)
        held = [source[0, :, lanes] for source in dec_in]
        for out_ref, value in zip(dec_out, adam_update(ref[...].astype(F32), *held)):
            out_ref[0, :, lanes] = value


def adam(position, grads, enc, dec):
    enc_part = pl.BlockSpec((OWN, FEATS), lambda i, at: (0, i))
    dec_part = pl.BlockSpec((OWN, QUARTER), lambda i, at: (0, 2 * FEATS // QUARTER + i))
    state = pl.BlockSpec((1, OWN, FEATS), lambda i, at: (0, 0, jnp.bitwise_xor(i, at[1])))
    return pl.pallas_call(
        adam_kernel,
        grid_spec=prefetched((2,), [enc_part] * 4 + [dec_part] * 4 + [state] * 6, [state] * 6),
        out_shape=[jax.ShapeDtypeStruct(array.shape, F32) for array in enc + dec],
        compiler_params=params(),
        cost_estimate=LITTLE,
        name="adam",
    )(position, *grads, *grads, *enc, *dec)


def body(
    streams, active_latents, enc_weight, enc_moment, enc_second, dec_weight, dec_moment, dec_second
):
    tokens_all = ROWS * 4
    enc_scale = 1.0 / math.sqrt(8 * 8192)
    dec_scale = 1.0 / math.sqrt(K)
    latent = lax.axis_index("latent")
    row = lax.axis_index("token")
    core = jnp.bitwise_and(latent, 1)
    column = jnp.right_shift(latent, 1)
    position = jnp.stack([row, core, column]).astype(jnp.int32)
    own_rows = streams[0]

    keep, send = cast_weights(position, enc_weight, dec_weight)
    got = over("latent", 8, send, 1)
    index, local = find_index(position, active_latents.T)
    got, local = lax.optimization_barrier((got, local))
    enc_pair, dec_pair = pair(keep, got)
    enc_pair, dec_pair, other_rows = lax.optimization_barrier((enc_pair, dec_pair, own_rows))
    turned = lax.ppermute(enc_pair, PLANE, TRANSPOSED)
    dec_moved = lax.ppermute(dec_pair, PLANE, ALONG_Y)
    far_rows = over("latent", 8, other_rows, 1)
    slots = None
    for piece in range(ROWS // PIECE):
        slots = find_slots(local, piece, slots)
    turned, dec_moved, slots, far_rows = lax.optimization_barrier((turned, dec_moved, slots, far_rows))
    enc_parts = token_gather(turned)
    dec_near = lax.ppermute(dec_moved, PLANE, ALONG_Z)
    enc_parts, dec_near = lax.optimization_barrier((enc_parts, dec_near))
    keep, send = pre_sums(position, own_rows, enc_parts, index)
    codes = with_partners("latent", [group_sum(position, keep, send, enc_scale)] * 4)
    keep, send, dec_near = lax.optimization_barrier((keep, send, dec_near))
    dec_parts = [dec_near] + [over("token", 4, dec_near, step) for step in range(1, 4)]
    keep, send, codes_wide, errors = errors_and_back(position, codes, slots, own_rows, dec_parts, index, dec_scale)
    coupled = group_sum(position, keep, send, dec_scale)
    keep, send, codes_wide, errors = lax.optimization_barrier((keep, send, codes_wide, errors))
    pieces = dec_gradient(position, codes_wide, errors, dec_scale / tokens_all)
    pieces = [pieces[0]] + [over("token", 4, pieces[step], step) for step in range(1, 4)]
    coupled, pieces = lax.optimization_barrier((coupled, pieces))
    backward = with_partners("latent", [coupled] * 4)
    dec_keep, dec_send = dec_total(pieces)
    dec_got = over("latent", 8, dec_send, 1)
    riders = enc_gradient(
        position, backward, slots, own_rows, far_rows, dec_keep, dec_got, enc_scale / tokens_all
    )
    grads = [lax.ppermute(part, PLANE, homeward(step)) for step, part in enumerate(riders)]
    return tuple(
        adam(position, grads, [enc_weight, enc_moment, enc_second], [dec_weight, dec_moment, dec_second])
    )


def solution(mesh):
    arrays = P("layer", "latent", "token")
    in_specs = (P("layer", "token", "latent"), P("token", None)) + (arrays,) * 6
    return jax.shard_map(body, mesh=mesh, in_specs=in_specs, out_specs=(arrays,) * 6, check_vma=False)
```

```python
import math

import jax
import jax.numpy as jnp
from jax import lax
from jax.experimental import pallas as pl
from jax.experimental.pallas import tpu as pltpu
from jax.sharding import PartitionSpec as P

K = 64
ADAM_STEP = 100
LATENTS = 384
OWN = 48
PAIR = 96
LANES = 128
PARTS = LATENTS // LANES
ROWS = 1024
FEATS = 1024
GROUP = ("layer", "latent")
GROUP_SIZE = 64
PLANE = ("latent", "token")
PIECE = 256
CHUNK = 512
CHUNKS = ROWS // CHUNK
HALF = CHUNK // 2
SHARE = ROWS // 4
BLOCK = SHARE // 4
HALF_STEPS = CHUNKS // 2
F32 = jnp.float32
BF16 = jnp.bfloat16
VMEM_BYTES = 20 * 1024 * 1024
SIDE = LATENTS // 2
QUARTER = 256


def place(z, core, y):
    return (z * 2 + core) * 4 + y


def plane_pairs(target):
    return [
        (place(z, core, y), place(*target(z, core, y)))
        for z in range(4)
        for core in range(2)
        for y in range(4)
    ]


TRANSPOSED = plane_pairs(lambda z, core, y: (y, core, z))
ALONG_Y = plane_pairs(lambda z, core, y: (z, core, z ^ y))
ALONG_Z = plane_pairs(lambda z, core, y: (z ^ y, core, y))


def homeward(step):
    return plane_pairs(lambda z, core, y: (y ^ step, core, z))


def swapped(count, step):
    return [(i, i ^ step) for i in range(count)]


def params():
    return pltpu.CompilerParams(vmem_limit_bytes=VMEM_BYTES)


LITTLE = pl.CostEstimate(flops=1024, bytes_accessed=1024, transcendentals=0)


def in_hbm(*arrays):
    return [pltpu.with_memory_space_constraint(array, pltpu.HBM) for array in arrays]


def lane_take(table, column):
    return jnp.take_along_axis(table, column, axis=1, mode="promise_in_bounds")


def compact(dense, index):
    pairs = dense.reshape(dense.shape[0] // 16, 2, 8, LATENTS)
    first = pairs[:, 0].reshape(dense.shape[0] // 2, LATENTS)
    second = pairs[:, 1].reshape(dense.shape[0] // 2, LATENTS)
    column = jnp.bitwise_and(index, LANES - 1)
    part = jnp.right_shift(index, 7)
    low = lax.broadcasted_iota(jnp.int32, index.shape, 1) < K
    out = None
    for q in range(PARTS):
        cut = slice(q * LANES, (q + 1) * LANES)
        found = jnp.where(low, lane_take(first[:, cut], column), lane_take(second[:, cut], column))
        out = found if out is None else jnp.where(part == q, found, out)
    return out


def spread(packed, slot):
    slot = slot.astype(F32).astype(jnp.int32)
    rows = slot.shape[0]
    pairs = slot.reshape(rows // 16, 2, 8, LATENTS)
    sides = []
    for side in range(2):
        at = pairs[:, side].reshape(rows // 2, LATENTS)
        cols = []
        for q in range(PARTS):
            here = at[:, q * LANES : (q + 1) * LANES]
            cols.append(jnp.where(here >= 0, lane_take(packed, jnp.bitwise_and(here, LANES - 1)), 0.0))
        sides.append(jnp.concatenate(cols, axis=1).reshape(rows // 16, 1, 8, LATENTS))
    return jnp.concatenate(sides, axis=1).reshape(rows, LATENTS).astype(BF16)


def index_kernel(place_ref, active_ref, index_ref, local_ref):
    width = active_ref.shape[1]
    active = active_ref[...]
    owner = jnp.right_shift(active * 1366, 16)
    side = jnp.bitwise_xor(jnp.bitwise_and(owner, 1), place_ref[1])
    step = jnp.bitwise_xor(jnp.right_shift(owner, 1), place_ref[0])
    local = side * SIDE + step * OWN + (active - owner * OWN)
    local_ref[...] = local
    turned = local.T.reshape(width // 16, 2, 8, K)
    index_ref[...] = jnp.concatenate(
        [turned[:, 0].reshape(width // 2, K), turned[:, 1].reshape(width // 2, K)], axis=1
    )


def find_index(position, active_t):
    return pl.pallas_call(
        index_kernel,
        grid_spec=pltpu.PrefetchScalarGridSpec(
            num_scalar_prefetch=1,
            grid=(2,),
            in_specs=[pl.BlockSpec((K, ROWS // 2), lambda i, at: (0, i))],
            out_specs=[
                pl.BlockSpec((ROWS // 4, LANES), lambda i, at: (i, 0)),
                pl.BlockSpec((K, ROWS // 2), lambda i, at: (0, i)),
            ],
        ),
        out_shape=[
            jax.ShapeDtypeStruct((ROWS // 2, LANES), jnp.int32),
            jax.ShapeDtypeStruct((K, ROWS), jnp.int32),
        ],
        compiler_params=params(),
        cost_estimate=LITTLE,
        name="find_index",
    )(position, active_t)


def slot_kernel(local_ref, *refs):
    slot_ref, table = refs[-2:]
    width = local_ref.shape[1]
    token = lax.broadcasted_iota(jnp.int32, (128, width), 1)
    lift = jnp.where(jnp.bitwise_and(token, 8) > 0, K, 0)
    for block in range(LATENTS // 128):
        ids = (lax.broadcasted_iota(jnp.int32, (128, width), 0) + block * 128).astype(jnp.int16)

        def look(k, held):
            row = jnp.broadcast_to(local_ref[pl.ds(k, 1), :], (16, width)).astype(jnp.int16)
            rows = jnp.concatenate([row] * 8, axis=0)
            return jnp.where(ids == rows, jnp.full((128, width), k, jnp.int32).astype(jnp.int16), held)

        held = lax.fori_loop(0, K, look, jnp.full((128, width), -1, jnp.int16), unroll=16).astype(jnp.int32)
        table[block * 128 : (block + 1) * 128, :] = jnp.where(held >= 0, held + lift, -1).astype(F32)
    slot_ref[...] = table[...].T.astype(BF16)


def find_slots(local, piece, before=None):
    steps = PIECE // LANES
    held = [] if before is None else [before]
    return pl.pallas_call(
        slot_kernel,
        grid=(steps,),
        in_specs=[pl.BlockSpec((K, LANES), lambda i: (0, piece * steps + i))]
        + [pl.BlockSpec(memory_space=pl.ANY)] * len(held),
        out_specs=pl.BlockSpec((LANES, LATENTS), lambda i: (piece * steps + i, 0)),
        out_shape=pltpu.HBM((ROWS, LATENTS), BF16),
        input_output_aliases={1: 0} if held else {},
        scratch_shapes=[pltpu.VMEM((LATENTS, LANES), F32)],
        compiler_params=params(),
        cost_estimate=LITTLE,
        name="find_slots",
    )(local, *in_hbm(*held))


def prefetched(grid, in_specs, out_specs, scratch=()):
    return pltpu.PrefetchScalarGridSpec(
        num_scalar_prefetch=1, grid=grid, in_specs=in_specs, out_specs=out_specs, scratch_shapes=scratch
    )


def quarter_lanes(position, step):
    start = jnp.bitwise_xor(position[0], step) * QUARTER
    return pl.ds(pl.multiple_of(start, QUARTER), QUARTER)


def cast_kernel(position, enc_ref, dec_ref, keep_ref, send_ref):
    for array, ref in enumerate((enc_ref, dec_ref)):
        for turned, out_ref in enumerate((keep_ref, send_ref)):
            start = jnp.bitwise_xor(position[1], turned) * FEATS
            half = ref[0, :, pl.ds(pl.multiple_of(start, FEATS), FEATS)]
            out_ref[array] = half.astype(BF16)


def cast_weights(position, enc, dec):
    return pl.pallas_call(
        cast_kernel,
        grid_spec=prefetched((1,), [whole_spec(enc.shape)] * 2, [whole_spec((2, OWN, FEATS))] * 2),
        out_shape=[jax.ShapeDtypeStruct((2, OWN, FEATS), BF16)] * 2,
        compiler_params=params(),
        cost_estimate=LITTLE,
        name="cast_weights",
    )(position, *in_hbm(enc, dec))


def pair_kernel(keep_ref, got_ref, enc_ref, dec_ref):
    for array, out_ref in enumerate((enc_ref, dec_ref)):
        out_ref[:OWN, :] = keep_ref[array]
        out_ref[OWN:, :] = got_ref[array]


def pair(keep, got):
    return pl.pallas_call(
        pair_kernel,
        out_shape=[jax.ShapeDtypeStruct((PAIR, FEATS), BF16)] * 2,
        compiler_params=params(),
        cost_estimate=LITTLE,
        name="pair",
    )(keep, got)


def over(axis, size, array, step):
    return lax.ppermute(array, axis, swapped(size, step))


def token_gather(near):
    one, three = over("token", 4, near, 1), over("token", 4, near, 3)
    return [near, one, three, over("token", 4, three[:OWN], 1), over("token", 4, one[OWN:], 3)]


def assemble(parts, whole, turn=0):
    for step, part in parts:
        for first in range(0, part.shape[0], OWN):
            side = first // OWN if part.shape[0] == PAIR else HALVES[step]
            start = side * SIDE + jnp.bitwise_xor(step & 3, turn) * OWN
            whole[pl.ds(pl.multiple_of(start, 16), OWN), :] = part[first : first + OWN, :]


HALVES = {2: 0, 6: 1}
ENC_SHAPES = ((PAIR, FEATS),) * 3 + ((OWN, FEATS),) * 2
ENC_STEPS = (0, 1, 3, 2, 6)
DEC_SHAPES = ((PAIR, FEATS),) * 4


def put_half(position, value, keep_ref, send_ref):
    step = pl.program_id(0)
    start = (step % HALF_STEPS) * HALF
    rows = pl.ds(pl.multiple_of(start, HALF), HALF)
    mine = step // HALF_STEPS == position[1]

    @pl.when(mine)
    def _():
        keep_ref[rows, :] = value

    @pl.when(jnp.logical_not(mine))
    def _():
        send_ref[rows, :] = value


def unpack(position, parts, packed):
    for step, part in enumerate(parts):
        block = jnp.bitwise_xor(position[2], step) * BLOCK
        for side in range(2):
            start = jnp.bitwise_xor(position[1], side) * SHARE + block
            rows = pl.ds(pl.multiple_of(start, BLOCK), BLOCK)
            packed[rows, :] = part[side * BLOCK : (side + 1) * BLOCK, :]


def packed_rows(packed):
    start = pl.program_id(0) * HALF
    return packed[pl.ds(pl.multiple_of(start, HALF), HALF), :].astype(F32)


def pre_kernel(position, streams_ref, q0, q1, q3, q2a, q2b, index_ref, keep_ref, send_ref, weight):
    @pl.when(pl.program_id(0) == 0)
    def _():
        assemble(list(zip(ENC_STEPS, (q0, q1, q3, q2a, q2b))), weight)

    pre = lax.dot_general(
        streams_ref[...], weight[...], (((1,), (1,)), ((), ())), preferred_element_type=F32
    )
    put_half(position, compact(pre, index_ref[...]), keep_ref, send_ref)


def whole_spec(shape):
    return pl.BlockSpec(shape, lambda i, *at: (0,) * len(shape))


def row_spec(rows, width):
    return pl.BlockSpec((rows, width), lambda i, *at: (i, 0))


def pre_sums(position, streams, enc_parts, index):
    return pl.pallas_call(
        pre_kernel,
        grid_spec=prefetched(
            (CHUNKS,),
            [row_spec(CHUNK, FEATS)] + [whole_spec(shape) for shape in ENC_SHAPES] + [row_spec(HALF, LANES)],
            [whole_spec((SHARE, LANES))] * 2,
            [pltpu.VMEM((LATENTS, FEATS), BF16)],
        ),
        out_shape=[jax.ShapeDtypeStruct((SHARE, LANES), F32)] * 2,
        compiler_params=params(),
        cost_estimate=LITTLE,
        name="pre_sums",
    )(position, streams, *enc_parts, index)


def fold_kernel(position, keep_ref, got_ref, *out_refs):
    for step, out_ref in enumerate(out_refs):
        start = jnp.bitwise_xor(position[2], step) * BLOCK
        rows = pl.ds(pl.multiple_of(start, BLOCK), BLOCK)
        out_ref[...] = keep_ref[rows, :] + got_ref[rows, :]


def fold(position, keep, got):
    return pl.pallas_call(
        fold_kernel,
        grid_spec=prefetched((1,), [whole_spec((SHARE, LANES))] * 2, [whole_spec((BLOCK, LANES))] * 4),
        out_shape=[jax.ShapeDtypeStruct((BLOCK, LANES), F32)] * 4,
        compiler_params=params(),
        cost_estimate=LITTLE,
        name="fold",
    )(position, keep, got)


def couple_kernel(own_ref, other_ref, out_ref):
    out_ref[:BLOCK, :] = own_ref[...]
    out_ref[BLOCK:, :] = other_ref[...]


def couple(own, other):
    return pl.pallas_call(
        couple_kernel,
        out_shape=jax.ShapeDtypeStruct((2 * BLOCK, LANES), BF16),
        compiler_params=params(),
        cost_estimate=LITTLE,
        name="couple",
    )(own, other)


def sum_of_four(parts):
    return (parts[0] + parts[1]) + (parts[2] + parts[3])


def with_partners(axis, parts):
    return [parts[0]] + [over(axis, 8, parts[step], 2 * step) for step in range(1, 4)]


def group_sum(position, keep, send, scale):
    parts = fold(position, keep, over("latent", 8, send, 1))
    block = sum_of_four(with_partners("latent", parts))
    block = sum_of_four(with_partners("layer", [block] * 4))
    total = ((block + over("layer", 8, block, 1)) * scale).astype(BF16)
    total = couple(total, over("latent", 8, total, 1))
    return with_partners("latent", [total] * 4)


def accumulate(part, total):
    step = pl.program_id(0)

    @pl.when(step == 0)
    def _():
        total[...] = part

    @pl.when(step > 0)
    def _():
        total[...] += part


def errors_body(
    scale, position, p0, p1, p2, p3, slot_ref, streams_ref, q0, q1, q2, q3, index_ref, keep_ref, send_ref, codes_ref, errors_ref, weight, packed
):
    @pl.when(pl.program_id(0) == 0)
    def _():
        assemble(list(enumerate((q0, q1, q2, q3))), weight, position[2])
        unpack(position, (p0, p1, p2, p3), packed)

    codes = spread(packed_rows(packed), slot_ref[...])
    codes_ref[...] = codes
    rebuilt = jnp.dot(codes, weight[...], preferred_element_type=F32) * scale
    errors = (rebuilt - streams_ref[...].astype(F32)).astype(BF16)
    errors_ref[...] = errors
    back = lax.dot_general(errors, weight[...], (((1,), (1,)), ((), ())), preferred_element_type=F32)
    put_half(position, compact(back, index_ref[...]), keep_ref, send_ref)


def errors_and_back(position, packed, slots, streams, dec_parts, index, scale):
    return pl.pallas_call(
        lambda *refs: errors_body(scale, *refs),
        grid_spec=prefetched(
            (CHUNKS,),
            [whole_spec((2 * BLOCK, LANES))] * 4
            + [row_spec(CHUNK, LATENTS), row_spec(CHUNK, FEATS)]
            + [whole_spec(shape) for shape in DEC_SHAPES]
            + [row_spec(HALF, LANES)],
            [whole_spec((SHARE, LANES))] * 2 + [row_spec(CHUNK, LATENTS), row_spec(CHUNK, FEATS)],
            [pltpu.VMEM((LATENTS, FEATS), BF16), pltpu.VMEM((ROWS // 2, LANES), BF16)],
        ),
        out_shape=[jax.ShapeDtypeStruct((SHARE, LANES), F32)] * 2
        + [jax.ShapeDtypeStruct((ROWS, LATENTS), BF16), jax.ShapeDtypeStruct((ROWS, FEATS), BF16)],
        compiler_params=params(),
        cost_estimate=LITTLE,
        name="errors_and_back",
    )(position, *packed, *in_hbm(slots), streams, *dec_parts, index)


def dec_gradient_body(scale, position, codes_ref, errors_ref, p0, p1, p2, p3, total):
    accumulate(
        lax.dot_general(codes_ref[...], errors_ref[...], (((0,), (0,)), ((), ())), preferred_element_type=F32),
        total,
    )

    @pl.when(pl.program_id(0) == CHUNKS - 1)
    def _():
        for step, out_ref in enumerate((p0, p1, p2, p3)):
            out_ref[...] = (total[:, quarter_lanes(position, step)] * scale).astype(BF16)


def dec_gradient(position, codes, errors, scale):
    return pl.pallas_call(
        lambda *refs: dec_gradient_body(scale, *refs),
        grid_spec=prefetched(
            (CHUNKS,),
            [row_spec(CHUNK, LATENTS), row_spec(CHUNK, FEATS)],
            [whole_spec((LATENTS, QUARTER))] * 4,
            [pltpu.VMEM((LATENTS, FEATS), F32)],
        ),
        out_shape=[jax.ShapeDtypeStruct((LATENTS, QUARTER), BF16)] * 4,
        compiler_params=params(),
        cost_estimate=LITTLE,
        name="dec_gradient",
    )(position, codes, errors)


def dec_total_kernel(p0, p1, p2, p3, keep_ref, send_ref):
    for side, out_ref in enumerate((keep_ref, send_ref)):
        for block in range(4):
            sums = None
            for step, part in enumerate((p0, p1, p2, p3)):
                start = side * SIDE + (block ^ step) * OWN
                term = part[start : start + OWN, :].astype(F32)
                sums = term if sums is None else sums + term
            out_ref[block * OWN : (block + 1) * OWN, :] = sums.astype(BF16)


def dec_total(parts):
    return pl.pallas_call(
        dec_total_kernel,
        out_shape=[jax.ShapeDtypeStruct((SIDE, QUARTER), BF16)] * 2,
        compiler_params=params(),
        cost_estimate=LITTLE,
        name="dec_total",
    )(*parts)


def enc_gradient_body(scale, position, p0, p1, p2, p3, slot_ref, near_ref, far_ref, keep_ref, got_ref, g0, g1, g2, g3, total, packed):
    @pl.when(pl.program_id(0) == 0)
    def _():
        unpack(position, (p0, p1, p2, p3), packed)

    codes = spread(packed_rows(packed), slot_ref[...])[:, :SIDE]
    parts = [
        lax.dot_general(codes, ref[...], (((0,), (0,)), ((), ())), preferred_element_type=F32)
        for ref in (near_ref, far_ref)
    ]
    accumulate(jnp.concatenate(parts, axis=1), total)

    @pl.when(pl.program_id(0) == CHUNKS - 1)
    def _():
        for step, out_ref in enumerate((g0, g1, g2, g3)):
            rows = slice(step * OWN, (step + 1) * OWN)
            out_ref[:, : 2 * FEATS] = (total[rows, :] * scale).astype(BF16)
            out_ref[:, 2 * FEATS : 2 * FEATS + QUARTER] = keep_ref[rows, :]
            out_ref[:, 2 * FEATS + QUARTER :] = got_ref[rows, :]


RIDE = 2 * FEATS + 2 * QUARTER


def enc_gradient(position, packed, slots, near, far, keep, got, scale):
    return pl.pallas_call(
        lambda *refs: enc_gradient_body(scale, *refs),
        grid_spec=prefetched(
            (CHUNKS,),
            [whole_spec((2 * BLOCK, LANES))] * 4
            + [row_spec(CHUNK, LATENTS)]
            + [row_spec(CHUNK, FEATS)] * 2
            + [whole_spec((SIDE, QUARTER))] * 2,
            [whole_spec((OWN, RIDE))] * 4,
            [pltpu.VMEM((SIDE, 2 * FEATS), F32), pltpu.VMEM((ROWS // 2, LANES), BF16)],
        ),
        out_shape=[jax.ShapeDtypeStruct((OWN, RIDE), BF16)] * 4,
        compiler_params=params(),
        cost_estimate=LITTLE,
        name="enc_gradient",
    )(position, *packed, *in_hbm(slots), near, far, keep, got)


def adam_update(gradient, weight, moment, second):
    moment_new = 0.9 * moment + 0.1 * gradient
    second_new = 0.999 * second + 0.001 * gradient * gradient
    first_fix = 1.0 - 0.9**ADAM_STEP
    second_fix = 1.0 - 0.999**ADAM_STEP
    weight_new = weight - 0.2 * (moment_new / first_fix) / (jnp.sqrt(second_new / second_fix) + 1e-08)
    return weight_new, moment_new, second_new


def adam_kernel(position, *refs):
    enc_grads, dec_grads, enc_in, dec_in, enc_out, dec_out = (
        refs[:4], refs[4:8], refs[8:11], refs[11:14], refs[14:17], refs[17:20]
    )
    gradient = sum(ref[...].astype(F32) for ref in enc_grads)
    for out_ref, value in zip(enc_out, adam_update(gradient, *[ref[0] for ref in enc_in])):
        out_ref[0] = value
    for step, ref in enumerate(dec_grads):
        start = jnp.bitwise_xor(position[2], step) * QUARTER
        lanes = pl.ds(pl.multiple_of(start, QUARTER), QUARTER)
        held = [source[0, :, lanes] for source in dec_in]
        for out_ref, value in zip(dec_out, adam_update(ref[...].astype(F32), *held)):
            out_ref[0, :, lanes] = value


def adam(position, grads, enc, dec):
    enc_part = pl.BlockSpec((OWN, FEATS), lambda i, at: (0, i))
    dec_part = pl.BlockSpec((OWN, QUARTER), lambda i, at: (0, 2 * FEATS // QUARTER + i))
    state = pl.BlockSpec((1, OWN, FEATS), lambda i, at: (0, 0, jnp.bitwise_xor(i, at[1])))
    return pl.pallas_call(
        adam_kernel,
        grid_spec=prefetched((2,), [enc_part] * 4 + [dec_part] * 4 + [state] * 6, [state] * 6),
        out_shape=[jax.ShapeDtypeStruct(array.shape, F32) for array in enc + dec],
        compiler_params=params(),
        cost_estimate=LITTLE,
        name="adam",
    )(position, *grads, *grads, *enc, *dec)


def body(
    streams, active_latents, enc_weight, enc_moment, enc_second, dec_weight, dec_moment, dec_second
):
    tokens_all = ROWS * 4
    enc_scale = 1.0 / math.sqrt(8 * 8192)
    dec_scale = 1.0 / math.sqrt(K)
    latent = lax.axis_index("latent")
    row = lax.axis_index("token")
    core = jnp.bitwise_and(latent, 1)
    column = jnp.right_shift(latent, 1)
    position = jnp.stack([row, core, column]).astype(jnp.int32)
    own_rows = streams[0]

    keep, send = cast_weights(position, enc_weight, dec_weight)
    got = over("latent", 8, send, 1)
    enc_pair, dec_pair = pair(keep, got)
    enc_pair, dec_pair, other_rows, active_t = lax.optimization_barrier(
        (enc_pair, dec_pair, own_rows, active_latents.T)
    )
    turned = lax.ppermute(enc_pair, PLANE, TRANSPOSED)
    dec_moved = lax.ppermute(dec_pair, PLANE, ALONG_Y)
    index, local = find_index(position, active_t)
    far_rows = over("latent", 8, other_rows, 1)
    slots = None
    for piece in range(ROWS // PIECE):
        slots = find_slots(local, piece, slots)
    turned, dec_moved, slots, far_rows = lax.optimization_barrier((turned, dec_moved, slots, far_rows))
    enc_parts = token_gather(turned)
    dec_near = lax.ppermute(dec_moved, PLANE, ALONG_Z)
    enc_parts, dec_near = lax.optimization_barrier((enc_parts, dec_near))
    keep, send = pre_sums(position, own_rows, enc_parts, index)
    codes = group_sum(position, keep, send, enc_scale)
    keep, send, dec_near = lax.optimization_barrier((keep, send, dec_near))
    dec_parts = [dec_near] + [over("token", 4, dec_near, step) for step in range(1, 4)]
    keep, send, codes_wide, errors = errors_and_back(position, codes, slots, own_rows, dec_parts, index, dec_scale)
    backward = group_sum(position, keep, send, dec_scale)
    keep, send, codes_wide, errors = lax.optimization_barrier((keep, send, codes_wide, errors))
    pieces = dec_gradient(position, codes_wide, errors, dec_scale / tokens_all)
    pieces = [pieces[0]] + [over("token", 4, pieces[step], step) for step in range(1, 4)]
    dec_keep, dec_send = dec_total(pieces)
    dec_got = over("latent", 8, dec_send, 1)
    riders = enc_gradient(
        position, backward, slots, own_rows, far_rows, dec_keep, dec_got, enc_scale / tokens_all
    )
    grads = [lax.ppermute(part, PLANE, homeward(step)) for step, part in enumerate(riders)]
    return tuple(
        adam(position, grads, [enc_weight, enc_moment, enc_second], [dec_weight, dec_moment, dec_second])
    )


def solution(mesh):
    arrays = P("layer", "latent", "token")
    in_specs = (P("layer", "token", "latent"), P("token", None)) + (arrays,) * 6
    return jax.shard_map(body, mesh=mesh, in_specs=in_specs, out_specs=(arrays,) * 6, check_vma=False)
```

```python
import math

import jax
import jax.numpy as jnp
from jax import lax
from jax.experimental import pallas as pl
from jax.experimental.pallas import tpu as pltpu
from jax.sharding import PartitionSpec as P

K = 64
ADAM_STEP = 100
LATENTS = 384
OWN = 48
PAIR = 96
LANES = 128
PARTS = LATENTS // LANES
ROWS = 1024
FEATS = 1024
GROUP = ("layer", "latent")
GROUP_SIZE = 64
PLANE = ("latent", "token")
PIECE = 256
CHUNK = 512
CHUNKS = ROWS // CHUNK
HALF = CHUNK // 2
SHARE = ROWS // 4
BLOCK = SHARE // 4
HALF_STEPS = CHUNKS // 2
F32 = jnp.float32
BF16 = jnp.bfloat16
VMEM_BYTES = 20 * 1024 * 1024
SIDE = LATENTS // 2
QUARTER = 256


def place(z, core, y):
    return (z * 2 + core) * 4 + y


def plane_pairs(target):
    return [
        (place(z, core, y), place(*target(z, core, y)))
        for z in range(4)
        for core in range(2)
        for y in range(4)
    ]


TRANSPOSED = plane_pairs(lambda z, core, y: (y, core, z))
ALONG_Y = plane_pairs(lambda z, core, y: (z, core, z ^ y))
ALONG_Z = plane_pairs(lambda z, core, y: (z ^ y, core, y))


def homeward(step):
    return plane_pairs(lambda z, core, y: (y ^ step, core, z))


def swapped(count, step):
    return [(i, i ^ step) for i in range(count)]


def params():
    return pltpu.CompilerParams(vmem_limit_bytes=VMEM_BYTES)


LITTLE = pl.CostEstimate(flops=1024, bytes_accessed=1024, transcendentals=0)


def in_hbm(*arrays):
    return [pltpu.with_memory_space_constraint(array, pltpu.HBM) for array in arrays]


def lane_take(table, column):
    return jnp.take_along_axis(table, column, axis=1, mode="promise_in_bounds")


def compact(dense, index):
    pairs = dense.reshape(dense.shape[0] // 16, 2, 8, LATENTS)
    first = pairs[:, 0].reshape(dense.shape[0] // 2, LATENTS)
    second = pairs[:, 1].reshape(dense.shape[0] // 2, LATENTS)
    column = jnp.bitwise_and(index, LANES - 1)
    part = jnp.right_shift(index, 7)
    low = lax.broadcasted_iota(jnp.int32, index.shape, 1) < K
    out = None
    for q in range(PARTS):
        cut = slice(q * LANES, (q + 1) * LANES)
        found = jnp.where(low, lane_take(first[:, cut], column), lane_take(second[:, cut], column))
        out = found if out is None else jnp.where(part == q, found, out)
    return out


def spread(packed, slot):
    slot = slot.astype(F32).astype(jnp.int32)
    rows = slot.shape[0]
    pairs = slot.reshape(rows // 16, 2, 8, LATENTS)
    sides = []
    for side in range(2):
        at = pairs[:, side].reshape(rows // 2, LATENTS)
        cols = []
        for q in range(PARTS):
            here = at[:, q * LANES : (q + 1) * LANES]
            cols.append(jnp.where(here >= 0, lane_take(packed, jnp.bitwise_and(here, LANES - 1)), 0.0))
        sides.append(jnp.concatenate(cols, axis=1).reshape(rows // 16, 1, 8, LATENTS))
    return jnp.concatenate(sides, axis=1).reshape(rows, LATENTS).astype(BF16)


def index_kernel(place_ref, active_ref, index_ref, local_ref):
    width = active_ref.shape[1]
    active = active_ref[...]
    owner = jnp.right_shift(active * 1366, 16)
    side = jnp.bitwise_xor(jnp.bitwise_and(owner, 1), place_ref[1])
    step = jnp.bitwise_xor(jnp.right_shift(owner, 1), place_ref[0])
    local = side * SIDE + step * OWN + (active - owner * OWN)
    local_ref[...] = local
    turned = local.T.reshape(width // 16, 2, 8, K)
    index_ref[...] = jnp.concatenate(
        [turned[:, 0].reshape(width // 2, K), turned[:, 1].reshape(width // 2, K)], axis=1
    )


def find_index(position, active_t):
    return pl.pallas_call(
        index_kernel,
        grid_spec=pltpu.PrefetchScalarGridSpec(
            num_scalar_prefetch=1,
            grid=(2,),
            in_specs=[pl.BlockSpec((K, ROWS // 2), lambda i, at: (0, i))],
            out_specs=[
                pl.BlockSpec((ROWS // 4, LANES), lambda i, at: (i, 0)),
                pl.BlockSpec((K, ROWS // 2), lambda i, at: (0, i)),
            ],
        ),
        out_shape=[
            jax.ShapeDtypeStruct((ROWS // 2, LANES), jnp.int32),
            jax.ShapeDtypeStruct((K, ROWS), jnp.int32),
        ],
        compiler_params=params(),
        cost_estimate=LITTLE,
        name="find_index",
    )(position, active_t)


def slot_kernel(local_ref, *refs):
    slot_ref, table = refs[-2:]
    width = local_ref.shape[1]
    token = lax.broadcasted_iota(jnp.int32, (128, width), 1)
    lift = jnp.where(jnp.bitwise_and(token, 8) > 0, K, 0)
    for block in range(LATENTS // 128):
        ids = (lax.broadcasted_iota(jnp.int32, (128, width), 0) + block * 128).astype(jnp.int16)

        def look(k, held):
            row = jnp.broadcast_to(local_ref[pl.ds(k, 1), :], (16, width)).astype(jnp.int16)
            rows = jnp.concatenate([row] * 8, axis=0)
            return jnp.where(ids == rows, jnp.full((128, width), k, jnp.int32).astype(jnp.int16), held)

        held = lax.fori_loop(0, K, look, jnp.full((128, width), -1, jnp.int16), unroll=16).astype(jnp.int32)
        table[block * 128 : (block + 1) * 128, :] = jnp.where(held >= 0, held + lift, -1).astype(F32)
    slot_ref[...] = table[...].T.astype(BF16)


def find_slots(local, piece, before=None):
    steps = PIECE // LANES
    held = [] if before is None else [before]
    return pl.pallas_call(
        slot_kernel,
        grid=(steps,),
        in_specs=[pl.BlockSpec((K, LANES), lambda i: (0, piece * steps + i))]
        + [pl.BlockSpec(memory_space=pl.ANY)] * len(held),
        out_specs=pl.BlockSpec((LANES, LATENTS), lambda i: (piece * steps + i, 0)),
        out_shape=pltpu.HBM((ROWS, LATENTS), BF16),
        input_output_aliases={1: 0} if held else {},
        scratch_shapes=[pltpu.VMEM((LATENTS, LANES), F32)],
        compiler_params=params(),
        cost_estimate=LITTLE,
        name="find_slots",
    )(local, *in_hbm(*held))


def prefetched(grid, in_specs, out_specs, scratch=()):
    return pltpu.PrefetchScalarGridSpec(
        num_scalar_prefetch=1, grid=grid, in_specs=in_specs, out_specs=out_specs, scratch_shapes=scratch
    )


def quarter_lanes(position, step):
    start = jnp.bitwise_xor(position[0], step) * QUARTER
    return pl.ds(pl.multiple_of(start, QUARTER), QUARTER)


def cast_kernel(position, enc_ref, dec_ref, keep_ref, send_ref):
    for array, ref in enumerate((enc_ref, dec_ref)):
        for turned, out_ref in enumerate((keep_ref, send_ref)):
            start = jnp.bitwise_xor(position[1], turned) * FEATS
            half = ref[0, :, pl.ds(pl.multiple_of(start, FEATS), FEATS)]
            out_ref[array] = half.astype(BF16)


def cast_weights(position, enc, dec):
    return pl.pallas_call(
        cast_kernel,
        grid_spec=prefetched((1,), [whole_spec(enc.shape)] * 2, [whole_spec((2, OWN, FEATS))] * 2),
        out_shape=[jax.ShapeDtypeStruct((2, OWN, FEATS), BF16)] * 2,
        compiler_params=params(),
        cost_estimate=LITTLE,
        name="cast_weights",
    )(position, *in_hbm(enc, dec))


def pair_kernel(keep_ref, got_ref, enc_ref, dec_ref):
    for array, out_ref in enumerate((enc_ref, dec_ref)):
        out_ref[:OWN, :] = keep_ref[array]
        out_ref[OWN:, :] = got_ref[array]


def pair(keep, got):
    return pl.pallas_call(
        pair_kernel,
        out_shape=[jax.ShapeDtypeStruct((PAIR, FEATS), BF16)] * 2,
        compiler_params=params(),
        cost_estimate=LITTLE,
        name="pair",
    )(keep, got)


def over(axis, size, array, step):
    return lax.ppermute(array, axis, swapped(size, step))


def token_gather(near):
    one, three = over("token", 4, near, 1), over("token", 4, near, 3)
    return [near, one, three, over("token", 4, three[:OWN], 1), over("token", 4, one[OWN:], 3)]


def assemble(parts, whole, turn=0):
    for step, part in parts:
        for first in range(0, part.shape[0], OWN):
            side = first // OWN if part.shape[0] == PAIR else HALVES[step]
            start = side * SIDE + jnp.bitwise_xor(step & 3, turn) * OWN
            whole[pl.ds(pl.multiple_of(start, 16), OWN), :] = part[first : first + OWN, :]


HALVES = {2: 0, 6: 1}
ENC_SHAPES = ((PAIR, FEATS),) * 3 + ((OWN, FEATS),) * 2
ENC_STEPS = (0, 1, 3, 2, 6)
DEC_SHAPES = ((PAIR, FEATS),) * 4


def put_half(position, value, keep_ref, send_ref):
    step = pl.program_id(0)
    start = (step % HALF_STEPS) * HALF
    rows = pl.ds(pl.multiple_of(start, HALF), HALF)
    mine = step // HALF_STEPS == position[1]

    @pl.when(mine)
    def _():
        keep_ref[rows, :] = value

    @pl.when(jnp.logical_not(mine))
    def _():
        send_ref[rows, :] = value


def unpack(position, parts, packed):
    for step, part in enumerate(parts):
        block = jnp.bitwise_xor(position[2], step) * BLOCK
        for side in range(2):
            start = jnp.bitwise_xor(position[1], side) * SHARE + block
            rows = pl.ds(pl.multiple_of(start, BLOCK), BLOCK)
            packed[rows, :] = part[side * BLOCK : (side + 1) * BLOCK, :]


def packed_rows(packed):
    start = pl.program_id(0) * HALF
    return packed[pl.ds(pl.multiple_of(start, HALF), HALF), :].astype(F32)


def pre_kernel(position, streams_ref, q0, q1, q3, q2a, q2b, index_ref, keep_ref, send_ref, weight):
    @pl.when(pl.program_id(0) == 0)
    def _():
        assemble(list(zip(ENC_STEPS, (q0, q1, q3, q2a, q2b))), weight)

    pre = lax.dot_general(
        streams_ref[...], weight[...], (((1,), (1,)), ((), ())), preferred_element_type=F32
    )
    put_half(position, compact(pre, index_ref[...]), keep_ref, send_ref)


def whole_spec(shape):
    return pl.BlockSpec(shape, lambda i, *at: (0,) * len(shape))


def row_spec(rows, width):
    return pl.BlockSpec((rows, width), lambda i, *at: (i, 0))


def pre_sums(position, streams, enc_parts, index):
    return pl.pallas_call(
        pre_kernel,
        grid_spec=prefetched(
            (CHUNKS,),
            [row_spec(CHUNK, FEATS)] + [whole_spec(shape) for shape in ENC_SHAPES] + [row_spec(HALF, LANES)],
            [whole_spec((SHARE, LANES))] * 2,
            [pltpu.VMEM((LATENTS, FEATS), BF16)],
        ),
        out_shape=[jax.ShapeDtypeStruct((SHARE, LANES), F32)] * 2,
        compiler_params=params(),
        cost_estimate=LITTLE,
        name="pre_sums",
    )(position, streams, *enc_parts, index)


def fold_kernel(position, keep_ref, got_ref, *out_refs):
    for step, out_ref in enumerate(out_refs):
        start = jnp.bitwise_xor(position[2], step) * BLOCK
        rows = pl.ds(pl.multiple_of(start, BLOCK), BLOCK)
        out_ref[...] = keep_ref[rows, :] + got_ref[rows, :]


def fold(position, keep, got):
    return pl.pallas_call(
        fold_kernel,
        grid_spec=prefetched((1,), [whole_spec((SHARE, LANES))] * 2, [whole_spec((BLOCK, LANES))] * 4),
        out_shape=[jax.ShapeDtypeStruct((BLOCK, LANES), F32)] * 4,
        compiler_params=params(),
        cost_estimate=LITTLE,
        name="fold",
    )(position, keep, got)


def couple_kernel(own_ref, other_ref, out_ref):
    out_ref[:BLOCK, :] = own_ref[...]
    out_ref[BLOCK:, :] = other_ref[...]


def couple(own, other):
    return pl.pallas_call(
        couple_kernel,
        out_shape=jax.ShapeDtypeStruct((2 * BLOCK, LANES), BF16),
        compiler_params=params(),
        cost_estimate=LITTLE,
        name="couple",
    )(own, other)


def sum_of_four(parts):
    return (parts[0] + parts[1]) + (parts[2] + parts[3])


def with_partners(axis, parts):
    return [parts[0]] + [over(axis, 8, parts[step], 2 * step) for step in range(1, 4)]


def group_sum(position, keep, send, scale):
    parts = fold(position, keep, over("latent", 8, send, 1))
    block = sum_of_four(with_partners("latent", parts))
    block = sum_of_four(with_partners("layer", [block] * 4))
    total = ((block + over("layer", 8, block, 1)) * scale).astype(BF16)
    total = couple(total, over("latent", 8, total, 1))
    return with_partners("latent", [total] * 4)


def accumulate(part, total):
    step = pl.program_id(0)

    @pl.when(step == 0)
    def _():
        total[...] = part

    @pl.when(step > 0)
    def _():
        total[...] += part


def errors_body(
    scale, position, p0, p1, p2, p3, slot_ref, streams_ref, q0, q1, q2, q3, index_ref, keep_ref, send_ref, codes_ref, errors_ref, weight, packed
):
    @pl.when(pl.program_id(0) == 0)
    def _():
        assemble(list(enumerate((q0, q1, q2, q3))), weight, position[2])
        unpack(position, (p0, p1, p2, p3), packed)

    codes = spread(packed_rows(packed), slot_ref[...])
    codes_ref[...] = codes
    rebuilt = jnp.dot(codes, weight[...], preferred_element_type=F32) * scale
    errors = (rebuilt - streams_ref[...].astype(F32)).astype(BF16)
    errors_ref[...] = errors
    back = lax.dot_general(errors, weight[...], (((1,), (1,)), ((), ())), preferred_element_type=F32)
    put_half(position, compact(back, index_ref[...]), keep_ref, send_ref)


def errors_and_back(position, packed, slots, streams, dec_parts, index, scale):
    return pl.pallas_call(
        lambda *refs: errors_body(scale, *refs),
        grid_spec=prefetched(
            (CHUNKS,),
            [whole_spec((2 * BLOCK, LANES))] * 4
            + [row_spec(CHUNK, LATENTS), row_spec(CHUNK, FEATS)]
            + [whole_spec(shape) for shape in DEC_SHAPES]
            + [row_spec(HALF, LANES)],
            [whole_spec((SHARE, LANES))] * 2 + [row_spec(CHUNK, LATENTS), row_spec(CHUNK, FEATS)],
            [pltpu.VMEM((LATENTS, FEATS), BF16), pltpu.VMEM((ROWS // 2, LANES), BF16)],
        ),
        out_shape=[jax.ShapeDtypeStruct((SHARE, LANES), F32)] * 2
        + [jax.ShapeDtypeStruct((ROWS, LATENTS), BF16), jax.ShapeDtypeStruct((ROWS, FEATS), BF16)],
        compiler_params=params(),
        cost_estimate=LITTLE,
        name="errors_and_back",
    )(position, *packed, *in_hbm(slots), streams, *dec_parts, index)


def dec_gradient_body(scale, position, codes_ref, errors_ref, p0, p1, p2, p3, total):
    accumulate(
        lax.dot_general(codes_ref[...], errors_ref[...], (((0,), (0,)), ((), ())), preferred_element_type=F32),
        total,
    )

    @pl.when(pl.program_id(0) == CHUNKS - 1)
    def _():
        for step, out_ref in enumerate((p0, p1, p2, p3)):
            out_ref[...] = (total[:, quarter_lanes(position, step)] * scale).astype(BF16)


def dec_gradient(position, codes, errors, scale):
    return pl.pallas_call(
        lambda *refs: dec_gradient_body(scale, *refs),
        grid_spec=prefetched(
            (CHUNKS,),
            [row_spec(CHUNK, LATENTS), row_spec(CHUNK, FEATS)],
            [whole_spec((LATENTS, QUARTER))] * 4,
            [pltpu.VMEM((LATENTS, FEATS), F32)],
        ),
        out_shape=[jax.ShapeDtypeStruct((LATENTS, QUARTER), BF16)] * 4,
        compiler_params=params(),
        cost_estimate=LITTLE,
        name="dec_gradient",
    )(position, codes, errors)


def dec_total_kernel(p0, p1, p2, p3, keep_ref, send_ref):
    for side, out_ref in enumerate((keep_ref, send_ref)):
        for block in range(4):
            sums = None
            for step, part in enumerate((p0, p1, p2, p3)):
                start = side * SIDE + (block ^ step) * OWN
                term = part[start : start + OWN, :].astype(F32)
                sums = term if sums is None else sums + term
            out_ref[block * OWN : (block + 1) * OWN, :] = sums.astype(BF16)


def dec_total(parts):
    return pl.pallas_call(
        dec_total_kernel,
        out_shape=[jax.ShapeDtypeStruct((SIDE, QUARTER), BF16)] * 2,
        compiler_params=params(),
        cost_estimate=LITTLE,
        name="dec_total",
    )(*parts)


def enc_gradient_body(scale, position, p0, p1, p2, p3, slot_ref, near_ref, far_ref, keep_ref, got_ref, g0, g1, g2, g3, total, packed):
    @pl.when(pl.program_id(0) == 0)
    def _():
        unpack(position, (p0, p1, p2, p3), packed)

    codes = spread(packed_rows(packed), slot_ref[...])[:, :SIDE]
    parts = [
        lax.dot_general(codes, ref[...], (((0,), (0,)), ((), ())), preferred_element_type=F32)
        for ref in (near_ref, far_ref)
    ]
    accumulate(jnp.concatenate(parts, axis=1), total)

    @pl.when(pl.program_id(0) == CHUNKS - 1)
    def _():
        for step, out_ref in enumerate((g0, g1, g2, g3)):
            rows = slice(step * OWN, (step + 1) * OWN)
            out_ref[:, : 2 * FEATS] = (total[rows, :] * scale).astype(BF16)
            out_ref[:, 2 * FEATS : 2 * FEATS + QUARTER] = keep_ref[rows, :]
            out_ref[:, 2 * FEATS + QUARTER :] = got_ref[rows, :]


RIDE = 2 * FEATS + 2 * QUARTER


def enc_gradient(position, packed, slots, near, far, keep, got, scale):
    return pl.pallas_call(
        lambda *refs: enc_gradient_body(scale, *refs),
        grid_spec=prefetched(
            (CHUNKS,),
            [whole_spec((2 * BLOCK, LANES))] * 4
            + [row_spec(CHUNK, LATENTS)]
            + [row_spec(CHUNK, FEATS)] * 2
            + [whole_spec((SIDE, QUARTER))] * 2,
            [whole_spec((OWN, RIDE))] * 4,
            [pltpu.VMEM((SIDE, 2 * FEATS), F32), pltpu.VMEM((ROWS // 2, LANES), BF16)],
        ),
        out_shape=[jax.ShapeDtypeStruct((OWN, RIDE), BF16)] * 4,
        compiler_params=params(),
        cost_estimate=LITTLE,
        name="enc_gradient",
    )(position, *packed, *in_hbm(slots), near, far, keep, got)


def adam_update(gradient, weight, moment, second):
    moment_new = 0.9 * moment + 0.1 * gradient
    second_new = 0.999 * second + 0.001 * gradient * gradient
    first_fix = 1.0 - 0.9**ADAM_STEP
    second_fix = 1.0 - 0.999**ADAM_STEP
    weight_new = weight - 0.2 * (moment_new / first_fix) / (jnp.sqrt(second_new / second_fix) + 1e-08)
    return weight_new, moment_new, second_new


def adam_kernel(position, *refs):
    enc_grads, dec_grads, enc_in, dec_in, enc_out, dec_out = (
        refs[:4], refs[4:8], refs[8:11], refs[11:14], refs[14:17], refs[17:20]
    )
    gradient = sum(ref[...].astype(F32) for ref in enc_grads)
    for out_ref, value in zip(enc_out, adam_update(gradient, *[ref[0] for ref in enc_in])):
        out_ref[0] = value
    for step, ref in enumerate(dec_grads):
        start = jnp.bitwise_xor(position[2], step) * QUARTER
        lanes = pl.ds(pl.multiple_of(start, QUARTER), QUARTER)
        held = [source[0, :, lanes] for source in dec_in]
        for out_ref, value in zip(dec_out, adam_update(ref[...].astype(F32), *held)):
            out_ref[0, :, lanes] = value


def adam(position, grads, enc, dec):
    enc_part = pl.BlockSpec((OWN, FEATS), lambda i, at: (0, i))
    dec_part = pl.BlockSpec((OWN, QUARTER), lambda i, at: (0, 2 * FEATS // QUARTER + i))
    state = pl.BlockSpec((1, OWN, FEATS), lambda i, at: (0, 0, jnp.bitwise_xor(i, at[1])))
    return pl.pallas_call(
        adam_kernel,
        grid_spec=prefetched((2,), [enc_part] * 4 + [dec_part] * 4 + [state] * 6, [state] * 6),
        out_shape=[jax.ShapeDtypeStruct(array.shape, F32) for array in enc + dec],
        compiler_params=params(),
        cost_estimate=LITTLE,
        name="adam",
    )(position, *grads, *grads, *enc, *dec)


def body(
    streams, active_latents, enc_weight, enc_moment, enc_second, dec_weight, dec_moment, dec_second
):
    tokens_all = ROWS * 4
    enc_scale = 1.0 / math.sqrt(8 * 8192)
    dec_scale = 1.0 / math.sqrt(K)
    latent = lax.axis_index("latent")
    row = lax.axis_index("token")
    core = jnp.bitwise_and(latent, 1)
    column = jnp.right_shift(latent, 1)
    position = jnp.stack([row, core, column]).astype(jnp.int32)
    own_rows = streams[0]

    keep, send = cast_weights(position, enc_weight, dec_weight)
    got = over("latent", 8, send, 1)
    enc_pair, dec_pair = pair(keep, got)
    enc_pair, dec_pair, other_rows, active_t = lax.optimization_barrier(
        (enc_pair, dec_pair, own_rows, active_latents.T)
    )
    turned = lax.ppermute(enc_pair, PLANE, TRANSPOSED)
    dec_moved = lax.ppermute(dec_pair, PLANE, ALONG_Y)
    index, local = find_index(position, active_t)
    far_rows = over("latent", 8, other_rows, 1)
    slots = None
    for piece in range(ROWS // PIECE):
        slots = find_slots(local, piece, slots)
    turned, dec_moved, slots, far_rows = lax.optimization_barrier((turned, dec_moved, slots, far_rows))
    enc_parts = token_gather(turned)
    dec_near = lax.ppermute(dec_moved, PLANE, ALONG_Z)
    enc_parts, dec_near = lax.optimization_barrier((enc_parts, dec_near))
    keep, send = pre_sums(position, own_rows, enc_parts, index)
    codes = group_sum(position, keep, send, enc_scale)
    keep, send, dec_near = lax.optimization_barrier((keep, send, dec_near))
    dec_parts = [dec_near] + [over("token", 4, dec_near, step) for step in range(1, 4)]
    keep, send, codes_wide, errors = errors_and_back(position, codes, slots, own_rows, dec_parts, index, dec_scale)
    backward = group_sum(position, keep, send, dec_scale)
    keep, send, codes_wide, errors = lax.optimization_barrier((keep, send, codes_wide, errors))
    pieces = dec_gradient(position, codes_wide, errors, dec_scale / tokens_all)
    pieces = [pieces[0]] + [over("token", 4, pieces[step], step) for step in range(1, 4)]
    dec_keep, dec_send = dec_total(pieces)
    dec_got = over("latent", 8, dec_send, 1)
    riders = enc_gradient(
        position, backward, slots, own_rows, far_rows, dec_keep, dec_got, enc_scale / tokens_all
    )
    home = {step: lax.ppermute(riders[step], PLANE, homeward(step)) for step in (0, 3, 1, 2)}
    grads = [home[step] for step in range(4)]
    return tuple(
        adam(position, grads, [enc_weight, enc_moment, enc_second], [dec_weight, dec_moment, dec_second])
    )


def solution(mesh):
    arrays = P("layer", "latent", "token")
    in_specs = (P("layer", "token", "latent"), P("token", None)) + (arrays,) * 6
    return jax.shard_map(body, mesh=mesh, in_specs=in_specs, out_specs=(arrays,) * 6, check_vma=False)
```

```python
import math

import jax
import jax.numpy as jnp
from jax import lax
from jax.experimental import pallas as pl
from jax.experimental.pallas import tpu as pltpu
from jax.sharding import PartitionSpec as P

K = 64
ADAM_STEP = 100
LATENTS = 384
OWN = 48
PAIR = 96
LANES = 128
PARTS = LATENTS // LANES
ROWS = 1024
FEATS = 1024
GROUP = ("layer", "latent")
GROUP_SIZE = 64
PLANE = ("latent", "token")
PIECE = 256
CHUNK = 512
CHUNKS = ROWS // CHUNK
HALF = CHUNK // 2
SHARE = ROWS // 4
BLOCK = SHARE // 4
HALF_STEPS = CHUNKS // 2
F32 = jnp.float32
BF16 = jnp.bfloat16
VMEM_BYTES = 20 * 1024 * 1024
SIDE = LATENTS // 2
QUARTER = 256


def place(z, core, y):
    return (z * 2 + core) * 4 + y


def plane_pairs(target):
    return [
        (place(z, core, y), place(*target(z, core, y)))
        for z in range(4)
        for core in range(2)
        for y in range(4)
    ]


TRANSPOSED = plane_pairs(lambda z, core, y: (y, core, z))
ALONG_Y = plane_pairs(lambda z, core, y: (z, core, z ^ y))
ALONG_Z = plane_pairs(lambda z, core, y: (z ^ y, core, y))


def homeward(step):
    return plane_pairs(lambda z, core, y: (y ^ step, core, z))


def swapped(count, step):
    return [(i, i ^ step) for i in range(count)]


def params():
    return pltpu.CompilerParams(vmem_limit_bytes=VMEM_BYTES)


LITTLE = pl.CostEstimate(flops=1024, bytes_accessed=1024, transcendentals=0)


def in_hbm(*arrays):
    return [pltpu.with_memory_space_constraint(array, pltpu.HBM) for array in arrays]


def lane_take(table, column):
    return jnp.take_along_axis(table, column, axis=1, mode="promise_in_bounds")


def compact(dense, index):
    pairs = dense.reshape(dense.shape[0] // 16, 2, 8, LATENTS)
    first = pairs[:, 0].reshape(dense.shape[0] // 2, LATENTS)
    second = pairs[:, 1].reshape(dense.shape[0] // 2, LATENTS)
    column = jnp.bitwise_and(index, LANES - 1)
    part = jnp.right_shift(index, 7)
    low = lax.broadcasted_iota(jnp.int32, index.shape, 1) < K
    out = None
    for q in range(PARTS):
        cut = slice(q * LANES, (q + 1) * LANES)
        found = jnp.where(low, lane_take(first[:, cut], column), lane_take(second[:, cut], column))
        out = found if out is None else jnp.where(part == q, found, out)
    return out


def spread(packed, slot):
    slot = slot.astype(F32).astype(jnp.int32)
    rows = slot.shape[0]
    pairs = slot.reshape(rows // 16, 2, 8, LATENTS)
    sides = []
    for side in range(2):
        at = pairs[:, side].reshape(rows // 2, LATENTS)
        cols = []
        for q in range(PARTS):
            here = at[:, q * LANES : (q + 1) * LANES]
            cols.append(jnp.where(here >= 0, lane_take(packed, jnp.bitwise_and(here, LANES - 1)), 0.0))
        sides.append(jnp.concatenate(cols, axis=1).reshape(rows // 16, 1, 8, LATENTS))
    return jnp.concatenate(sides, axis=1).reshape(rows, LATENTS).astype(BF16)


def index_kernel(place_ref, active_ref, index_ref, local_ref):
    width = active_ref.shape[1]
    active = active_ref[...]
    owner = jnp.right_shift(active * 1366, 16)
    side = jnp.bitwise_xor(jnp.bitwise_and(owner, 1), place_ref[1])
    step = jnp.bitwise_xor(jnp.right_shift(owner, 1), place_ref[0])
    local = side * SIDE + step * OWN + (active - owner * OWN)
    local_ref[...] = local
    turned = local.T.reshape(width // 16, 2, 8, K)
    index_ref[...] = jnp.concatenate(
        [turned[:, 0].reshape(width // 2, K), turned[:, 1].reshape(width // 2, K)], axis=1
    )


def find_index(position, active_t):
    return pl.pallas_call(
        index_kernel,
        grid_spec=pltpu.PrefetchScalarGridSpec(
            num_scalar_prefetch=1,
            grid=(2,),
            in_specs=[pl.BlockSpec((K, ROWS // 2), lambda i, at: (0, i))],
            out_specs=[
                pl.BlockSpec((ROWS // 4, LANES), lambda i, at: (i, 0)),
                pl.BlockSpec((K, ROWS // 2), lambda i, at: (0, i)),
            ],
        ),
        out_shape=[
            jax.ShapeDtypeStruct((ROWS // 2, LANES), jnp.int32),
            jax.ShapeDtypeStruct((K, ROWS), jnp.int32),
        ],
        compiler_params=params(),
        cost_estimate=LITTLE,
        name="find_index",
    )(position, active_t)


def slot_kernel(local_ref, *refs):
    slot_ref, table = refs[-2:]
    width = local_ref.shape[1]
    token = lax.broadcasted_iota(jnp.int32, (128, width), 1)
    lift = jnp.where(jnp.bitwise_and(token, 8) > 0, K, 0)
    for block in range(LATENTS // 128):
        ids = (lax.broadcasted_iota(jnp.int32, (128, width), 0) + block * 128).astype(jnp.int16)

        def look(k, held):
            row = jnp.broadcast_to(local_ref[pl.ds(k, 1), :], (16, width)).astype(jnp.int16)
            rows = jnp.concatenate([row] * 8, axis=0)
            return jnp.where(ids == rows, jnp.full((128, width), k, jnp.int32).astype(jnp.int16), held)

        held = lax.fori_loop(0, K, look, jnp.full((128, width), -1, jnp.int16), unroll=16).astype(jnp.int32)
        table[block * 128 : (block + 1) * 128, :] = jnp.where(held >= 0, held + lift, -1).astype(F32)
    slot_ref[...] = table[...].T.astype(BF16)


def find_slots(local, piece, before=None):
    steps = PIECE // LANES
    held = [] if before is None else [before]
    return pl.pallas_call(
        slot_kernel,
        grid=(steps,),
        in_specs=[pl.BlockSpec((K, LANES), lambda i: (0, piece * steps + i))]
        + [pl.BlockSpec(memory_space=pl.ANY)] * len(held),
        out_specs=pl.BlockSpec((LANES, LATENTS), lambda i: (piece * steps + i, 0)),
        out_shape=pltpu.HBM((ROWS, LATENTS), BF16),
        input_output_aliases={1: 0} if held else {},
        scratch_shapes=[pltpu.VMEM((LATENTS, LANES), F32)],
        compiler_params=params(),
        cost_estimate=LITTLE,
        name="find_slots",
    )(local, *in_hbm(*held))


def prefetched(grid, in_specs, out_specs, scratch=()):
    return pltpu.PrefetchScalarGridSpec(
        num_scalar_prefetch=1, grid=grid, in_specs=in_specs, out_specs=out_specs, scratch_shapes=scratch
    )


def quarter_lanes(position, step):
    start = jnp.bitwise_xor(position[0], step) * QUARTER
    return pl.ds(pl.multiple_of(start, QUARTER), QUARTER)


def cast_kernel(position, enc_ref, dec_ref, keep_ref, send_ref):
    for array, ref in enumerate((enc_ref, dec_ref)):
        for turned, out_ref in enumerate((keep_ref, send_ref)):
            start = jnp.bitwise_xor(position[1], turned) * FEATS
            half = ref[0, :, pl.ds(pl.multiple_of(start, FEATS), FEATS)]
            out_ref[array] = half.astype(BF16)


def cast_weights(position, enc, dec):
    return pl.pallas_call(
        cast_kernel,
        grid_spec=prefetched((1,), [whole_spec(enc.shape)] * 2, [whole_spec((2, OWN, FEATS))] * 2),
        out_shape=[jax.ShapeDtypeStruct((2, OWN, FEATS), BF16)] * 2,
        compiler_params=params(),
        cost_estimate=LITTLE,
        name="cast_weights",
    )(position, *in_hbm(enc, dec))


def pair_kernel(keep_ref, got_ref, enc_ref, dec_ref):
    for array, out_ref in enumerate((enc_ref, dec_ref)):
        out_ref[:OWN, :] = keep_ref[array]
        out_ref[OWN:, :] = got_ref[array]


def pair(keep, got):
    return pl.pallas_call(
        pair_kernel,
        out_shape=[jax.ShapeDtypeStruct((PAIR, FEATS), BF16)] * 2,
        compiler_params=params(),
        cost_estimate=LITTLE,
        name="pair",
    )(keep, got)


def over(axis, size, array, step):
    return lax.ppermute(array, axis, swapped(size, step))


def token_gather(near):
    one, three = over("token", 4, near, 1), over("token", 4, near, 3)
    return [near, one, three, over("token", 4, three[:OWN], 1), over("token", 4, one[OWN:], 3)]


def assemble(parts, whole, turn=0):
    for step, part in parts:
        for first in range(0, part.shape[0], OWN):
            side = first // OWN if part.shape[0] == PAIR else HALVES[step]
            start = side * SIDE + jnp.bitwise_xor(step & 3, turn) * OWN
            whole[pl.ds(pl.multiple_of(start, 16), OWN), :] = part[first : first + OWN, :]


HALVES = {2: 0, 6: 1}
ENC_SHAPES = ((PAIR, FEATS),) * 3 + ((OWN, FEATS),) * 2
ENC_STEPS = (0, 1, 3, 2, 6)
DEC_SHAPES = ((PAIR, FEATS),) * 4


def put_half(position, value, keep_ref, send_ref):
    step = pl.program_id(0)
    start = (step % HALF_STEPS) * HALF
    rows = pl.ds(pl.multiple_of(start, HALF), HALF)
    mine = step // HALF_STEPS == position[1]

    @pl.when(mine)
    def _():
        keep_ref[rows, :] = value

    @pl.when(jnp.logical_not(mine))
    def _():
        send_ref[rows, :] = value


def unpack(position, parts, packed):
    for step, part in enumerate(parts):
        block = jnp.bitwise_xor(position[2], step) * BLOCK
        for side in range(2):
            start = jnp.bitwise_xor(position[1], side) * SHARE + block
            rows = pl.ds(pl.multiple_of(start, BLOCK), BLOCK)
            packed[rows, :] = part[side * BLOCK : (side + 1) * BLOCK, :]


def packed_rows(packed):
    start = pl.program_id(0) * HALF
    return packed[pl.ds(pl.multiple_of(start, HALF), HALF), :].astype(F32)


def pre_kernel(position, streams_ref, q0, q1, q3, q2a, q2b, index_ref, keep_ref, send_ref, weight):
    @pl.when(pl.program_id(0) == 0)
    def _():
        assemble(list(zip(ENC_STEPS, (q0, q1, q3, q2a, q2b))), weight)

    pre = lax.dot_general(
        streams_ref[...], weight[...], (((1,), (1,)), ((), ())), preferred_element_type=F32
    )
    put_half(position, compact(pre, index_ref[...]), keep_ref, send_ref)


def whole_spec(shape):
    return pl.BlockSpec(shape, lambda i, *at: (0,) * len(shape))


def row_spec(rows, width):
    return pl.BlockSpec((rows, width), lambda i, *at: (i, 0))


def pre_sums(position, streams, enc_parts, index):
    return pl.pallas_call(
        pre_kernel,
        grid_spec=prefetched(
            (CHUNKS,),
            [row_spec(CHUNK, FEATS)] + [whole_spec(shape) for shape in ENC_SHAPES] + [row_spec(HALF, LANES)],
            [whole_spec((SHARE, LANES))] * 2,
            [pltpu.VMEM((LATENTS, FEATS), BF16)],
        ),
        out_shape=[jax.ShapeDtypeStruct((SHARE, LANES), F32)] * 2,
        compiler_params=params(),
        cost_estimate=LITTLE,
        name="pre_sums",
    )(position, streams, *enc_parts, index)


def fold_kernel(position, keep_ref, got_ref, *out_refs):
    for step, out_ref in enumerate(out_refs):
        start = jnp.bitwise_xor(position[2], step) * BLOCK
        rows = pl.ds(pl.multiple_of(start, BLOCK), BLOCK)
        out_ref[...] = keep_ref[rows, :] + got_ref[rows, :]


def fold(position, keep, got):
    return pl.pallas_call(
        fold_kernel,
        grid_spec=prefetched((1,), [whole_spec((SHARE, LANES))] * 2, [whole_spec((BLOCK, LANES))] * 4),
        out_shape=[jax.ShapeDtypeStruct((BLOCK, LANES), F32)] * 4,
        compiler_params=params(),
        cost_estimate=LITTLE,
        name="fold",
    )(position, keep, got)


def couple_kernel(own_ref, other_ref, out_ref):
    out_ref[:BLOCK, :] = own_ref[...]
    out_ref[BLOCK:, :] = other_ref[...]


def couple(own, other):
    return pl.pallas_call(
        couple_kernel,
        out_shape=jax.ShapeDtypeStruct((2 * BLOCK, LANES), BF16),
        compiler_params=params(),
        cost_estimate=LITTLE,
        name="couple",
    )(own, other)


def sum_of_four(parts):
    return (parts[0] + parts[1]) + (parts[2] + parts[3])


def with_partners(axis, parts):
    return [parts[0]] + [over(axis, 8, parts[step], 2 * step) for step in range(1, 4)]


def group_sum(position, keep, send, scale):
    parts = fold(position, keep, over("latent", 8, send, 1))
    block = sum_of_four(with_partners("latent", parts))
    block = sum_of_four(with_partners("layer", [block] * 4))
    total = ((block + over("layer", 8, block, 1)) * scale).astype(BF16)
    total = couple(total, over("latent", 8, total, 1))
    return with_partners("latent", [total] * 4)


def accumulate(part, total):
    step = pl.program_id(0)

    @pl.when(step == 0)
    def _():
        total[...] = part

    @pl.when(step > 0)
    def _():
        total[...] += part


def errors_body(
    scale, position, p0, p1, p2, p3, slot_ref, streams_ref, q0, q1, q2, q3, index_ref, keep_ref, send_ref, codes_ref, errors_ref, weight, packed
):
    @pl.when(pl.program_id(0) == 0)
    def _():
        assemble(list(enumerate((q0, q1, q2, q3))), weight, position[2])
        unpack(position, (p0, p1, p2, p3), packed)

    codes = spread(packed_rows(packed), slot_ref[...])
    codes_ref[...] = codes
    rebuilt = jnp.dot(codes, weight[...], preferred_element_type=F32) * scale
    errors = (rebuilt - streams_ref[...].astype(F32)).astype(BF16)
    errors_ref[...] = errors
    back = lax.dot_general(errors, weight[...], (((1,), (1,)), ((), ())), preferred_element_type=F32)
    put_half(position, compact(back, index_ref[...]), keep_ref, send_ref)


def errors_and_back(position, packed, slots, streams, dec_parts, index, scale):
    return pl.pallas_call(
        lambda *refs: errors_body(scale, *refs),
        grid_spec=prefetched(
            (CHUNKS,),
            [whole_spec((2 * BLOCK, LANES))] * 4
            + [row_spec(CHUNK, LATENTS), row_spec(CHUNK, FEATS)]
            + [whole_spec(shape) for shape in DEC_SHAPES]
            + [row_spec(HALF, LANES)],
            [whole_spec((SHARE, LANES))] * 2 + [row_spec(CHUNK, LATENTS), row_spec(CHUNK, FEATS)],
            [pltpu.VMEM((LATENTS, FEATS), BF16), pltpu.VMEM((ROWS // 2, LANES), BF16)],
        ),
        out_shape=[jax.ShapeDtypeStruct((SHARE, LANES), F32)] * 2
        + [jax.ShapeDtypeStruct((ROWS, LATENTS), BF16), jax.ShapeDtypeStruct((ROWS, FEATS), BF16)],
        compiler_params=params(),
        cost_estimate=LITTLE,
        name="errors_and_back",
    )(position, *packed, *in_hbm(slots), streams, *dec_parts, index)


def dec_gradient_body(scale, position, codes_ref, errors_ref, p0, p1, p2, p3, total):
    accumulate(
        lax.dot_general(codes_ref[...], errors_ref[...], (((0,), (0,)), ((), ())), preferred_element_type=F32),
        total,
    )

    @pl.when(pl.program_id(0) == CHUNKS - 1)
    def _():
        for step, out_ref in enumerate((p0, p1, p2, p3)):
            out_ref[...] = (total[:, quarter_lanes(position, step)] * scale).astype(BF16)


def dec_gradient(position, codes, errors, scale):
    return pl.pallas_call(
        lambda *refs: dec_gradient_body(scale, *refs),
        grid_spec=prefetched(
            (CHUNKS,),
            [row_spec(CHUNK, LATENTS), row_spec(CHUNK, FEATS)],
            [whole_spec((LATENTS, QUARTER))] * 4,
            [pltpu.VMEM((LATENTS, FEATS), F32)],
        ),
        out_shape=[jax.ShapeDtypeStruct((LATENTS, QUARTER), BF16)] * 4,
        compiler_params=params(),
        cost_estimate=LITTLE,
        name="dec_gradient",
    )(position, codes, errors)


def dec_total_kernel(p0, p1, p2, p3, keep_ref, send_ref):
    for side, out_ref in enumerate((keep_ref, send_ref)):
        for block in range(4):
            sums = None
            for step, part in enumerate((p0, p1, p2, p3)):
                start = side * SIDE + (block ^ step) * OWN
                term = part[start : start + OWN, :].astype(F32)
                sums = term if sums is None else sums + term
            out_ref[block * OWN : (block + 1) * OWN, :] = sums.astype(BF16)


def dec_total(parts):
    return pl.pallas_call(
        dec_total_kernel,
        out_shape=[jax.ShapeDtypeStruct((SIDE, QUARTER), BF16)] * 2,
        compiler_params=params(),
        cost_estimate=LITTLE,
        name="dec_total",
    )(*parts)


def enc_gradient_body(scale, position, p0, p1, p2, p3, slot_ref, near_ref, far_ref, keep_ref, got_ref, g0, g1, g2, g3, total, packed):
    @pl.when(pl.program_id(0) == 0)
    def _():
        unpack(position, (p0, p1, p2, p3), packed)

    codes = spread(packed_rows(packed), slot_ref[...])[:, :SIDE]
    parts = [
        lax.dot_general(codes, ref[...], (((0,), (0,)), ((), ())), preferred_element_type=F32)
        for ref in (near_ref, far_ref)
    ]
    accumulate(jnp.concatenate(parts, axis=1), total)

    @pl.when(pl.program_id(0) == CHUNKS - 1)
    def _():
        for step, out_ref in enumerate((g0, g1, g2, g3)):
            rows = slice(step * OWN, (step + 1) * OWN)
            out_ref[:, : 2 * FEATS] = (total[rows, :] * scale).astype(BF16)
            out_ref[:, 2 * FEATS : 2 * FEATS + QUARTER] = keep_ref[rows, :]
            out_ref[:, 2 * FEATS + QUARTER :] = got_ref[rows, :]


RIDE = 2 * FEATS + 2 * QUARTER


def enc_gradient(position, packed, slots, near, far, keep, got, scale):
    return pl.pallas_call(
        lambda *refs: enc_gradient_body(scale, *refs),
        grid_spec=prefetched(
            (CHUNKS,),
            [whole_spec((2 * BLOCK, LANES))] * 4
            + [row_spec(CHUNK, LATENTS)]
            + [row_spec(CHUNK, FEATS)] * 2
            + [whole_spec((SIDE, QUARTER))] * 2,
            [whole_spec((OWN, RIDE))] * 4,
            [pltpu.VMEM((SIDE, 2 * FEATS), F32), pltpu.VMEM((ROWS // 2, LANES), BF16)],
        ),
        out_shape=[jax.ShapeDtypeStruct((OWN, RIDE), BF16)] * 4,
        compiler_params=params(),
        cost_estimate=LITTLE,
        name="enc_gradient",
    )(position, *packed, *in_hbm(slots), near, far, keep, got)


def adam_update(gradient, weight, moment, second):
    moment_new = 0.9 * moment + 0.1 * gradient
    second_new = 0.999 * second + 0.001 * gradient * gradient
    first_fix = 1.0 - 0.9**ADAM_STEP
    second_fix = 1.0 - 0.999**ADAM_STEP
    weight_new = weight - 0.2 * (moment_new / first_fix) / (jnp.sqrt(second_new / second_fix) + 1e-08)
    return weight_new, moment_new, second_new


def adam_kernel(position, *refs):
    enc_grads, dec_grads, enc_in, dec_in, enc_out, dec_out = (
        refs[:4], refs[4:8], refs[8:11], refs[11:14], refs[14:17], refs[17:20]
    )
    gradient = sum(ref[...].astype(F32) for ref in enc_grads)
    for out_ref, value in zip(enc_out, adam_update(gradient, *[ref[0] for ref in enc_in])):
        out_ref[0] = value
    for step, ref in enumerate(dec_grads):
        start = jnp.bitwise_xor(position[2], step) * QUARTER
        lanes = pl.ds(pl.multiple_of(start, QUARTER), QUARTER)
        held = [source[0, :, lanes] for source in dec_in]
        for out_ref, value in zip(dec_out, adam_update(ref[...].astype(F32), *held)):
            out_ref[0, :, lanes] = value


def adam(position, grads, enc, dec):
    enc_part = pl.BlockSpec((OWN, FEATS), lambda i, at: (0, i))
    dec_part = pl.BlockSpec((OWN, QUARTER), lambda i, at: (0, 2 * FEATS // QUARTER + i))
    state = pl.BlockSpec((1, OWN, FEATS), lambda i, at: (0, 0, jnp.bitwise_xor(i, at[1])))
    return pl.pallas_call(
        adam_kernel,
        grid_spec=prefetched((2,), [enc_part] * 4 + [dec_part] * 4 + [state] * 6, [state] * 6),
        out_shape=[jax.ShapeDtypeStruct(array.shape, F32) for array in enc + dec],
        compiler_params=params(),
        cost_estimate=LITTLE,
        name="adam",
    )(position, *grads, *grads, *enc, *dec)


def body(
    streams, active_latents, enc_weight, enc_moment, enc_second, dec_weight, dec_moment, dec_second
):
    tokens_all = ROWS * 4
    enc_scale = 1.0 / math.sqrt(8 * 8192)
    dec_scale = 1.0 / math.sqrt(K)
    latent = lax.axis_index("latent")
    row = lax.axis_index("token")
    core = jnp.bitwise_and(latent, 1)
    column = jnp.right_shift(latent, 1)
    position = jnp.stack([row, core, column]).astype(jnp.int32)
    own_rows = streams[0]

    keep, send = cast_weights(position, enc_weight, dec_weight)
    got = over("latent", 8, send, 1)
    enc_pair, dec_pair = pair(keep, got)
    enc_pair, dec_pair, other_rows, active_t = lax.optimization_barrier(
        (enc_pair, dec_pair, own_rows, active_latents.T)
    )
    turned = lax.ppermute(enc_pair, PLANE, TRANSPOSED)
    dec_moved = lax.ppermute(dec_pair, PLANE, ALONG_Y)
    index, local = find_index(position, active_t)
    far_rows = over("latent", 8, other_rows, 1)
    slots = None
    for piece in range(ROWS // PIECE):
        slots = find_slots(local, piece, slots)
    turned, dec_moved, slots, far_rows = lax.optimization_barrier((turned, dec_moved, slots, far_rows))
    enc_parts = token_gather(turned)
    dec_near = lax.ppermute(dec_moved, PLANE, ALONG_Z)
    enc_parts, dec_near = lax.optimization_barrier((enc_parts, dec_near))
    keep, send = pre_sums(position, own_rows, enc_parts, index)
    codes = group_sum(position, keep, send, enc_scale)
    keep, send, dec_near = lax.optimization_barrier((keep, send, dec_near))
    dec_parts = [dec_near] + [over("token", 4, dec_near, step) for step in range(1, 4)]
    keep, send, codes_wide, errors = errors_and_back(position, codes, slots, own_rows, dec_parts, index, dec_scale)
    backward = group_sum(position, keep, send, dec_scale)
    keep, send, codes_wide, errors = lax.optimization_barrier((keep, send, codes_wide, errors))
    pieces = dec_gradient(position, codes_wide, errors, dec_scale / tokens_all)
    moved = {step: over("token", 4, pieces[step], step) for step in (2, 1, 3)}
    pieces = [pieces[0]] + [moved[step] for step in range(1, 4)]
    dec_keep, dec_send = dec_total(pieces)
    dec_got = over("latent", 8, dec_send, 1)
    riders = enc_gradient(
        position, backward, slots, own_rows, far_rows, dec_keep, dec_got, enc_scale / tokens_all
    )
    home = {step: lax.ppermute(riders[step], PLANE, homeward(step)) for step in (0, 3, 1, 2)}
    grads = [home[step] for step in range(4)]
    return tuple(
        adam(position, grads, [enc_weight, enc_moment, enc_second], [dec_weight, dec_moment, dec_second])
    )


def solution(mesh):
    arrays = P("layer", "latent", "token")
    in_specs = (P("layer", "token", "latent"), P("token", None)) + (arrays,) * 6
    return jax.shard_map(body, mesh=mesh, in_specs=in_specs, out_specs=(arrays,) * 6, check_vma=False)
```
